32 devices in a mesh: groups: 2 (over y), space: 8 (over z, x), tm: 2 (over core).
Axes of the slice: x: 2, y: 2, z: 4, core: 2. Of those that a mesh axis runs over, the one named last changes fastest.
Arguments:
- start_state: float32 [256, 32, 16], P(('groups', 'space')), parts along dimension 0, may hold values from -6 to 6
- timesteps: int32 [8], P(('groups', 'tm')), parts along dimension 0, may hold values from 0 to 999
- step_sizes: float32 [8], P(('groups', 'tm')), parts along dimension 0, may hold values from 0.1 to 0.4
- in_weight: float32 [16, 256], replicated, may hold values from -1.5 to 1.5
- time_weight: float32 [256, 256], replicated, may hold values from -0.375 to 0.375
- conv_kernel: float32 [2, 7, 7, 256], replicated, may hold values from -0.875 to 0.875
- norm_gain: float32 [2, 256], replicated, may hold values from 0.5 to 1.5
- up_weight: bfloat16 [2, 256, 1024], replicated, may hold values from -0.375 to 0.375
- up_bias: float32 [2, 1024], replicated, may hold values from -3 to 3
- down_weight: bfloat16 [2, 1024, 256], replicated, may hold values from -0.1875 to 0.1875
- out_weight: float32 [256, 16], replicated, may hold values from -0.375 to 0.375
Outputs:
- next_states: float32 [4, 256, 32, 16], P('tm', ('groups', 'space')), parts along dimension 1
The draws below stay inside these ranges and needn't reach their ends.
There are 2 independent parts, one for each index of `groups`. The reference program is written for one: setup_inputs(seed, part) draws one part's arguments, and reference() takes and returns one part's arrays. A program takes and returns all parts, laid end to end along the dimension named above; an argument that names none is the same for every part. Nothing has to cross between parts.
All inputs are finite; a program needn't handle non-finite values.
Results may differ from the reference program's by a relative error of at most 0.0035.
Values may be sent and summed in bfloat16 or wider, within the bound.
No kernel may reach another device: no remote copies, remote signals or barrier semaphores. Data moves between devices by JAX's collectives and lax.ppermute only.
A program may use at most 64 MiB of HBM per device.

```python
import math
import jax
import jax.numpy as jnp
from jax import lax

C_LAT = 16
WIDTH = 256
HIDDEN_SIZE = 1024
BLOCKS = 2
SWEEPS = 2
COLS = 32
TIMES = 4
ROWS = 128


def touch_ends(values, own_key, least, largest):
    longest = values.shape.index(max(values.shape))
    spots = []
    for shift in (0, 1):
        where = [jax.random.randint(jax.random.fold_in(own_key, axis), (), 0, length) for axis, length in enumerate(values.shape)]
        where[longest] = (where[longest] + shift) % values.shape[longest]
        spots.append(tuple(where))
    return values.at[spots[0]].set(least).at[spots[1]].set(largest)


def level_of(own_key, extent, split, low, high):
    level, own = 1.0, jax.random.fold_in(own_key, 6)
    for axis_at, shards_of in split:
        heights = jnp.exp(jax.random.uniform(jax.random.fold_in(own, axis_at), (shards_of,), jnp.float32, low / len(split), high / len(split)))
        level = level * jnp.repeat(heights, extent[axis_at] // shards_of).reshape([-1 if axis == axis_at else 1 for axis in range(len(extent))])
    return level


def noise(stream_key, dims, deviation, most, split=(), kind=jnp.bfloat16):
    loudness = level_of(stream_key, dims, split, -0.22, 0.18) if split else 1.0
    array = jax.random.normal(stream_key, dims, jnp.float32) * deviation * loudness
    return jnp.minimum(jnp.maximum(array, -most), most).astype(kind)


def setup_inputs(seed: int = 0, part: int = 0) -> dict:
    arg_keys = jax.random.split(jax.random.key(seed), 12)
    part_splits = jax.random.split(jax.random.fold_in(arg_keys[11], part), 12)
    start_state = noise(part_splits[0], (ROWS, COLS, C_LAT), 1.0, 6.0, ((0, 8),), jnp.float32)
    timesteps = touch_ends(jax.random.randint(part_splits[1], (TIMES,), 0, 1000), jax.random.fold_in(part_splits[1], 1), 0, 999).astype(jnp.int32)
    step_sizes = jnp.clip(jnp.exp(math.log(0.4) - 1.3862944 * jax.random.uniform(part_splits[2], (TIMES,), jnp.float32) ** level_of(part_splits[2], (TIMES,), ((0, 2),), -0.2, 0.2)), 0.1, 0.4)
    in_weight = noise(arg_keys[3], (C_LAT, WIDTH), C_LAT ** -0.5, 1.5, (), jnp.float32)
    time_weight = noise(arg_keys[4], (WIDTH, WIDTH), WIDTH ** -0.5, 0.375, (), jnp.float32)
    conv_kernel = noise(arg_keys[5], (BLOCKS, 7, 7, WIDTH), 49 ** -0.5, 0.875, (), jnp.float32)
    norm_gain = jnp.clip(1.0 + 0.1 * jax.random.normal(arg_keys[6], (BLOCKS, WIDTH), jnp.float32), 0.5, 1.5)
    up_weight = noise(arg_keys[7], (BLOCKS, WIDTH, HIDDEN_SIZE), WIDTH ** -0.5, 0.375)
    up_bias = noise(arg_keys[8], (BLOCKS, HIDDEN_SIZE), 0.5, 3.0, (), jnp.float32)
    down_weight = noise(arg_keys[9], (BLOCKS, HIDDEN_SIZE, WIDTH), HIDDEN_SIZE ** -0.5, 0.1875)
    out_weight = noise(arg_keys[10], (WIDTH, C_LAT), WIDTH ** -0.5, 0.375, (), jnp.float32)
    return {"start_state": start_state, "timesteps": timesteps, "step_sizes": step_sizes, "in_weight": in_weight, "time_weight": time_weight, "conv_kernel": conv_kernel, "norm_gain": norm_gain, "up_weight": up_weight, "up_bias": up_bias, "down_weight": down_weight, "out_weight": out_weight}


HIGH = lax.Precision.HIGHEST

def embed_time(step, time_weight):
    half = time_weight.shape[0] // 2
    freqs = jnp.exp(-math.log(10000.0) * jnp.arange(half, dtype=jnp.float32) / half)
    angle = step.astype(jnp.float32) * freqs
    feats = jnp.concatenate([jnp.sin(angle), jnp.cos(angle)])
    return jnp.dot(feats, time_weight, precision=HIGH)

def drift_field(state, step, in_weight, time_weight, conv_kernel, norm_gain, up_weight, up_bias, down_weight, out_weight):
    height, width_cols = (state.shape[0], state.shape[1])
    stream = jnp.einsum('hwc,cd->hwd', state, in_weight, precision=HIGH) + embed_time(step, time_weight)
    for block in range(BLOCKS):
        conv_in = stream.astype(jnp.bfloat16)
        padded = jnp.pad(conv_in, ((3, 3), (3, 3), (0, 0)))
        conv = jnp.zeros(stream.shape, jnp.float32)
        for dy in range(7):
            for dx in range(7):
                conv = conv + padded[dy:dy + height, dx:dx + width_cols].astype(jnp.float32) * conv_kernel[block, dy, dx]
        mean = lax.optimization_barrier(jnp.mean(conv, axis=-1, keepdims=True))
        centered = conv - mean
        var = lax.optimization_barrier(jnp.mean(centered * centered, axis=-1, keepdims=True))
        normed = (centered * lax.rsqrt(var + 1e-06) * norm_gain[block]).astype(jnp.bfloat16)
        upper = jnp.einsum('hwc,cf->hwf', normed.astype(jnp.float32), up_weight[block].astype(jnp.float32), precision=HIGH) + up_bias[block]
        hidden = jax.nn.gelu(upper, approximate=True).astype(jnp.bfloat16)
        stream = stream + jnp.einsum('hwf,fc->hwc', hidden.astype(jnp.float32), down_weight[block].astype(jnp.float32), precision=HIGH)
    return jnp.einsum('hwd,dc->hwc', stream, out_weight, precision=HIGH)

def reference(start_state, timesteps, step_sizes, in_weight, time_weight, conv_kernel, norm_gain, up_weight, up_bias, down_weight, out_weight):
    states = jnp.broadcast_to(start_state[None], (timesteps.shape[0],) + start_state.shape)

    def one_time(pair):
        return drift_field(pair[0], pair[1], in_weight, time_weight, conv_kernel, norm_gain, up_weight, up_bias, down_weight, out_weight)
    result = states
    for sweep in range(SWEEPS):
        drifts = lax.map(one_time, (states, timesteps))
        terms = drifts * step_sizes[:, None, None, None]
        inclusive = jnp.cumsum(terms, axis=0)
        if sweep < SWEEPS - 1:
            exclusive = jnp.concatenate([jnp.zeros_like(terms[:1]), inclusive[:-1]], axis=0)
            states = start_state[None] + exclusive
        else:
            result = start_state[None] + inclusive
    return result
```

```python
import functools
import math

import jax
import jax.numpy as jnp
from jax import lax
from jax.experimental import pallas as pl
from jax.experimental.pallas import tpu as pltpu
from jax.sharding import PartitionSpec as P

HIGH = lax.Precision.HIGHEST
F32, BF16 = jnp.float32, jnp.bfloat16
COLS, CHAN, WIDTH, HIDDEN, LANES = 32, 16, 256, 1024, 128
OWN, TAPS, HALO = 8, 7, 3
FIRST = OWN + 2 * HALO
DEEP = OWN + 4 * HALO
PAD = 8
WIDE = COLS + 2 * PAD
TIMES = 3


def embed_times(steps, time_weight):
    half = time_weight.shape[0] // 2
    freqs = jnp.exp(-math.log(10000.0) * jnp.arange(half, dtype=F32) / half)
    angle = steps[:, None] * freqs[None, :]
    feats = jnp.concatenate([jnp.sin(angle), jnp.cos(angle)], axis=1)
    return jnp.dot(feats, time_weight, precision=HIGH)


def split(x):
    hi = x.astype(BF16)
    return hi, (x - hi.astype(F32)).astype(BF16)


def dot(a, b):
    return lax.dot_general(a, b, (((1,), (0,)), ((), ())), preferred_element_type=F32)


def dot_nt(a, b):
    return lax.dot_general(a, b, (((1,), (1,)), ((), ())), preferred_element_type=F32)


def lane_group(shape):
    return lax.broadcasted_iota(jnp.int32, shape, len(shape) - 1) // CHAN


def spreader():
    row = lax.broadcasted_iota(jnp.int32, (LANES, OWN * LANES), 0)
    col = lax.broadcasted_iota(jnp.int32, (LANES, OWN * LANES), 1)
    hit = (row // CHAN == col // LANES) & (row % CHAN == col % CHAN)
    return jnp.where(hit, 1.0, 0.0).astype(BF16)


def normalise(conv, gain):
    mean = jnp.mean(conv, axis=-1, keepdims=True)
    centered = conv - mean
    var = jnp.mean(centered * centered, axis=-1, keepdims=True)
    return (centered * lax.rsqrt(var + 1e-06) * gain).astype(BF16)


def gelu(x):
    inner = x * (0.7978845608028654 + 0.035677408136300125 * (x * x))
    half = 0.5 * x
    return half + half * jnp.tanh(inner)


def mlp(normed, up, bias, down):
    hidden = gelu(dot(normed, up) + bias).astype(BF16)
    return dot(hidden, down)


def sweep_kernel(
    count, first_time, flags, steps, state, temb, in_w, taps, gain, up_w, up_b, down_w, out_t,
    terms, shift, patch_hi, patch_lo, weff_hi, weff_lo, wide, conv_buf,
):
    turn, inside = flags[0], flags[1].astype(F32)

    weff_hi[...] = jnp.zeros_like(weff_hi)
    weff_lo[...] = jnp.zeros_like(weff_lo)
    for dy in range(TAPS):
        at = dy + turn * (TAPS - 1 - 2 * dy)
        for dx in range(TAPS):
            hi, lo = split(in_w[...] * taps[at, dx, 0:1, :])
            weff_hi[dy, dx * CHAN : (dx + 1) * CHAN, :] = hi
            weff_lo[dy, dx * CHAN : (dx + 1) * CHAN, :] = lo
    gap = jnp.zeros((3 * CHAN, WIDTH), F32)
    in_hi, in_lo = split(jnp.concatenate([gap, in_w[...], gap, gap[:CHAN]], axis=0))

    column = lax.broadcasted_iota(jnp.int32, (COLS, WIDTH), 0)
    by_row = []
    for dy in range(TAPS):
        at = dy + turn * (TAPS - 1 - 2 * dy)
        total = jnp.zeros((COLS, WIDTH), F32)
        for dx in range(TAPS):
            ok = (column + (dx - HALO) >= 0) & (column + (dx - HALO) < COLS)
            total = total + jnp.where(ok, taps[at, dx, 0:1, :], 0.0)
        by_row.append(total)
    ones = []
    for r in range(-HALO, OWN + HALO):
        total = jnp.zeros((COLS, WIDTH), F32)
        for dy in range(TAPS):
            total = total + (by_row[dy] if r + dy - HALO >= 0 else by_row[dy] * inside)
        ones.append(total)
    ones = jnp.concatenate(ones, axis=0)

    shift[...] = jnp.zeros_like(shift)
    wide[...] = jnp.zeros_like(wide)
    spread = spreader()
    group = lane_group((1, 1, LANES))

    def patches(piece, out):
        flat = dot(piece, spread)
        for j in range(OWN):
            lanes = slice(j * LANES, (j + 1) * LANES)
            if j < 2 * HALO:
                shift[2 * HALO - 1 - j, PAD : PAD + COLS, :] = flat[0:COLS, lanes]
            shift[2 * HALO + j, PAD : PAD + COLS, :] = flat[COLS : 2 * COLS, lanes]
            if j >= OWN - 2 * HALO:
                shift[2 * HALO + 15 - j, PAD : PAD + COLS, :] = flat[2 * COLS :, lanes]
        start = PAD - HALO
        picked = shift[:, start : start + COLS, :]
        for dx in range(1, TAPS):
            picked = jnp.where(group == dx, shift[:, start + dx : start + dx + COLS, :], picked)
        out[...] = picked.astype(BF16)

    def rows(ref, dy):
        return ref[dy : dy + FIRST].reshape(FIRST * COLS, LANES)

    for t in range(TIMES):
        if t < count:
            hi, lo = split(state[t].reshape(3 * COLS, LANES))
            patches(hi, patch_hi)
            patches(lo, patch_lo)
            base = jnp.zeros((FIRST * COLS, WIDTH), F32)
            for dy in range(TAPS):
                base = base + dot(rows(patch_hi, dy), weff_hi[dy])
                base = base + dot(rows(patch_lo, dy), weff_hi[dy])
                base = base + dot(rows(patch_hi, dy), weff_lo[dy])
            stream = dot(rows(patch_hi, HALO), in_hi) + dot(rows(patch_lo, HALO), in_hi) + dot(rows(patch_hi, HALO), in_lo)
        shown = temb[first_time + t : first_time + t + 1, :]
        normed = normalise(base + ones * shown, gain[0:1, :])
        after = stream + shown + mlp(normed, up_w[0], up_b[0:1, :], down_w[0])
        after = after.reshape(FIRST, COLS, WIDTH)
        for half in range(2):
            lanes = slice(half * LANES, (half + 1) * LANES)
            wide[2 * t + half, 0:HALO, PAD : PAD + COLS, :] = after[0:HALO, :, lanes] * inside
            wide[2 * t + half, HALO:, PAD : PAD + COLS, :] = after[HALO:, :, lanes]

    def depthwise(t, half):
        lanes = slice(half * LANES, (half + 1) * LANES)
        acc = [jnp.zeros((COLS, LANES), F32) for _ in range(OWN)]
        for dx in range(TAPS):
            tap = [taps[dy + turn * (TAPS - 1 - 2 * dy), dx, 1:2, lanes] for dy in range(TAPS)]
            for i in range(FIRST):
                x = wide[2 * t + half, i, PAD - HALO + dx : PAD - HALO + dx + COLS, :]
                for dy in range(TAPS):
                    if 0 <= i - dy < OWN:
                        acc[i - dy] = acc[i - dy] + x * tap[dy]
        for h in range(OWN):
            conv_buf[t, h, :, lanes] = acc[h]

    for half in range(2):
        lax.fori_loop(0, TIMES, lambda t, carry: (depthwise(t, half), carry)[1], 0)

    out_hi, out_lo = split(jnp.concatenate([out_t[...]] * 8, axis=0))
    for t in range(TIMES):
        normed = normalise(conv_buf[t].reshape(OWN * COLS, WIDTH), gain[1:2, :])
        stream = jnp.concatenate(
            [
                wide[2 * t + half, HALO : HALO + OWN, PAD : PAD + COLS, :].reshape(OWN * COLS, LANES)
                for half in range(2)
            ],
            axis=-1,
        )
        stream = stream + mlp(normed, up_w[1], up_b[1:2, :], down_w[1])
        hi, lo = split(stream)
        drift = dot_nt(hi, out_hi) + dot_nt(lo, out_hi) + dot_nt(hi, out_lo)
        drift = (drift * steps[first_time + t]).reshape(OWN, COLS, LANES)
        dense = drift[0]
        for j in range(1, OWN):
            dense = jnp.where(group[0] == j, drift[j], dense)
        terms[t] = dense


def sweep(first_time, flags, steps, state, temb, in_w, taps, gain, up_w, up_b, down_w, out_t):
    smem = pl.BlockSpec(memory_space=pltpu.SMEM)
    vmem = pl.BlockSpec(memory_space=pltpu.VMEM)
    return pl.pallas_call(
        functools.partial(sweep_kernel, state.shape[0], first_time),
        out_shape=jax.ShapeDtypeStruct((TIMES, COLS, LANES), F32),
        in_specs=[smem, smem] + [vmem] * 9,
        out_specs=vmem,
        scratch_shapes=[
            pltpu.VMEM((DEEP, WIDE, LANES), F32),
            pltpu.VMEM((DEEP, COLS, LANES), BF16),
            pltpu.VMEM((DEEP, COLS, LANES), BF16),
            pltpu.VMEM((TAPS, LANES, WIDTH), BF16),
            pltpu.VMEM((TAPS, LANES, WIDTH), BF16),
            pltpu.VMEM((2 * TIMES, FIRST, WIDE, LANES), F32),
            pltpu.VMEM((TIMES, OWN, COLS, WIDTH), F32),
        ],
        compiler_params=pltpu.CompilerParams(vmem_limit_bytes=48 * 2**20),
    )(flags, steps, state, temb, in_w, taps, gain, up_w, up_b, down_w, out_t)


def to_dense(x):
    return x.reshape(LANES, COLS).T


def from_dense(x):
    return x.reshape(x.shape[0], COLS, OWN, CHAN).transpose(0, 2, 1, 3)


def on_device(
    start_state, timesteps, step_sizes, in_weight, time_weight, conv_kernel, norm_gain, up_weight, up_bias, down_weight, out_weight,
):
    space = lax.axis_size("space")
    s, tm = lax.axis_index("space"), lax.axis_index("tm")
    beside = [(0, 1), (1, 0)]
    across = []
    for i in range(space - 1):
        across += [(2 * i + 1, 2 * i + 2), (2 * i + 2, 2 * i + 1)]

    def over_tm(x):
        return lax.ppermute(x, "tm", beside)

    def over_space(x):
        return lax.ppermute(x, ("space", "tm"), across)

    own_clock = jnp.concatenate([timesteps.astype(F32), step_sizes])
    other_clock = over_tm(own_clock)
    low = jnp.where(tm == 0, own_clock, other_clock)
    high = jnp.where(tm == 0, other_clock, own_clock)
    times = jnp.concatenate([low[:2], high[:2]])
    steps = jnp.concatenate([low[2:], high[2:]])
    temb = embed_times(times, time_weight)
    flags = jnp.stack([tm, jnp.where(tm == 0, s > 0, s < space - 1).astype(jnp.int32)]).astype(jnp.int32)

    turned = start_state.transpose(0, 2, 1)
    top, bottom = to_dense(turned[:OWN]), to_dense(turned[: OWN - 1 : -1])
    own = jnp.where(tm == 0, top, bottom)
    inner = jnp.where(tm == 0, bottom, top)
    outer = over_space(own)
    start = jnp.stack([outer, own, inner])

    weights = (in_weight, conv_kernel.transpose(1, 2, 0, 3), norm_gain, up_weight, up_bias, down_weight, out_weight.T)
    terms = sweep(0, flags, steps, start[None], temb, *weights)
    sent = terms.astype(BF16)
    outer_terms, inner_terms = over_space(sent), over_tm(sent)
    all_terms = jnp.stack([outer_terms.astype(F32), terms, inner_terms.astype(F32)], axis=1)
    one = start + all_terms[0]
    two = one + all_terms[1]
    three = two + all_terms[2]
    later = sweep(1, flags, steps, jnp.stack([one, two, three]), temb, *weights)
    n0 = one[1]
    n1 = n0 + later[0]
    n2 = n1 + later[1]
    n3 = n2 + later[2]
    early, late = jnp.stack([n0, n1]), jnp.stack([n2, n3])
    keep, give = jnp.where(tm == 0, early, late), jnp.where(tm == 0, late, early)
    got = over_tm(give)
    upper = from_dense(jnp.where(tm == 0, keep, got))
    lower = from_dense(jnp.where(tm == 0, got, keep))[:, ::-1]
    return jnp.concatenate([upper, lower], axis=1)


def solution(mesh):
    both = P(("groups", "tm"))
    return jax.shard_map(
        on_device,
        mesh=mesh,
        in_specs=(P(("groups", "space"), None, None), both, both) + (P(),) * 8,
        out_specs=P("tm", ("groups", "space"), None, None),
        check_vma=False,
    )
```

```python
import functools
import math

import jax
import jax.numpy as jnp
from jax import lax
from jax.experimental import pallas as pl
from jax.experimental.pallas import tpu as pltpu
from jax.sharding import PartitionSpec as P

HIGH = lax.Precision.HIGHEST
F32, BF16 = jnp.float32, jnp.bfloat16
COLS, CHAN, WIDTH, HIDDEN, LANES = 32, 16, 256, 1024, 128
OWN, TAPS, HALO = 8, 7, 3
FIRST = OWN + 2 * HALO
DEEP = OWN + 4 * HALO
PAD = 8
WIDE = COLS + 2 * PAD
TIMES = 3


def embed_times(steps, time_weight):
    half = time_weight.shape[0] // 2
    freqs = jnp.exp(-math.log(10000.0) * jnp.arange(half, dtype=F32) / half)
    angle = steps[:, None] * freqs[None, :]
    feats = jnp.concatenate([jnp.sin(angle), jnp.cos(angle)], axis=1)
    return jnp.dot(feats, time_weight, precision=HIGH)


def split(x):
    hi = x.astype(BF16)
    return hi, (x - hi.astype(F32)).astype(BF16)


def dot(a, b):
    return lax.dot_general(a, b, (((1,), (0,)), ((), ())), preferred_element_type=F32)


def dot_nt(a, b):
    return lax.dot_general(a, b, (((1,), (1,)), ((), ())), preferred_element_type=F32)


def lane_group(shape):
    return lax.broadcasted_iota(jnp.int32, shape, len(shape) - 1) // CHAN


def spreader(wanted):
    row = lax.broadcasted_iota(jnp.int32, (LANES, OWN * LANES), 0)
    col = lax.broadcasted_iota(jnp.int32, (LANES, OWN * LANES), 1)
    hit = (row // CHAN == col // LANES) & (row % CHAN == col % CHAN) & wanted((col % LANES) // CHAN)
    return jnp.where(hit, 1.0, 0.0).astype(BF16)


def normalise(conv, gain):
    mean = jnp.mean(conv, axis=-1, keepdims=True)
    centered = conv - mean
    var = jnp.mean(centered * centered, axis=-1, keepdims=True)
    return (centered * lax.rsqrt(var + 1e-06) * gain).astype(BF16)


def gelu(x):
    inner = x * (0.7978845608028654 + 0.035677408136300125 * (x * x))
    half = 0.5 * x
    return half + half * jnp.tanh(inner)


def mlp(normed, up, bias, down):
    hidden = gelu(dot(normed, up) + bias).astype(BF16)
    return dot(hidden, down)


def prepare_kernel(flags, start, own, inner):
    turned = flags[0] == 1
    top = to_dense([start[h] for h in range(OWN)])
    bottom = to_dense([start[2 * OWN - 1 - h] for h in range(OWN)])
    own[...] = jnp.where(turned, bottom, top)
    inner[...] = jnp.where(turned, top, bottom)


def finish_kernel(flags, keep, got, out):
    turned = flags[0] == 1
    for t in range(2):
        top = jnp.where(turned, got[t], keep[t])
        bottom = jnp.where(turned, keep[t], got[t])
        out[t, 0:OWN] = top.T.reshape(OWN, CHAN, COLS)
        flipped = bottom.T.reshape(OWN, CHAN, COLS)
        for h in range(OWN):
            out[t, 2 * OWN - 1 - h] = flipped[h]


def to_dense(rows):
    return jnp.concatenate(rows, axis=0).T


def sweep_kernel(
    last, flags, steps, start, outer, mine, inner, temb, in_w, taps, gain, up_b, out_t, up_hbm, down_hbm,
    first_out, second_out,
    shift, patch, centre, weff, wide, conv_buf, up_w, down_w, sems,
):
    copies = []
    for block in range(2):
        copies.append(pltpu.make_async_copy(up_hbm.at[block], up_w.at[block], sems.at[2 * block]))
        copies.append(pltpu.make_async_copy(down_hbm.at[block], down_w.at[block], sems.at[2 * block + 1]))
    for copy in copies:
        copy.start()
    turn, inside = flags[0], flags[1].astype(F32)
    first_time = 1 if last else 0

    weff[...] = jnp.zeros_like(weff)
    for dy in range(TAPS):
        at = dy + turn * (TAPS - 1 - 2 * dy)
        for dx in range(TAPS):
            low = dy * LANES + dx * CHAN
            weff[low : low + CHAN, :] = (in_w[...] * taps[at, dx, 0:1, :]).astype(BF16)
    in_hi, in_lo = split(in_w[...])
    in_three = jnp.concatenate([in_hi, in_hi, in_lo, jnp.zeros((LANES - 3 * CHAN, WIDTH), BF16)], axis=0)

    column = lax.broadcasted_iota(jnp.int32, (COLS, WIDTH), 0)
    by_row = []
    for dy in range(TAPS):
        at = dy + turn * (TAPS - 1 - 2 * dy)
        total = jnp.zeros((COLS, WIDTH), F32)
        for dx in range(TAPS):
            ok = (column + (dx - HALO) >= 0) & (column + (dx - HALO) < COLS)
            total = total + jnp.where(ok, taps[at, dx, 0:1, :], 0.0)
        by_row.append(total)
    ones = []
    for r in range(-HALO, OWN + HALO):
        total = jnp.zeros((COLS, WIDTH), F32)
        for dy in range(TAPS):
            total = total + (by_row[dy] if r + dy - HALO >= 0 else by_row[dy] * inside)
        ones.append(total)
    ones = jnp.concatenate(ones, axis=0)

    shift[...] = jnp.zeros_like(shift)
    wide[...] = jnp.zeros_like(wide)
    group = lane_group((1, 1, LANES))
    spread = spreader(lambda column_group: column_group >= 0)
    three = jnp.concatenate(
        [spreader(lambda g: (g == 0) | (g == 2)), spreader(lambda g: g == 1)], axis=0
    )

    def by_rows(flat):
        found = {}
        for j in range(OWN):
            lanes = slice(j * LANES, (j + 1) * LANES)
            if j < 2 * HALO:
                found[2 * HALO - 1 - j] = flat[0:COLS, lanes]
            found[2 * HALO + j] = flat[COLS : 2 * COLS, lanes]
            if j >= OWN - 2 * HALO:
                found[2 * HALO + 15 - j] = flat[2 * COLS :, lanes]
        return found

    def rows(ref, dy):
        return ref[dy : dy + FIRST].reshape(FIRST * COLS, LANES)

    sums = [start[i] for i in range(3)]
    for t in range(TIMES):
        if last:
            sums[0] = sums[0] + outer[t].astype(F32)
            sums[1] = sums[1] + mine[t]
            sums[2] = sums[2] + inner[t].astype(F32)
            if t == 0:
                n0 = sums[1]
        if last or t == 0:
            hi, lo = split(jnp.concatenate(sums, axis=0))
            for i, x in by_rows(dot(hi, spread)).items():
                shift[i, PAD : PAD + COLS, :] = x
            for i, x in by_rows(dot(jnp.concatenate([hi, lo], axis=-1), three)).items():
                if HALO <= i < HALO + FIRST:
                    centre[i - HALO] = x.astype(BF16)
            at = PAD - HALO
            picked = shift[:, at : at + COLS, :]
            for dx in range(1, TAPS):
                picked = jnp.where(group == dx, shift[:, at + dx : at + dx + COLS, :], picked)
            patch[...] = picked.astype(BF16)
            base = dot(jnp.concatenate([rows(patch, dy) for dy in range(TAPS)], axis=-1), weff[...])
            stream = dot(rows(centre, 0), in_three)
        shown = temb[first_time + t : first_time + t + 1, :]
        normed = normalise(base + ones * shown, gain[0:1, :])
        if t == 0:
            copies[0].wait()
            copies[1].wait()
        after = stream + shown + mlp(normed, up_w[0], up_b[0:1, :], down_w[0])
        after = after.reshape(FIRST, COLS, WIDTH)
        for half in range(2):
            lanes = slice(half * LANES, (half + 1) * LANES)
            wide[2 * t + half, 0:HALO, PAD : PAD + COLS, :] = after[0:HALO, :, lanes] * inside
            wide[2 * t + half, HALO:, PAD : PAD + COLS, :] = after[HALO:, :, lanes]

    def depthwise(t, half):
        lanes = slice(half * LANES, (half + 1) * LANES)
        acc = [jnp.zeros((COLS, LANES), F32) for _ in range(OWN)]
        for dx in range(TAPS):
            tap = [taps[dy + turn * (TAPS - 1 - 2 * dy), dx, 1:2, lanes] for dy in range(TAPS)]
            for i in range(FIRST):
                x = wide[2 * t + half, i, PAD - HALO + dx : PAD - HALO + dx + COLS, :]
                for dy in range(TAPS):
                    if 0 <= i - dy < OWN:
                        acc[i - dy] = acc[i - dy] + x * tap[dy]
        for h in range(OWN):
            conv_buf[t, h, :, lanes] = acc[h]

    for half in range(2):
        lax.fori_loop(0, TIMES, lambda t, carry: (depthwise(t, half), carry)[1], 0)

    copies[2].wait()
    copies[3].wait()
    out_hi, out_lo = split(jnp.concatenate([out_t[...]] * 8, axis=0))
    out_three = jnp.concatenate([out_hi, out_hi, out_lo], axis=-1)
    terms = []
    for t in range(TIMES):
        normed = normalise(conv_buf[t].reshape(OWN * COLS, WIDTH), gain[1:2, :])
        stream = jnp.concatenate(
            [
                wide[2 * t + half, HALO : HALO + OWN, PAD : PAD + COLS, :].reshape(OWN * COLS, LANES)
                for half in range(2)
            ],
            axis=-1,
        )
        stream = stream + mlp(normed, up_w[1], up_b[1:2, :], down_w[1])
        hi, lo = split(stream)
        drift = dot_nt(jnp.concatenate([hi, lo, hi], axis=-1), out_three)
        drift = (drift * steps[first_time + t]).reshape(OWN, COLS, LANES)
        dense = drift[0]
        for j in range(1, OWN):
            dense = jnp.where(group[0] == j, drift[j], dense)
        terms.append(dense)
    if last:
        n1 = n0 + terms[0]
        n2 = n1 + terms[1]
        n3 = n2 + terms[2]
        turned = turn == 1
        for i, (early, late) in enumerate(((n0, n2), (n1, n3))):
            first_out[i] = jnp.where(turned, late, early)
            second_out[i] = jnp.where(turned, early, late)
    else:
        for t in range(TIMES):
            first_out[t] = terms[t]
            second_out[t] = terms[t].astype(BF16)


SMEM = pl.BlockSpec(memory_space=pltpu.SMEM)
VMEM = pl.BlockSpec(memory_space=pltpu.VMEM)
HBM = pl.BlockSpec(memory_space=pltpu.HBM)


def sweep(last, flags, steps, start, outer, mine, inner, temb, in_w, taps, gain, up_b, out_t, up_w, down_w):
    if last:
        outs = [jax.ShapeDtypeStruct((2, COLS, LANES), F32)] * 2
    else:
        outs = [jax.ShapeDtypeStruct((TIMES, COLS, LANES), kind) for kind in (F32, BF16)]
    return pl.pallas_call(
        functools.partial(sweep_kernel, last),
        out_shape=outs,
        in_specs=[SMEM, SMEM] + [VMEM] * 10 + [HBM] * 2,
        out_specs=[VMEM, VMEM],
        scratch_shapes=[
            pltpu.VMEM((DEEP, WIDE, LANES), F32),
            pltpu.VMEM((DEEP, COLS, LANES), BF16),
            pltpu.VMEM((FIRST, COLS, LANES), BF16),
            pltpu.VMEM((TAPS * LANES, WIDTH), BF16),
            pltpu.VMEM((2 * TIMES, FIRST, WIDE, LANES), F32),
            pltpu.VMEM((TIMES, OWN, COLS, WIDTH), F32),
            pltpu.VMEM(up_w.shape, BF16),
            pltpu.VMEM(down_w.shape, BF16),
            pltpu.SemaphoreType.DMA((4,)),
        ],
        compiler_params=pltpu.CompilerParams(vmem_limit_bytes=48 * 2**20),
    )(flags, steps, start, outer, mine, inner, temb, in_w, taps, gain, up_b, out_t, up_w, down_w)


def prepare(flags, turned_start):
    dense = jax.ShapeDtypeStruct((COLS, LANES), F32)
    return pl.pallas_call(
        prepare_kernel, out_shape=[dense, dense], in_specs=[SMEM, VMEM], out_specs=[VMEM, VMEM]
    )(flags, turned_start)


def finish(flags, keep, got):
    return pl.pallas_call(
        finish_kernel,
        out_shape=jax.ShapeDtypeStruct((2, 2 * OWN, CHAN, COLS), F32),
        in_specs=[SMEM, VMEM, VMEM],
        out_specs=VMEM,
    )(flags, keep, got)


def on_device(
    start_state, timesteps, step_sizes, in_weight, time_weight, conv_kernel, norm_gain, up_weight, up_bias, down_weight, out_weight,
):
    space = lax.axis_size("space")
    s, tm = lax.axis_index("space"), lax.axis_index("tm")
    beside = [(0, 1), (1, 0)]
    across = []
    for i in range(space - 1):
        across += [(2 * i + 1, 2 * i + 2), (2 * i + 2, 2 * i + 1)]

    def over_tm(x):
        return lax.ppermute(x, "tm", beside)

    def over_space(x):
        return lax.ppermute(x, ("space", "tm"), across)

    flags = jnp.stack([tm, jnp.where(tm == 0, s > 0, s < space - 1).astype(jnp.int32)]).astype(jnp.int32)
    own_clock = jnp.concatenate([timesteps.astype(F32), step_sizes])
    other_clock = over_tm(own_clock)
    own, inner = prepare(flags, start_state.transpose(0, 2, 1))
    outer = over_space(own)
    low = jnp.where(tm == 0, own_clock, other_clock)
    high = jnp.where(tm == 0, other_clock, own_clock)
    times = jnp.concatenate([low[:2], high[:2]])
    steps = jnp.concatenate([low[2:], high[2:]])
    temb = embed_times(times, time_weight)
    start = jnp.stack([outer, own, inner])

    weights = (temb, in_weight, conv_kernel.transpose(1, 2, 0, 3), norm_gain, up_bias, out_weight.T, up_weight, down_weight)
    blank = jnp.zeros((8, LANES), F32)
    terms, sent = sweep(False, flags, steps, start, blank, blank, blank, *weights)
    inner_terms, outer_terms = over_tm(sent), over_space(sent)
    keep, give = sweep(True, flags, steps, start, outer_terms, terms, inner_terms, *weights)
    return finish(flags, keep, over_tm(give)).transpose(0, 1, 3, 2)


def solution(mesh):
    both = P(("groups", "tm"))
    return jax.shard_map(
        on_device,
        mesh=mesh,
        in_specs=(P(("groups", "space"), None, None), both, both) + (P(),) * 8,
        out_specs=P("tm", ("groups", "space"), None, None),
        check_vma=False,
    )
```

```python
import functools
import math

import jax
import jax.numpy as jnp
from jax import lax
from jax.experimental import pallas as pl
from jax.experimental.pallas import tpu as pltpu
from jax.sharding import PartitionSpec as P

HIGH = lax.Precision.HIGHEST
F32, BF16 = jnp.float32, jnp.bfloat16
COLS, CHAN, WIDTH, HIDDEN, LANES = 32, 16, 256, 1024, 128
OWN, TAPS, HALO = 8, 7, 3
FIRST = OWN + 2 * HALO
DEEP = OWN + 4 * HALO
PAD = 8
WIDE = COLS + 2 * PAD
TIMES = 3


def embed_times(steps, time_weight):
    half = time_weight.shape[0] // 2
    freqs = jnp.exp(-math.log(10000.0) * jnp.arange(half, dtype=F32) / half)
    angle = steps[:, None] * freqs[None, :]
    feats = jnp.concatenate([jnp.sin(angle), jnp.cos(angle)], axis=1)
    return jnp.dot(feats, time_weight, precision=HIGH)


def split(x):
    hi = x.astype(BF16)
    return hi, (x - hi.astype(F32)).astype(BF16)


def dot(a, b):
    return lax.dot_general(a, b, (((1,), (0,)), ((), ())), preferred_element_type=F32)


def dot_nt(a, b):
    return lax.dot_general(a, b, (((1,), (1,)), ((), ())), preferred_element_type=F32)


def lane_group(shape):
    return lax.broadcasted_iota(jnp.int32, shape, len(shape) - 1) // CHAN


def spreader(wanted):
    row = lax.broadcasted_iota(jnp.int32, (LANES, OWN * LANES), 0)
    col = lax.broadcasted_iota(jnp.int32, (LANES, OWN * LANES), 1)
    hit = (row // CHAN == col // LANES) & (row % CHAN == col % CHAN) & wanted((col % LANES) // CHAN)
    return jnp.where(hit, 1.0, 0.0).astype(BF16)


def normalise(conv, gain):
    mean = jnp.mean(conv, axis=-1, keepdims=True)
    centered = conv - mean
    var = jnp.mean(centered * centered, axis=-1, keepdims=True)
    return (centered * lax.rsqrt(var + 1e-06) * gain).astype(BF16)


def gelu(x):
    inner = x * (0.7978845608028654 + 0.035677408136300125 * (x * x))
    half = 0.5 * x
    return half + half * jnp.tanh(inner)


def mlp(normed, up, bias, down):
    hidden = gelu(dot(normed, up) + bias).astype(BF16)
    return dot(hidden, down)


def prepare_kernel(flags, start, own, inner):
    turned = flags[0] == 1
    top = to_dense([start[h] for h in range(OWN)])
    bottom = to_dense([start[2 * OWN - 1 - h] for h in range(OWN)])
    own[...] = jnp.where(turned, bottom, top)
    inner[...] = jnp.where(turned, top, bottom)


def finish_kernel(flags, keep, got, out):
    turned = flags[0] == 1
    for t in range(2):
        top = jnp.where(turned, got[t], keep[t])
        bottom = jnp.where(turned, keep[t], got[t])
        out[t, 0:OWN] = top.T.reshape(OWN, CHAN, COLS)
        flipped = bottom.T.reshape(OWN, CHAN, COLS)
        for h in range(OWN):
            out[t, 2 * OWN - 1 - h] = flipped[h]


def pinned(x):
    return pltpu.with_memory_space_constraint(x, pltpu.HBM)


def to_dense(rows):
    return jnp.concatenate(rows, axis=0).T


def sweep_kernel(
    last, flags, steps, start, outer, mine, inner, temb, in_w, taps, gain, up_b, out_t, up_hbm, down_hbm,
    first_out, second_out,
    shift, patch, centre, weff, wide, conv_buf, up_w, down_w, sems,
):
    copies = []
    for block in range(2):
        copies.append(pltpu.make_async_copy(up_hbm.at[block], up_w.at[block], sems.at[2 * block]))
        copies.append(pltpu.make_async_copy(down_hbm.at[block], down_w.at[block], sems.at[2 * block + 1]))
    for copy in copies:
        copy.start()
    turn, inside = flags[0], flags[1].astype(F32)
    first_time = 1 if last else 0

    weff[...] = jnp.zeros_like(weff)
    for dy in range(TAPS):
        at = dy + turn * (TAPS - 1 - 2 * dy)
        for dx in range(TAPS):
            low = dy * LANES + dx * CHAN
            weff[low : low + CHAN, :] = (in_w[...] * taps[at, dx, 0:1, :]).astype(BF16)
    in_hi, in_lo = split(in_w[...])
    in_three = jnp.concatenate([in_hi, in_hi, in_lo, jnp.zeros((LANES - 3 * CHAN, WIDTH), BF16)], axis=0)

    column = lax.broadcasted_iota(jnp.int32, (COLS, WIDTH), 0)
    by_row = []
    for dy in range(TAPS):
        at = dy + turn * (TAPS - 1 - 2 * dy)
        total = jnp.zeros((COLS, WIDTH), F32)
        for dx in range(TAPS):
            ok = (column + (dx - HALO) >= 0) & (column + (dx - HALO) < COLS)
            total = total + jnp.where(ok, taps[at, dx, 0:1, :], 0.0)
        by_row.append(total)
    ones = []
    for r in range(-HALO, OWN + HALO):
        total = jnp.zeros((COLS, WIDTH), F32)
        for dy in range(TAPS):
            total = total + (by_row[dy] if r + dy - HALO >= 0 else by_row[dy] * inside)
        ones.append(total)
    ones = jnp.concatenate(ones, axis=0)

    shift[...] = jnp.zeros_like(shift)
    wide[...] = jnp.zeros_like(wide)
    group = lane_group((1, 1, LANES))
    spread = spreader(lambda column_group: column_group >= 0)
    three = jnp.concatenate(
        [spreader(lambda g: (g == 0) | (g == 2)), spreader(lambda g: g == 1)], axis=0
    )

    def by_rows(flat):
        found = {}
        for j in range(OWN):
            lanes = slice(j * LANES, (j + 1) * LANES)
            if j < 2 * HALO:
                found[2 * HALO - 1 - j] = flat[0:COLS, lanes]
            found[2 * HALO + j] = flat[COLS : 2 * COLS, lanes]
            if j >= OWN - 2 * HALO:
                found[2 * HALO + 15 - j] = flat[2 * COLS :, lanes]
        return found

    def rows(ref, dy):
        return ref[dy : dy + FIRST].reshape(FIRST * COLS, LANES)

    sums = [start[i] for i in range(3)]
    for t in range(TIMES):
        if last:
            sums[0] = sums[0] + outer[t].astype(F32)
            sums[1] = sums[1] + mine[t]
            sums[2] = sums[2] + inner[t].astype(F32)
            if t == 0:
                n0 = sums[1]
        if last or t == 0:
            hi, lo = split(jnp.concatenate(sums, axis=0))
            for i, x in by_rows(dot(hi, spread)).items():
                shift[i, PAD : PAD + COLS, :] = x
            for i, x in by_rows(dot(jnp.concatenate([hi, lo], axis=-1), three)).items():
                if HALO <= i < HALO + FIRST:
                    centre[i - HALO] = x.astype(BF16)
            at = PAD - HALO
            picked = shift[:, at : at + COLS, :]
            for dx in range(1, TAPS):
                picked = jnp.where(group == dx, shift[:, at + dx : at + dx + COLS, :], picked)
            patch[...] = picked.astype(BF16)
            base = dot(jnp.concatenate([rows(patch, dy) for dy in range(TAPS)], axis=-1), weff[...])
            stream = dot(rows(centre, 0), in_three)
        shown = temb[first_time + t : first_time + t + 1, :]
        normed = normalise(base + ones * shown, gain[0:1, :])
        if t == 0:
            copies[0].wait()
            copies[1].wait()
        after = stream + shown + mlp(normed, up_w[0], up_b[0:1, :], down_w[0])
        after = after.reshape(FIRST, COLS, WIDTH)
        for half in range(2):
            lanes = slice(half * LANES, (half + 1) * LANES)
            wide[2 * t + half, 0:HALO, PAD : PAD + COLS, :] = after[0:HALO, :, lanes] * inside
            wide[2 * t + half, HALO:, PAD : PAD + COLS, :] = after[HALO:, :, lanes]

    def depthwise(t, half):
        lanes = slice(half * LANES, (half + 1) * LANES)
        acc = [jnp.zeros((COLS, LANES), F32) for _ in range(OWN)]
        for dx in range(TAPS):
            tap = [taps[dy + turn * (TAPS - 1 - 2 * dy), dx, 1:2, lanes] for dy in range(TAPS)]
            for i in range(FIRST):
                x = wide[2 * t + half, i, PAD - HALO + dx : PAD - HALO + dx + COLS, :]
                for dy in range(TAPS):
                    if 0 <= i - dy < OWN:
                        acc[i - dy] = acc[i - dy] + x * tap[dy]
        for h in range(OWN):
            conv_buf[t, h, :, lanes] = acc[h]

    for half in range(2):
        lax.fori_loop(0, TIMES, lambda t, carry: (depthwise(t, half), carry)[1], 0)

    copies[2].wait()
    copies[3].wait()
    out_hi, out_lo = split(jnp.concatenate([out_t[...]] * 8, axis=0))
    out_three = jnp.concatenate([out_hi, out_hi, out_lo], axis=-1)
    terms = []
    for t in range(TIMES):
        normed = normalise(conv_buf[t].reshape(OWN * COLS, WIDTH), gain[1:2, :])
        stream = jnp.concatenate(
            [
                wide[2 * t + half, HALO : HALO + OWN, PAD : PAD + COLS, :].reshape(OWN * COLS, LANES)
                for half in range(2)
            ],
            axis=-1,
        )
        stream = stream + mlp(normed, up_w[1], up_b[1:2, :], down_w[1])
        hi, lo = split(stream)
        drift = dot_nt(jnp.concatenate([hi, lo, hi], axis=-1), out_three)
        drift = (drift * steps[first_time + t]).reshape(OWN, COLS, LANES)
        dense = drift[0]
        for j in range(1, OWN):
            dense = jnp.where(group[0] == j, drift[j], dense)
        terms.append(dense)
    if last:
        n1 = n0 + terms[0]
        n2 = n1 + terms[1]
        n3 = n2 + terms[2]
        turned = turn == 1
        for i, (early, late) in enumerate(((n0, n2), (n1, n3))):
            first_out[i] = jnp.where(turned, late, early)
            second_out[i] = jnp.where(turned, early, late)
    else:
        for t in range(TIMES):
            first_out[t] = terms[t]
            second_out[t] = terms[t].astype(BF16)


SMEM = pl.BlockSpec(memory_space=pltpu.SMEM)
VMEM = pl.BlockSpec(memory_space=pltpu.VMEM)
HBM = pl.BlockSpec(memory_space=pltpu.HBM)
SMALL = pltpu.CompilerParams(vmem_limit_bytes=4 * 2**20)


def sweep(last, flags, steps, start, outer, mine, inner, temb, in_w, taps, gain, up_b, out_t, up_w, down_w):
    if last:
        outs = [jax.ShapeDtypeStruct((2, COLS, LANES), F32)] * 2
    else:
        outs = [jax.ShapeDtypeStruct((TIMES, COLS, LANES), kind) for kind in (F32, BF16)]
    return pl.pallas_call(
        functools.partial(sweep_kernel, last),
        out_shape=outs,
        in_specs=[SMEM, SMEM] + [VMEM] * 10 + [HBM] * 2,
        out_specs=[VMEM, VMEM],
        scratch_shapes=[
            pltpu.VMEM((DEEP, WIDE, LANES), F32),
            pltpu.VMEM((DEEP, COLS, LANES), BF16),
            pltpu.VMEM((FIRST, COLS, LANES), BF16),
            pltpu.VMEM((TAPS * LANES, WIDTH), BF16),
            pltpu.VMEM((2 * TIMES, FIRST, WIDE, LANES), F32),
            pltpu.VMEM((TIMES, OWN, COLS, WIDTH), F32),
            pltpu.VMEM(up_w.shape, BF16),
            pltpu.VMEM(down_w.shape, BF16),
            pltpu.SemaphoreType.DMA((4,)),
        ],
        compiler_params=pltpu.CompilerParams(vmem_limit_bytes=24 * 2**20),
    )(flags, steps, start, outer, mine, inner, temb, in_w, taps, gain, up_b, out_t, up_w, down_w)


def prepare(flags, turned_start):
    dense = jax.ShapeDtypeStruct((COLS, LANES), F32)
    return pl.pallas_call(
        prepare_kernel, out_shape=[dense, dense], in_specs=[SMEM, VMEM], out_specs=[VMEM, VMEM], compiler_params=SMALL
    )(flags, turned_start)


def finish(flags, keep, got):
    return pl.pallas_call(
        finish_kernel,
        out_shape=jax.ShapeDtypeStruct((2, 2 * OWN, CHAN, COLS), F32),
        in_specs=[SMEM, VMEM, VMEM],
        out_specs=VMEM,
        compiler_params=SMALL,
    )(flags, keep, got)


def on_device(
    start_state, timesteps, step_sizes, in_weight, time_weight, conv_kernel, norm_gain, up_weight, up_bias, down_weight, out_weight,
):
    space = lax.axis_size("space")
    s, tm = lax.axis_index("space"), lax.axis_index("tm")
    beside = [(0, 1), (1, 0)]
    across = []
    for i in range(space - 1):
        across += [(2 * i + 1, 2 * i + 2), (2 * i + 2, 2 * i + 1)]

    def over_tm(x):
        return lax.ppermute(x, "tm", beside)

    def over_space(x):
        return lax.ppermute(x, ("space", "tm"), across)

    flags = jnp.stack([tm, jnp.where(tm == 0, s > 0, s < space - 1).astype(jnp.int32)]).astype(jnp.int32)
    own_clock = jnp.concatenate([timesteps.astype(F32), step_sizes])
    other_clock = over_tm(own_clock)
    own, inner = prepare(flags, start_state.transpose(0, 2, 1))
    outer = over_space(own)
    low = jnp.where(tm == 0, own_clock, other_clock)
    high = jnp.where(tm == 0, other_clock, own_clock)
    times = jnp.concatenate([low[:2], high[:2]])
    steps = jnp.concatenate([low[2:], high[2:]])
    temb = embed_times(times, time_weight)
    start = jnp.stack([outer, own, inner])

    weights = (temb, in_weight, conv_kernel.transpose(1, 2, 0, 3), norm_gain, up_bias, out_weight.T, pinned(up_weight), pinned(down_weight))
    blank = jnp.zeros((8, LANES), F32)
    terms, sent = sweep(False, flags, steps, start, blank, blank, blank, *weights)
    inner_terms, outer_terms = over_tm(sent), over_space(sent)
    keep, give = sweep(True, flags, steps, start, outer_terms, terms, inner_terms, *weights)
    return finish(flags, keep, over_tm(give)).transpose(0, 1, 3, 2)


def solution(mesh):
    both = P(("groups", "tm"))
    return jax.shard_map(
        on_device,
        mesh=mesh,
        in_specs=(P(("groups", "space"), None, None), both, both) + (P(),) * 8,
        out_specs=P("tm", ("groups", "space"), None, None),
        check_vma=False,
    )
```

```python
import functools
import math

import jax
import jax.numpy as jnp
from jax import lax
from jax.experimental import pallas as pl
from jax.experimental.pallas import tpu as pltpu
from jax.sharding import PartitionSpec as P

HIGH = lax.Precision.HIGHEST
F32, BF16 = jnp.float32, jnp.bfloat16
COLS, CHAN, WIDTH, HIDDEN, LANES = 32, 16, 256, 1024, 128
OWN, TAPS, HALO = 8, 7, 3
REACH = 2 * HALO
PAD = 8
WIDE = COLS + 2 * PAD
TIMES = 3
CHUNK = 256


def split(x):
    hi = x.astype(BF16)
    return hi, (x - hi.astype(F32)).astype(BF16)


def dot(a, b):
    return lax.dot_general(a, b, (((1,), (0,)), ((), ())), preferred_element_type=F32)


def dot_nt(a, b):
    return lax.dot_general(a, b, (((1,), (1,)), ((), ())), preferred_element_type=F32)


def lane_group(shape):
    return lax.broadcasted_iota(jnp.int32, shape, len(shape) - 1) // CHAN


def spreader(wanted):
    row = lax.broadcasted_iota(jnp.int32, (LANES, OWN * LANES), 0)
    col = lax.broadcasted_iota(jnp.int32, (LANES, OWN * LANES), 1)
    hit = (row // CHAN == col // LANES) & (row % CHAN == col % CHAN) & wanted((col % LANES) // CHAN)
    return jnp.where(hit, 1.0, 0.0).astype(BF16)


def normalise(conv, gain):
    mean = jnp.mean(conv, axis=-1, keepdims=True)
    centered = conv - mean
    var = jnp.mean(centered * centered, axis=-1, keepdims=True)
    return (centered * lax.rsqrt(var + 1e-06) * gain).astype(BF16)


def gelu(x):
    x = x.astype(BF16)
    inner = x * (BF16(0.7978845608028654) + BF16(0.035677408136300125) * (x * x))
    half = BF16(0.5) * x
    return half + half * jnp.tanh(inner)


def interleave(first, second):
    total = max(len(first), len(second))
    for i in range(total):
        for steps in (first, second):
            for at in range(i * len(steps) // total, (i + 1) * len(steps) // total):
                steps[at]()


def prepare_kernel(flags, times, sizes, start, own, inner, clock):
    turned = flags[0] == 1
    top = to_dense([start[h] for h in range(OWN)])
    bottom = to_dense([start[2 * OWN - 1 - h] for h in range(OWN)])
    own[...] = jnp.where(turned, bottom, top)
    inner[...] = jnp.where(turned, top, bottom)
    lane = lax.broadcasted_iota(jnp.int32, (8, LANES), 1)
    values = (times[0].astype(F32), times[1].astype(F32), sizes[0], sizes[1])
    filled = jnp.zeros((8, LANES), F32)
    for i, value in enumerate(values):
        filled = jnp.where(lane == i, value, filled)
    clock[...] = filled


def finish_kernel(flags, keep, got, out):
    turned = flags[0] == 1
    for t in range(2):
        top = jnp.where(turned, got[t], keep[t])
        bottom = jnp.where(turned, keep[t], got[t])
        out[t, 0:OWN] = top.T.reshape(OWN, CHAN, COLS)
        flipped = bottom.T.reshape(OWN, CHAN, COLS)
        for h in range(OWN):
            out[t, 2 * OWN - 1 - h] = flipped[h]


def pinned(x):
    return pltpu.with_memory_space_constraint(x, pltpu.HBM)


def to_dense(rows):
    return jnp.concatenate(rows, axis=0).T


def row_of(turn, dy):
    return dy + turn * (TAPS - 1 - 2 * dy)


def both_clocks(turn, mine, other):
    first = turn == 0
    return jnp.where(first, mine[0:1, :], other[0:1, :]), jnp.where(first, other[0:1, :], mine[0:1, :])


def embed(turn, mine, other, time_w):
    low, high = both_clocks(turn, mine, other)
    steps = jnp.concatenate([low[:, 0:1], low[:, 1:2], high[:, 0:1], high[:, 1:2]] * 2, axis=0)
    lane = lax.broadcasted_iota(jnp.int32, (1, LANES), 1).astype(F32)
    angle = steps * jnp.exp(lane * (-math.log(10000.0) / LANES))
    feats = jnp.concatenate([jnp.sin(angle), jnp.cos(angle)], axis=1)
    return lax.dot_general(feats, time_w[...], (((1,), (0,)), ((), ())), precision=HIGH, preferred_element_type=F32)


def make_weff(turn, in_w, taps, weff):
    weff[...] = jnp.zeros_like(weff)
    for dy in range(TAPS):
        for dx in range(TAPS):
            low = dy * LANES + dx * CHAN
            weff[low : low + CHAN, :] = (in_w[...] * taps[row_of(turn, dy), dx, 0:1, :]).astype(BF16)


def make_by_row(turn, taps, by_row):
    column = lax.broadcasted_iota(jnp.int32, (COLS, WIDTH), 0)
    for dy in range(TAPS):
        total = jnp.zeros((COLS, WIDTH), F32)
        for dx in range(TAPS):
            ok = (column + (dx - HALO) >= 0) & (column + (dx - HALO) < COLS)
            total = total + jnp.where(ok, taps[row_of(turn, dy), dx, 0:1, :], 0.0)
        by_row[dy] = total


def three_in(in_w):
    hi, lo = split(in_w[...])
    return jnp.concatenate([hi, hi, lo, jnp.zeros((LANES - 3 * CHAN, WIDTH), BF16)], axis=0)


def block_zero(sums, place, first, count, weff, in_three, shift, patch, centre, spread, three):
    rows = count + REACH
    hi, lo = split(jnp.concatenate(sums, axis=0))

    def spots(flat):
        for k in range(len(sums)):
            for j in range(OWN):
                i = place(k, j)
                if i is not None:
                    yield i, flat[k * COLS : (k + 1) * COLS, j * LANES : (j + 1) * LANES]

    for i, x in spots(dot(hi, spread)):
        shift[i, PAD : PAD + COLS, :] = x
    for i, x in spots(dot(jnp.concatenate([hi, lo], axis=-1), three)):
        if HALO <= i < HALO + count:
            centre[i - HALO] = x.astype(BF16)
    group = lane_group((1, 1, LANES))
    at = PAD - HALO
    picked = shift[0:rows, at : at + COLS, :]
    for dx in range(1, TAPS):
        picked = jnp.where(group == dx, shift[0:rows, at + dx : at + dx + COLS, :], picked)
    patch[...] = picked.astype(BF16)
    wide = [patch[dy : dy + count].reshape(count * COLS, LANES) for dy in range(TAPS)]
    base = dot(jnp.concatenate(wide, axis=-1), weff[...])
    return base, dot(centre[...].reshape(count * COLS, LANES), in_three)


def pointwise(get, block, up_w, up_b, down_w, put):
    hidden = []

    def piece(low):
        upper = dot(get(), up_w[block, :, low : low + CHUNK]) + up_b[block : block + 1, low : low + CHUNK]
        hidden.append(gelu(upper))

    steps = [functools.partial(piece, low) for low in range(0, HIDDEN, CHUNK)]
    steps.append(lambda: put(dot(jnp.concatenate(hidden, axis=-1), down_w[block])))
    return steps


def depthwise(turn, taps, source, pairs, begin, done):
    def piece(half, heights):
        lanes = slice(half * LANES, (half + 1) * LANES)
        acc = {h: begin(h, half) for h in heights}
        needed = sorted({i for h in heights for i in pairs[h]})
        for dx in range(TAPS):
            for i in needed:
                x = source(i, half, dx)
                for h in heights:
                    if i in pairs[h]:
                        acc[h] = acc[h] + x * taps[row_of(turn, i - h + HALO), dx, 1:2, lanes]
        for h in heights:
            done(h, half, acc[h])

    heights = sorted(pairs)
    groups = [heights[i : i + 4] for i in range(0, len(heights), 4)]
    return [functools.partial(piece, half, group) for half in range(2) for group in groups]


NEAR = range(HALO, OWN + HALO)
EDGE = range(-HALO, HALO)


def pairs_of(rows):
    found = {h: [i for i in rows if abs(i - h) <= HALO] for h in range(OWN)}
    return {h: listed for h, listed in found.items() if listed}


def near_kernel(last, *refs):
    if last:
        (flags, own, inner, mine, inner_terms, temb, weff, by_row, up_w, down_w, in_w, taps, gain, up_b,
         partial, kept, shift, patch, centre, *wide) = refs
        turn = flags[0]
        copies = []
    else:
        (flags, own, inner, clock, other_clock, time_w, up_hbm, down_hbm, in_w, taps, gain, up_b,
         partial, kept, temb, weff, by_row, up_w, down_w, shift, patch, centre, *wide, sems) = refs
        turn = flags[0]
        copies = []
        for block in range(2):
            copies.append(pltpu.make_async_copy(up_hbm.at[block], up_w.at[block], sems.at[2 * block]))
            copies.append(pltpu.make_async_copy(down_hbm.at[block], down_w.at[block], sems.at[2 * block + 1]))
        for copy in copies:
            copy.start()
        make_weff(turn, in_w, taps, weff)
        make_by_row(turn, taps, by_row)
        temb[...] = embed(turn, clock, other_clock, time_w)
    first_time = 1 if last else 0
    count = len(NEAR)
    ones = by_row[0]
    for dy in range(1, TAPS):
        ones = ones + by_row[dy]
    ones = jnp.concatenate([ones] * count, axis=0)
    shift[...] = jnp.zeros_like(shift)
    for ref in wide:
        ref[...] = jnp.zeros_like(ref)
    spread = spreader(lambda g: g >= 0)
    three = jnp.concatenate([spreader(lambda g: (g == 0) | (g == 2)), spreader(lambda g: g == 1)], axis=0)
    in_three = three_in(in_w)

    def place(k, j):
        i = j if k == 0 else 2 * OWN - 1 - j
        return i if i < count + REACH else None

    state = {"sums": [own[...], inner[...]]}

    def first_block(t):
        held = {}

        def begin():
            if last:
                state["sums"] = [state["sums"][0] + mine[t], state["sums"][1] + inner_terms[t].astype(F32)]
            if last or t == 0:
                state["base"], state["stream"] = block_zero(
                    state["sums"], place, HALO, count, weff, in_three, shift, patch, centre, spread, three
                )
            shown = temb[first_time + t : first_time + t + 1, :]
            held["normed"] = normalise(state["base"] + ones * shown, gain[0:1, :])
            held["stream"] = state["stream"] + shown
            if t == 0 and copies:
                copies[0].wait()
                copies[1].wait()

        def put(x):
            after = (held["stream"] + x).reshape(count, COLS, WIDTH)
            kept[t] = after[0 : OWN - HALO]
            for half in range(2):
                wide[2 * t + half][:, PAD : PAD + COLS, :] = after[:, :, half * LANES : (half + 1) * LANES]

        return [begin] + pointwise(lambda: held["normed"], 0, up_w, up_b, down_w, put)

    def taps_of(t):
        def source(i, half, dx):
            at = PAD - HALO + dx
            return wide[2 * t + half][i - HALO, at : at + COLS, :]

        def done(h, half, x):
            partial[2 * t + half, h] = x

        return depthwise(turn, taps, source, pairs_of(NEAR), lambda h, half: jnp.zeros((COLS, LANES), F32), done)

    interleave(first_block(0), [])
    for t in range(1, TIMES):
        interleave(first_block(t), taps_of(t - 1))
    interleave(taps_of(TIMES - 1), [])
    for copy in copies[2:]:
        copy.wait()


def edge_kernel(last, *refs):
    if last:
        flags, outer, own, outer_terms, mine, *refs = refs
    else:
        flags, outer, own, *refs = refs
    (clock, other_clock, partial, kept, temb, weff, by_row, up_w, down_w, in_w, taps, gain, up_b, out_t,
     first_out, second_out, shift, patch, centre, *wide) = refs
    conv_buf = wide[2 * TIMES :]
    turn, inside = flags[0], flags[1].astype(F32)
    first_time = 1 if last else 0
    count = len(EDGE)
    ones = []
    for r in EDGE:
        total = jnp.zeros((COLS, WIDTH), F32)
        for dy in range(TAPS):
            total = total + (by_row[dy] if r + dy - HALO >= 0 else by_row[dy] * inside)
        ones.append(total)
    ones = jnp.concatenate(ones, axis=0)
    shift[...] = jnp.zeros_like(shift)
    for ref in wide[: 2 * TIMES]:
        ref[...] = jnp.zeros_like(ref)
    spread = spreader(lambda g: g >= 0)
    three = jnp.concatenate([spreader(lambda g: (g == 0) | (g == 2)), spreader(lambda g: g == 1)], axis=0)
    in_three = three_in(in_w)
    out_hi, out_lo = split(jnp.concatenate([out_t[...]] * 8, axis=0))
    out_three = jnp.concatenate([out_hi, out_hi, out_lo], axis=-1)
    low, high = both_clocks(turn, clock, other_clock)
    sizes = [low[:, 2:3], low[:, 3:4], high[:, 2:3], high[:, 3:4]]
    group = lane_group((1, LANES))

    def place(k, j):
        if k == 0:
            return REACH - 1 - j if j < REACH else None
        return REACH + j if j < REACH else None

    state = {"sums": [outer[...], own[...]]}
    terms = [None] * TIMES

    def first_block(t):
        held = {}

        def begin():
            if last:
                state["sums"] = [state["sums"][0] + outer_terms[t].astype(F32), state["sums"][1] + mine[t]]
                if t == 0:
                    state["n0"] = state["sums"][1]
            if last or t == 0:
                state["base"], state["stream"] = block_zero(
                    state["sums"], place, -HALO, count, weff, in_three, shift, patch, centre, spread, three
                )
            shown = temb[first_time + t : first_time + t + 1, :]
            held["normed"] = normalise(state["base"] + ones * shown, gain[0:1, :])
            held["stream"] = state["stream"] + shown

        def put(x):
            after = (held["stream"] + x).reshape(count, COLS, WIDTH)
            for half in range(2):
                lanes = slice(half * LANES, (half + 1) * LANES)
                wide[2 * t + half][0:HALO, PAD : PAD + COLS, :] = after[0:HALO, :, lanes] * inside
                wide[2 * t + half][HALO:, PAD : PAD + COLS, :] = after[HALO:, :, lanes]

        return [begin] + pointwise(lambda: held["normed"], 0, up_w, up_b, down_w, put)

    def taps_of(t):
        def source(i, half, dx):
            at = PAD - HALO + dx
            return wide[2 * t + half][i + HALO, at : at + COLS, :]

        def done(h, half, x):
            conv_buf[t][h, :, half * LANES : (half + 1) * LANES] = x

        return depthwise(turn, taps, source, pairs_of(EDGE), lambda h, half: partial[2 * t + half, h], done)

    def second_block(t):
        held = {}
        touched = len(pairs_of(EDGE))

        def begin():
            conv = [conv_buf[t][...].reshape(touched * COLS, WIDTH)]
            rest = [partial[2 * t + half, touched:].reshape((OWN - touched) * COLS, LANES) for half in range(2)]
            conv.append(jnp.concatenate(rest, axis=-1))
            held["normed"] = normalise(jnp.concatenate(conv, axis=0), gain[1:2, :])

        def put(x):
            ends = [wide[2 * t + half][HALO:, PAD : PAD + COLS, :].reshape(HALO * COLS, LANES) for half in range(2)]
            stream = [jnp.concatenate(ends, axis=-1), kept[t].reshape((OWN - HALO) * COLS, WIDTH)]
            hi, lo = split(jnp.concatenate(stream, axis=0) + x)
            drift = dot_nt(jnp.concatenate([hi, lo, hi], axis=-1), out_three) * sizes[first_time + t]
            drift = drift.reshape(OWN, COLS, LANES)
            dense = drift[0]
            for j in range(1, OWN):
                dense = jnp.where(group == j, drift[j], dense)
            terms[t] = dense

        return [begin] + pointwise(lambda: held["normed"], 1, up_w, up_b, down_w, put)

    interleave(first_block(0), [])
    for t in range(1, TIMES):
        interleave(first_block(t), taps_of(t - 1))
    interleave(second_block(0), taps_of(TIMES - 1))
    for t in range(1, TIMES):
        interleave(second_block(t), [])
    if last:
        n0 = state["n0"]
        n1 = n0 + terms[0]
        n2 = n1 + terms[1]
        n3 = n2 + terms[2]
        turned = turn == 1
        for i, (early, late) in enumerate(((n0, n2), (n1, n3))):
            first_out[i] = jnp.where(turned, late, early)
            second_out[i] = jnp.where(turned, early, late)
    else:
        for t in range(TIMES):
            first_out[t] = terms[t]
            second_out[t] = terms[t].astype(BF16)


SMEM = pl.BlockSpec(memory_space=pltpu.SMEM)
VMEM = pl.BlockSpec(memory_space=pltpu.VMEM)
HBM = pl.BlockSpec(memory_space=pltpu.HBM)
SMALL = pltpu.CompilerParams(vmem_limit_bytes=4 * 2**20)
LARGE = pltpu.CompilerParams(vmem_limit_bytes=20 * 2**20)


def working(count):
    return [
        pltpu.VMEM((count + REACH, WIDE, LANES), F32),
        pltpu.VMEM((count + REACH, COLS, LANES), BF16),
        pltpu.VMEM((count, COLS, LANES), BF16),
    ] + [pltpu.VMEM((count, WIDE, LANES), F32)] * (2 * TIMES)


def near(last, up_w, down_w, *args):
    outs = [pltpu.VMEM((2 * TIMES, OWN, COLS, LANES), F32), pltpu.VMEM((TIMES, OWN - HALO, COLS, WIDTH), F32)]
    scratch = working(len(NEAR))
    if last:
        specs = [SMEM] + [VMEM] * (len(args) - 1)
    else:
        outs += [pltpu.VMEM((8, WIDTH), F32), pltpu.VMEM((TAPS * LANES, WIDTH), BF16), pltpu.VMEM((TAPS, COLS, WIDTH), F32)]
        outs += [pltpu.VMEM(up_w.shape, BF16), pltpu.VMEM(down_w.shape, BF16)]
        scratch += [pltpu.SemaphoreType.DMA((4,))]
        specs = [SMEM] + [VMEM] * 5 + [HBM] * 2 + [VMEM] * 4
    return pl.pallas_call(
        functools.partial(near_kernel, last),
        out_shape=outs,
        in_specs=specs,
        out_specs=[VMEM] * len(outs),
        scratch_shapes=scratch,
        compiler_params=LARGE,
    )(*args)


def edge(last, *args):
    if last:
        outs = [jax.ShapeDtypeStruct((2, COLS, LANES), F32)] * 2
    else:
        outs = [jax.ShapeDtypeStruct((TIMES, COLS, LANES), kind) for kind in (F32, BF16)]
    touched = len(pairs_of(EDGE))
    return pl.pallas_call(
        functools.partial(edge_kernel, last),
        out_shape=outs,
        in_specs=[SMEM] + [VMEM] * (len(args) - 1),
        out_specs=[VMEM, VMEM],
        scratch_shapes=working(len(EDGE)) + [pltpu.VMEM((touched, COLS, WIDTH), F32)] * TIMES,
        compiler_params=LARGE,
    )(*args)


def prepare(flags, times, sizes, turned_start):
    dense = jax.ShapeDtypeStruct((COLS, LANES), F32)
    return pl.pallas_call(
        prepare_kernel,
        out_shape=[dense, dense, jax.ShapeDtypeStruct((8, LANES), F32)],
        in_specs=[SMEM, SMEM, SMEM, VMEM],
        out_specs=[VMEM] * 3,
        compiler_params=SMALL,
    )(flags, times, sizes, turned_start)


def finish(flags, keep, got):
    return pl.pallas_call(
        finish_kernel,
        out_shape=jax.ShapeDtypeStruct((2, 2 * OWN, CHAN, COLS), F32),
        in_specs=[SMEM, VMEM, VMEM],
        out_specs=VMEM,
        compiler_params=SMALL,
    )(flags, keep, got)


def on_device(
    start_state, timesteps, step_sizes, in_weight, time_weight, conv_kernel, norm_gain, up_weight, up_bias, down_weight, out_weight,
):
    space = lax.axis_size("space")
    s, tm = lax.axis_index("space"), lax.axis_index("tm")
    beside = [(0, 1), (1, 0)]
    across = []
    for i in range(space - 1):
        across += [(2 * i + 1, 2 * i + 2), (2 * i + 2, 2 * i + 1)]

    def over_tm(x):
        return lax.ppermute(x, "tm", beside)

    def over_space(x):
        return lax.ppermute(x, ("space", "tm"), across)

    flags = jnp.stack([tm, jnp.where(tm == 0, s > 0, s < space - 1).astype(jnp.int32)]).astype(jnp.int32)
    own, inner, clock = prepare(flags, timesteps, step_sizes, start_state.transpose(0, 2, 1))
    outer = over_space(own)
    other_clock = over_tm(clock)
    taps = conv_kernel.transpose(1, 2, 0, 3)
    up_hbm, down_hbm = pinned(up_weight), pinned(down_weight)

    partial, kept, *made = near(
        False, up_weight, down_weight,
        flags, own, inner, clock, other_clock, time_weight, up_hbm, down_hbm, in_weight, taps, norm_gain, up_bias,
    )
    rest = (in_weight, taps, norm_gain, up_bias, out_weight.T)
    terms, sent = edge(False, flags, outer, own, clock, other_clock, partial, kept, *made, *rest)
    inner_terms, outer_terms = over_tm(sent), over_space(sent)
    partial, kept = near(True, up_weight, down_weight, flags, own, inner, terms, inner_terms, *made, *rest[:-1])
    keep, give = edge(True, flags, outer, own, outer_terms, terms, clock, other_clock, partial, kept, *made, *rest)
    return finish(flags, keep, over_tm(give)).transpose(0, 1, 3, 2)


def solution(mesh):
    both = P(("groups", "tm"))
    return jax.shard_map(
        on_device,
        mesh=mesh,
        in_specs=(P(("groups", "space"), None, None), both, both) + (P(),) * 8,
        out_specs=P("tm", ("groups", "space"), None, None),
        check_vma=False,
    )
```

```python
import functools
import math

import jax
import jax.numpy as jnp
from jax import lax
from jax.experimental import pallas as pl
from jax.experimental.pallas import tpu as pltpu
from jax.sharding import PartitionSpec as P

HIGH = lax.Precision.HIGHEST
F32, BF16 = jnp.float32, jnp.bfloat16
COLS, CHAN, WIDTH, HIDDEN, LANES = 32, 16, 256, 1024, 128
OWN, TAPS, HALO = 8, 7, 3
REACH = 2 * HALO
PAD = 8
WIDE = COLS + 2 * PAD
TIMES = 3
CHUNK = 256


def split(x):
    hi = x.astype(BF16)
    return hi, (x - hi.astype(F32)).astype(BF16)


def dot(a, b):
    return lax.dot_general(a, b, (((1,), (0,)), ((), ())), preferred_element_type=F32)


def dot_nt(a, b):
    return lax.dot_general(a, b, (((1,), (1,)), ((), ())), preferred_element_type=F32)


def lane_group(shape):
    return lax.broadcasted_iota(jnp.int32, shape, len(shape) - 1) // CHAN


def make_spread(spread, three):
    row = lax.broadcasted_iota(jnp.int32, (CHAN, LANES), 0)
    col = lax.broadcasted_iota(jnp.int32, (CHAN, LANES), 1)
    hit, group = row == col % CHAN, col // CHAN
    spread[...] = jnp.zeros_like(spread)
    three[...] = jnp.zeros_like(three)

    def cells(where):
        return jnp.where(where, 1.0, 0.0).astype(BF16)

    for j in range(OWN):
        rows, lanes = slice(j * CHAN, (j + 1) * CHAN), slice(j * LANES, (j + 1) * LANES)
        spread[rows, lanes] = cells(hit)
        three[rows, lanes] = cells(hit & ((group == 0) | (group == 2)))
        three[LANES + j * CHAN : LANES + (j + 1) * CHAN, lanes] = cells(hit & (group == 1))


def normalise(conv, gain):
    mean = jnp.mean(conv, axis=-1, keepdims=True)
    centered = conv - mean
    var = jnp.mean(centered * centered, axis=-1, keepdims=True)
    return (centered * lax.rsqrt(var + 1e-06) * gain).astype(BF16)


def gelu(x):
    x = x.astype(BF16)
    inner = x * (BF16(0.7978845608028654) + BF16(0.035677408136300125) * (x * x))
    half = BF16(0.5) * x
    return half + half * jnp.tanh(inner)


def prepare_kernel(flags, times, sizes, start, own, inner, clock):
    turned = flags[0] == 1
    top = to_dense([start[h] for h in range(OWN)])
    bottom = to_dense([start[2 * OWN - 1 - h] for h in range(OWN)])
    own[...] = jnp.where(turned, bottom, top)
    inner[...] = jnp.where(turned, top, bottom)
    lane = lax.broadcasted_iota(jnp.int32, (8, LANES), 1)
    values = (times[0].astype(F32), times[1].astype(F32), sizes[0], sizes[1])
    filled = jnp.zeros((8, LANES), F32)
    for i, value in enumerate(values):
        filled = jnp.where(lane == i, value, filled)
    clock[...] = filled


def finish_kernel(flags, keep, got, out):
    turned = flags[0] == 1
    for t in range(2):
        top = jnp.where(turned, got[t], keep[t])
        bottom = jnp.where(turned, keep[t], got[t])
        out[t, 0:OWN] = top.T.reshape(OWN, CHAN, COLS)
        flipped = bottom.T.reshape(OWN, CHAN, COLS)
        for h in range(OWN):
            out[t, 2 * OWN - 1 - h] = flipped[h]


def pinned(x):
    return pltpu.with_memory_space_constraint(x, pltpu.HBM)


def to_dense(rows):
    return jnp.concatenate(rows, axis=0).T


def row_of(turn, dy):
    return dy + turn * (TAPS - 1 - 2 * dy)


def both_clocks(turn, mine, other):
    first = turn == 0
    return jnp.where(first, mine[0:1, :], other[0:1, :]), jnp.where(first, other[0:1, :], mine[0:1, :])


def embed(turn, mine, other, time_w):
    low, high = both_clocks(turn, mine, other)
    steps = jnp.concatenate([low[:, 0:1], low[:, 1:2], high[:, 0:1], high[:, 1:2]] * 2, axis=0)
    lane = lax.broadcasted_iota(jnp.int32, (1, LANES), 1).astype(F32)
    angle = steps * jnp.exp(lane * (-math.log(10000.0) / LANES))
    feats = jnp.concatenate([jnp.sin(angle), jnp.cos(angle)], axis=1)
    return lax.dot_general(feats, time_w[...], (((1,), (0,)), ((), ())), precision=HIGH, preferred_element_type=F32)


def make_weff(turn, in_w, taps, weff):
    weff[...] = jnp.zeros_like(weff)
    for dy in range(TAPS):
        for dx in range(TAPS):
            low = dy * LANES + dx * CHAN
            weff[low : low + CHAN, :] = (in_w[...] * taps[row_of(turn, dy), dx, 0:1, :]).astype(BF16)


def make_by_row(turn, taps, by_row):
    column = lax.broadcasted_iota(jnp.int32, (COLS, WIDTH), 0)
    for dy in range(TAPS):
        total = jnp.zeros((COLS, WIDTH), F32)
        for dx in range(TAPS):
            ok = (column + (dx - HALO) >= 0) & (column + (dx - HALO) < COLS)
            total = total + jnp.where(ok, taps[row_of(turn, dy), dx, 0:1, :], 0.0)
        by_row[dy] = total


def make_in_three(in_w, in_three):
    hi, lo = split(in_w[...])
    in_three[...] = jnp.concatenate([hi, hi, lo, jnp.zeros((LANES - 3 * CHAN, WIDTH), BF16)], axis=0)


def make_tap_rows(turn, taps, tap_rows):
    for dy in range(TAPS):
        for dx in range(TAPS):
            for half in range(2):
                lanes = slice(half * LANES, (half + 1) * LANES)
                tap_rows[half, dy * TAPS + dx : dy * TAPS + dx + 1, :] = taps[row_of(turn, dy), dx, 1:2, lanes]


def clear_sides(ref):
    side = jnp.zeros(ref.shape[:-2] + (PAD, LANES), F32)
    ref[..., 0:PAD, :] = side
    ref[..., PAD + COLS :, :] = side


def block_zero(states, place, count, weff, in_three, shift, patch, centre, spread, three):
    rows, many, blocks = count + REACH, len(states), len(states[0])
    hi, lo = split(jnp.concatenate([block for state in states for block in state], axis=0))

    def spots(flat):
        for n in range(many):
            for k in range(blocks):
                low = (n * blocks + k) * COLS
                for j in range(OWN):
                    i = place(k, j)
                    if i is not None:
                        yield n, i, flat[low : low + COLS, j * LANES : (j + 1) * LANES]

    clear_sides(shift)
    for n, i, x in spots(dot(hi, spread[...])):
        shift[n, i, PAD : PAD + COLS, :] = x
    for n, i, x in spots(dot(jnp.concatenate([hi, lo], axis=-1), three[...])):
        if HALO <= i < HALO + count:
            centre[n, i - HALO] = x.astype(BF16)
    group = lane_group((1, 1, 1, LANES))
    at = PAD - HALO
    picked = shift[0:many, :, at : at + COLS, :]
    for dx in range(1, TAPS):
        picked = jnp.where(group == dx, shift[0:many, :, at + dx : at + dx + COLS, :], picked)
    patch[0:many] = picked.astype(BF16)
    cells = many * count * COLS
    wide = [patch[0:many, dy : dy + count].reshape(cells, LANES) for dy in range(TAPS)]
    base = dot(jnp.concatenate(wide, axis=-1), weff[...])
    stream = dot(centre[0:many].reshape(cells, LANES), in_three[...])
    shape = (many, count, COLS, WIDTH)
    return base.reshape(shape), stream.reshape(shape)


def first_block(states, place, count, ones, first_time, temb, gain, up_w, up_b, down_w, weff, in_three, *scratch):
    base, stream = block_zero(states, place, count, weff, in_three, *scratch)
    normed, residual = [], []
    for t in range(TIMES):
        n = min(t, len(states) - 1)
        shown = temb[first_time + t : first_time + t + 1, :]
        conv = base[n] + ones * shown
        normed.append(normalise(conv.reshape(count * COLS, WIDTH), gain[0:1, :]))
        residual.append(stream[n] + shown)
    out = pointwise(jnp.concatenate(normed, axis=0), 0, up_w, up_b, down_w).reshape(TIMES, count, COLS, WIDTH)
    return [residual[t] + out[t] for t in range(TIMES)]


def pointwise(normed, block, up_w, up_b, down_w):
    hidden = []
    for low in range(0, HIDDEN, CHUNK):
        hidden.append(gelu(dot(normed, up_w[block, :, low : low + CHUNK]) + up_b[block : block + 1, low : low + CHUNK]))
    return dot(jnp.concatenate(hidden, axis=-1), down_w[block])


def depthwise(tap_rows, source, pairs, begin, done):
    heights = sorted(pairs)
    groups = [heights[i : i + 4] for i in range(0, len(heights), 4)]
    for half in range(2):
        for group in groups:
            acc = {h: begin(h, half) for h in group}
            needed = sorted({i for h in group for i in pairs[h]})
            for dx in range(TAPS):
                for i in needed:
                    x = source(i, half, dx)
                    for h in group:
                        if i in pairs[h]:
                            at = (i - h + HALO) * TAPS + dx
                            acc[h] = acc[h] + x * tap_rows[half, at : at + 1, :]
            for h in group:
                done(h, half, acc[h])


NEAR = range(HALO, OWN + HALO)
EDGE = range(-HALO, HALO)


def pairs_of(rows):
    found = {h: [i for i in rows if abs(i - h) <= HALO] for h in range(OWN)}
    return {h: listed for h, listed in found.items() if listed}


def near_kernel(last, *refs):
    first_time = 1 if last else 0
    count = len(NEAR)
    if last:
        (flags, own, inner, mine, inner_terms, temb, weff, by_row, tap_rows, spread, three, in_three, up_w, down_w, gain, up_b,
         partial, kept, shift, patch, centre, *wide) = refs
        turn = flags[0]
        states, state = [], [own[...], inner[...]]
        for t in range(TIMES):
            state = [state[0] + mine[t], state[1] + inner_terms[t].astype(F32)]
            states.append(state)
    else:
        (flags, own, inner, clock, other_clock, time_hbm, up_hbm, down_hbm, in_w, taps, gain, up_b,
         partial, kept, temb, weff, by_row, tap_rows, spread, three, in_three, up_w, down_w,
         shift, patch, centre, *wide, time_w, sems) = refs
        turn = flags[0]
        copies = [pltpu.make_async_copy(time_hbm, time_w, sems.at[4])]
        for block in range(2):
            copies.append(pltpu.make_async_copy(up_hbm.at[block], up_w.at[block], sems.at[2 * block]))
            copies.append(pltpu.make_async_copy(down_hbm.at[block], down_w.at[block], sems.at[2 * block + 1]))
        for copy in copies:
            copy.start()
        make_weff(turn, in_w, taps, weff)
        make_by_row(turn, taps, by_row)
        make_tap_rows(turn, taps, tap_rows)
        make_spread(spread, three)
        make_in_three(in_w, in_three)
        copies[0].wait()
        temb[...] = embed(turn, clock, other_clock, time_w)
        states = [[own[...], inner[...]]]
        copies[1].wait()
        copies[2].wait()
    ones = by_row[0]
    for dy in range(1, TAPS):
        ones = ones + by_row[dy]
    for ref in wide:
        clear_sides(ref)

    def place(k, j):
        i = j if k == 0 else 2 * OWN - 1 - j
        return i if i < count + REACH else None

    after = first_block(
        states, place, count, ones[None], first_time, temb, gain, up_w, up_b, down_w, weff, in_three,
        shift, patch, centre, spread, three,
    )
    for t in range(TIMES):
        kept[t] = after[t][0 : OWN - HALO]
        for half in range(2):
            wide[2 * t + half][:, PAD : PAD + COLS, :] = after[t][:, :, half * LANES : (half + 1) * LANES]
    for t in range(TIMES):

        def source(i, half, dx):
            at = PAD - HALO + dx
            return wide[2 * t + half][i - HALO, at : at + COLS, :]

        def done(h, half, x):
            partial[2 * t + half, h] = x

        depthwise(tap_rows, source, pairs_of(NEAR), lambda h, half: jnp.zeros((COLS, LANES), F32), done)
    if not last:
        copies[3].wait()
        copies[4].wait()


def edge_kernel(last, *refs):
    if last:
        flags, outer, own, outer_terms, mine, *refs = refs
    else:
        flags, outer, own, *refs = refs
    (clock, other_clock, partial, kept, temb, weff, by_row, tap_rows, spread, three, in_three, up_w, down_w, gain, up_b, out_t,
     first_out, second_out, shift, patch, centre, *wide) = refs
    conv_buf = wide[2 * TIMES :]
    turn, inside = flags[0], flags[1].astype(F32)
    first_time = 1 if last else 0
    count = len(EDGE)
    ones = []
    for r in EDGE:
        seen = jnp.zeros((COLS, WIDTH), F32)
        hidden = jnp.zeros((COLS, WIDTH), F32)
        for dy in range(TAPS):
            if r + dy - HALO >= 0:
                seen = seen + by_row[dy]
            else:
                hidden = hidden + by_row[dy]
        ones.append(seen + hidden * inside)
    ones = jnp.concatenate(ones, axis=0).reshape(count, COLS, WIDTH)
    for ref in wide[: 2 * TIMES]:
        clear_sides(ref)
    out_hi, out_lo = split(jnp.concatenate([out_t[...]] * 8, axis=0))
    out_three = jnp.concatenate([out_hi, out_hi, out_lo], axis=-1)
    low, high = both_clocks(turn, clock, other_clock)
    sizes = [low[:, 2:3], low[:, 3:4], high[:, 2:3], high[:, 3:4]]
    group = lane_group((1, LANES))

    def place(k, j):
        if j >= REACH:
            return None
        return REACH - 1 - j if k == 0 else REACH + j

    states, state = [], [outer[...], own[...]]
    for t in range(TIMES if last else 0):
        state = [state[0] + outer_terms[t].astype(F32), state[1] + mine[t]]
        states.append(state)
    after = first_block(
        states if last else [state], place, count, ones, first_time, temb, gain, up_w, up_b, down_w, weff, in_three,
        shift, patch, centre, spread, three,
    )
    for t in range(TIMES):
        for half in range(2):
            lanes = slice(half * LANES, (half + 1) * LANES)
            wide[2 * t + half][0:HALO, PAD : PAD + COLS, :] = after[t][0:HALO, :, lanes] * inside
            wide[2 * t + half][HALO:, PAD : PAD + COLS, :] = after[t][HALO:, :, lanes]
    touched = len(pairs_of(EDGE))
    normed, stream = [], []
    for t in range(TIMES):

        def source(i, half, dx):
            at = PAD - HALO + dx
            return wide[2 * t + half][i + HALO, at : at + COLS, :]

        def done(h, half, x):
            conv_buf[t][h, :, half * LANES : (half + 1) * LANES] = x

        depthwise(tap_rows, source, pairs_of(EDGE), lambda h, half: partial[2 * t + half, h], done)
        rest = [partial[2 * t + half, touched:].reshape((OWN - touched) * COLS, LANES) for half in range(2)]
        conv = [conv_buf[t][...].reshape(touched * COLS, WIDTH), jnp.concatenate(rest, axis=-1)]
        normed.append(normalise(jnp.concatenate(conv, axis=0), gain[1:2, :]))
        stream += [after[t][HALO:].reshape(HALO * COLS, WIDTH), kept[t].reshape((OWN - HALO) * COLS, WIDTH)]
    out = pointwise(jnp.concatenate(normed, axis=0), 1, up_w, up_b, down_w)
    hi, lo = split(jnp.concatenate(stream, axis=0) + out)
    drifts = dot_nt(jnp.concatenate([hi, lo, hi], axis=-1), out_three).reshape(TIMES, OWN, COLS, LANES)
    terms = []
    for t in range(TIMES):
        dense = drifts[t, 0]
        for j in range(1, OWN):
            dense = jnp.where(group == j, drifts[t, j], dense)
        terms.append(dense * sizes[first_time + t])
    if last:
        n0 = states[0][1]
        n1 = n0 + terms[0]
        n2 = n1 + terms[1]
        n3 = n2 + terms[2]
        turned = turn == 1
        for i, (early, late) in enumerate(((n0, n2), (n1, n3))):
            first_out[i] = jnp.where(turned, late, early)
            second_out[i] = jnp.where(turned, early, late)
    else:
        for t in range(TIMES):
            first_out[t] = terms[t]
            second_out[t] = terms[t].astype(BF16)


SMEM = pl.BlockSpec(memory_space=pltpu.SMEM)
VMEM = pl.BlockSpec(memory_space=pltpu.VMEM)
HBM = pl.BlockSpec(memory_space=pltpu.HBM)
SMALL = pltpu.CompilerParams(vmem_limit_bytes=4 * 2**20)
LARGE = pltpu.CompilerParams(vmem_limit_bytes=20 * 2**20)


def working(count, many):
    return [
        pltpu.VMEM((many, count + REACH, WIDE, LANES), F32),
        pltpu.VMEM((many, count + REACH, COLS, LANES), BF16),
        pltpu.VMEM((many, count, COLS, LANES), BF16),
    ] + [pltpu.VMEM((count, WIDE, LANES), F32)] * (2 * TIMES)


def near(last, up_w, down_w, *args):
    outs = [pltpu.VMEM((2 * TIMES, OWN, COLS, LANES), F32), pltpu.VMEM((TIMES, OWN - HALO, COLS, WIDTH), F32)]
    scratch = working(len(NEAR), TIMES if last else 1)
    if last:
        specs = [SMEM] + [VMEM] * (len(args) - 1)
    else:
        outs += [pltpu.VMEM((8, WIDTH), F32), pltpu.VMEM((TAPS * LANES, WIDTH), BF16), pltpu.VMEM((TAPS, COLS, WIDTH), F32)]
        outs += [pltpu.VMEM((2, 56, LANES), F32), pltpu.VMEM((LANES, OWN * LANES), BF16)]
        outs += [pltpu.VMEM((2 * LANES, OWN * LANES), BF16), pltpu.VMEM((LANES, WIDTH), BF16)]
        outs += [pltpu.VMEM(up_w.shape, BF16), pltpu.VMEM(down_w.shape, BF16)]
        scratch += [pltpu.VMEM((WIDTH, WIDTH), F32), pltpu.SemaphoreType.DMA((5,))]
        specs = [SMEM] + [VMEM] * 4 + [HBM] * 3 + [VMEM] * 4
    return pl.pallas_call(
        functools.partial(near_kernel, last),
        out_shape=outs,
        in_specs=specs,
        out_specs=[VMEM] * len(outs),
        scratch_shapes=scratch,
        compiler_params=LARGE,
    )(*args)


def edge(last, *args):
    if last:
        outs = [jax.ShapeDtypeStruct((2, COLS, LANES), F32)] * 2
    else:
        outs = [jax.ShapeDtypeStruct((TIMES, COLS, LANES), kind) for kind in (F32, BF16)]
    touched = len(pairs_of(EDGE))
    return pl.pallas_call(
        functools.partial(edge_kernel, last),
        out_shape=outs,
        in_specs=[SMEM] + [VMEM] * (len(args) - 1),
        out_specs=[VMEM, VMEM],
        scratch_shapes=working(len(EDGE), TIMES if last else 1) + [pltpu.VMEM((touched, COLS, WIDTH), F32)] * TIMES,
        compiler_params=LARGE,
    )(*args)


def prepare(flags, times, sizes, turned_start):
    dense = jax.ShapeDtypeStruct((COLS, LANES), F32)
    return pl.pallas_call(
        prepare_kernel,
        out_shape=[dense, dense, jax.ShapeDtypeStruct((8, LANES), F32)],
        in_specs=[SMEM, SMEM, SMEM, VMEM],
        out_specs=[VMEM] * 3,
        compiler_params=SMALL,
    )(flags, times, sizes, turned_start)


def finish(flags, keep, got):
    return pl.pallas_call(
        finish_kernel,
        out_shape=jax.ShapeDtypeStruct((2, 2 * OWN, CHAN, COLS), F32),
        in_specs=[SMEM, VMEM, VMEM],
        out_specs=VMEM,
        compiler_params=SMALL,
    )(flags, keep, got)


def on_device(
    start_state, timesteps, step_sizes, in_weight, time_weight, conv_kernel, norm_gain, up_weight, up_bias, down_weight, out_weight,
):
    space = lax.axis_size("space")
    s, tm = lax.axis_index("space"), lax.axis_index("tm")
    beside = [(0, 1), (1, 0)]
    across = []
    for i in range(space - 1):
        across += [(2 * i + 1, 2 * i + 2), (2 * i + 2, 2 * i + 1)]

    def over_tm(x):
        return lax.ppermute(x, "tm", beside)

    def over_space(x):
        return lax.ppermute(x, ("space", "tm"), across)

    flags = jnp.stack([tm, jnp.where(tm == 0, s > 0, s < space - 1).astype(jnp.int32)]).astype(jnp.int32)
    own, inner, clock = prepare(flags, pinned(timesteps), pinned(step_sizes), pinned(start_state.transpose(0, 2, 1)))
    other_clock = over_tm(clock)
    outer = over_space(own)
    taps = conv_kernel.transpose(1, 2, 0, 3)

    partial, kept, *made = near(
        False, up_weight, down_weight, flags, own, inner, clock, other_clock,
        pinned(time_weight), pinned(up_weight), pinned(down_weight), in_weight, taps, norm_gain, up_bias,
    )
    rest = (norm_gain, up_bias, out_weight.T)
    terms, sent = edge(False, flags, outer, own, clock, other_clock, partial, kept, *made, *rest)
    inner_terms, outer_terms = over_tm(sent), over_space(sent)
    partial, kept = near(True, up_weight, down_weight, flags, own, inner, terms, inner_terms, *made, *rest[:-1])
    keep, give = edge(True, flags, outer, own, outer_terms, terms, clock, other_clock, partial, kept, *made, *rest)
    return finish(flags, keep, over_tm(give)).transpose(0, 1, 3, 2)


def solution(mesh):
    both = P(("groups", "tm"))
    return jax.shard_map(
        on_device,
        mesh=mesh,
        in_specs=(P(("groups", "space"), None, None), both, both) + (P(),) * 8,
        out_specs=P("tm", ("groups", "space"), None, None),
        check_vma=False,
    )
```

```python
import functools
import math

import jax
import jax.numpy as jnp
from jax import lax
from jax.experimental import pallas as pl
from jax.experimental.pallas import tpu as pltpu
from jax.sharding import PartitionSpec as P

HIGH = lax.Precision.HIGHEST
F32, BF16 = jnp.float32, jnp.bfloat16
COLS, CHAN, WIDTH, HIDDEN, LANES = 32, 16, 256, 1024, 128
OWN, TAPS, HALO = 8, 7, 3
REACH = 2 * HALO
PAD = 8
WIDE = COLS + 2 * PAD
TIMES = 3
CHUNK = 256


def split(x):
    hi = x.astype(BF16)
    return hi, (x - hi.astype(F32)).astype(BF16)


def dot(a, b):
    return lax.dot_general(a, b, (((1,), (0,)), ((), ())), preferred_element_type=F32)


def dot_nt(a, b):
    return lax.dot_general(a, b, (((1,), (1,)), ((), ())), preferred_element_type=F32)


def lane_group(shape):
    return lax.broadcasted_iota(jnp.int32, shape, len(shape) - 1) // CHAN


def make_spread(spread, three):
    row = lax.broadcasted_iota(jnp.int32, (CHAN, LANES), 0)
    col = lax.broadcasted_iota(jnp.int32, (CHAN, LANES), 1)
    hit, group = row == col % CHAN, col // CHAN
    spread[...] = jnp.zeros_like(spread)
    three[...] = jnp.zeros_like(three)

    def cells(where):
        return jnp.where(where, 1.0, 0.0).astype(BF16)

    for j in range(OWN):
        rows, lanes = slice(j * CHAN, (j + 1) * CHAN), slice(j * LANES, (j + 1) * LANES)
        spread[rows, lanes] = cells(hit)
        three[rows, lanes] = cells(hit & ((group == 0) | (group == 2)))
        three[LANES + j * CHAN : LANES + (j + 1) * CHAN, lanes] = cells(hit & (group == 1))


def normalise(conv, gain):
    mean = jnp.mean(conv, axis=-1, keepdims=True)
    centered = conv - mean
    var = jnp.mean(centered * centered, axis=-1, keepdims=True)
    return (centered * lax.rsqrt(var + 1e-06) * gain).astype(BF16)


def gelu(x):
    x = x.astype(BF16)
    inner = x * (BF16(0.7978845608028654) + BF16(0.035677408136300125) * (x * x))
    half = BF16(0.5) * x
    return half + half * jnp.tanh(inner)


def prepare_kernel(flags, times, sizes, start, own, inner, clock):
    turned = flags[0] == 1
    top = to_dense([start[h] for h in range(OWN)])
    bottom = to_dense([start[2 * OWN - 1 - h] for h in range(OWN)])
    own[...] = jnp.where(turned, bottom, top)
    inner[...] = jnp.where(turned, top, bottom)
    lane = lax.broadcasted_iota(jnp.int32, (8, LANES), 1)
    values = (times[0].astype(F32), times[1].astype(F32), sizes[0], sizes[1])
    filled = jnp.zeros((8, LANES), F32)
    for i, value in enumerate(values):
        filled = jnp.where(lane == i, value, filled)
    clock[...] = filled


def finish_kernel(flags, keep, got, out):
    turned = flags[0] == 1
    for t in range(2):
        top = jnp.where(turned, got[t], keep[t])
        bottom = jnp.where(turned, keep[t], got[t])
        out[t, 0:OWN] = top.T.reshape(OWN, CHAN, COLS)
        flipped = bottom.T.reshape(OWN, CHAN, COLS)
        for h in range(OWN):
            out[t, 2 * OWN - 1 - h] = flipped[h]


def pinned(x):
    return pltpu.with_memory_space_constraint(x, pltpu.HBM)


def to_dense(rows):
    return jnp.concatenate(rows, axis=0).T


def row_of(turn, dy):
    return dy + turn * (TAPS - 1 - 2 * dy)


def both_clocks(turn, mine, other):
    first = turn == 0
    return jnp.where(first, mine[0:1, :], other[0:1, :]), jnp.where(first, other[0:1, :], mine[0:1, :])


def embed(turn, mine, other, time_w):
    low, high = both_clocks(turn, mine, other)
    steps = jnp.concatenate([low[:, 0:1], low[:, 1:2], high[:, 0:1], high[:, 1:2]] * 2, axis=0)
    lane = lax.broadcasted_iota(jnp.int32, (1, LANES), 1).astype(F32)
    angle = steps * jnp.exp(lane * (-math.log(10000.0) / LANES))
    feats = jnp.concatenate([jnp.sin(angle), jnp.cos(angle)], axis=1)
    return lax.dot_general(feats, time_w[...], (((1,), (0,)), ((), ())), precision=HIGH, preferred_element_type=F32)


def make_weff(turn, in_w, taps, weff):
    weff[...] = jnp.zeros_like(weff)
    for dy in range(TAPS):
        for dx in range(TAPS):
            low = dy * LANES + dx * CHAN
            weff[low : low + CHAN, :] = (in_w[...] * taps[row_of(turn, dy), dx, 0:1, :]).astype(BF16)


def make_by_row(turn, taps, by_row):
    column = lax.broadcasted_iota(jnp.int32, (COLS, WIDTH), 0)
    for dy in range(TAPS):
        total = jnp.zeros((COLS, WIDTH), F32)
        for dx in range(TAPS):
            ok = (column + (dx - HALO) >= 0) & (column + (dx - HALO) < COLS)
            total = total + jnp.where(ok, taps[row_of(turn, dy), dx, 0:1, :], 0.0)
        by_row[dy] = total


def make_in_three(in_w, in_three):
    hi, lo = split(in_w[...])
    in_three[...] = jnp.concatenate([hi, hi, lo, jnp.zeros((LANES - 3 * CHAN, WIDTH), BF16)], axis=0)


def make_tap_rows(turn, taps, tap_rows):
    for dy in range(TAPS):
        for dx in range(TAPS):
            for half in range(2):
                lanes = slice(half * LANES, (half + 1) * LANES)
                tap_rows[half, dy * TAPS + dx : dy * TAPS + dx + 1, :] = taps[row_of(turn, dy), dx, 1:2, lanes]


def clear_sides(ref):
    side = jnp.zeros(ref.shape[:-2] + (PAD, LANES), F32)
    ref[..., 0:PAD, :] = side
    ref[..., PAD + COLS :, :] = side


def block_zero(states, place, count, weff, in_three, shift, patch, centre, spread, three):
    rows, many, blocks = count + REACH, len(states), len(states[0])
    hi, lo = split(jnp.concatenate([block for state in states for block in state], axis=0))

    def spots(flat):
        for n in range(many):
            for k in range(blocks):
                low = (n * blocks + k) * COLS
                for j in range(OWN):
                    i = place(k, j)
                    if i is not None:
                        yield n, i, flat[low : low + COLS, j * LANES : (j + 1) * LANES]

    clear_sides(shift)
    for n, i, x in spots(dot(hi, spread[...])):
        shift[n, i, PAD : PAD + COLS, :] = x
    for n, i, x in spots(dot(jnp.concatenate([hi, lo], axis=-1), three[...])):
        if HALO <= i < HALO + count:
            centre[n, i - HALO] = x.astype(BF16)
    group = lane_group((COLS, LANES))
    at = PAD - HALO
    for n in range(many):
        for i in range(rows):
            picked = shift[n, i, at : at + COLS, :]
            for dx in range(1, TAPS):
                picked = jnp.where(group == dx, shift[n, i, at + dx : at + dx + COLS, :], picked)
            patch[n, i] = picked.astype(BF16)
    cells = many * count * COLS
    wide = [patch[0:many, dy : dy + count].reshape(cells, LANES) for dy in range(TAPS)]
    base = dot(jnp.concatenate(wide, axis=-1), weff[...])
    stream = dot(centre[0:many].reshape(cells, LANES), in_three[...])
    shape = (many, count, COLS, WIDTH)
    return base.reshape(shape), stream.reshape(shape)


def first_block(states, place, count, ones, first_time, temb, gain, up_w, up_b, down_w, weff, in_three, *scratch):
    *scratch, normed = scratch
    base, stream = block_zero(states, place, count, weff, in_three, *scratch)
    residual = []
    for t in range(TIMES):
        n = min(t, len(states) - 1)
        shown = temb[first_time + t : first_time + t + 1, :]
        lift = [ones[i] * shown for i in range(len(ones))]
        for i in range(count):
            low = (t * count + i) * COLS
            normed[low : low + COLS, :] = normalise(base[n, i] + lift[min(i, len(ones) - 1)], gain[0:1, :])
        residual.append(stream[n] + shown)
    out = pointwise(normed[...], 0, up_w, up_b, down_w).reshape(TIMES, count, COLS, WIDTH)
    return [residual[t] + out[t] for t in range(TIMES)]


def pointwise(normed, block, up_w, up_b, down_w):
    hidden = []
    for low in range(0, HIDDEN, CHUNK):
        hidden.append(gelu(dot(normed, up_w[block, :, low : low + CHUNK]) + up_b[block : block + 1, low : low + CHUNK]))
    return dot(jnp.concatenate(hidden, axis=-1), down_w[block])


def depthwise(tap_rows, source, pairs, begin, done):
    heights = sorted(pairs)
    groups = [heights[i : i + 4] for i in range(0, len(heights), 4)]
    for half in range(2):
        for group in groups:
            acc = {h: begin(h, half) for h in group}
            needed = sorted({i for h in group for i in pairs[h]})
            for dx in range(TAPS):
                for i in needed:
                    x = source(i, half, dx)
                    for h in group:
                        if i in pairs[h]:
                            at = (i - h + HALO) * TAPS + dx
                            acc[h] = acc[h] + x * tap_rows[half, at : at + 1, :]
            for h in group:
                done(h, half, acc[h])


NEAR = range(HALO, OWN + HALO)
EDGE = range(-HALO, HALO)


def pairs_of(rows):
    found = {h: [i for i in rows if abs(i - h) <= HALO] for h in range(OWN)}
    return {h: listed for h, listed in found.items() if listed}


def near_kernel(last, *refs):
    first_time = 1 if last else 0
    count = len(NEAR)
    if last:
        (flags, own, inner, mine, inner_terms, temb, weff, by_row, tap_rows, spread, three, in_three, _, up_w, down_w, gain, up_b,
         partial, kept, shift, patch, centre, normed, *wide) = refs
        turn = flags[0]
        states, state = [], [own[...], inner[...]]
        for t in range(TIMES):
            state = [state[0] + mine[t], state[1] + inner_terms[t].astype(F32)]
            states.append(state)
    else:
        (flags, own, inner, clock, other_clock, time_hbm, up_hbm, down_hbm, in_w, taps, gain, up_b, out_t,
         partial, kept, temb, weff, by_row, tap_rows, spread, three, in_three, out_three, up_w, down_w,
         shift, patch, centre, normed, *wide, time_w, sems) = refs
        turn = flags[0]
        copies = [pltpu.make_async_copy(time_hbm, time_w, sems.at[4])]
        for block in range(2):
            copies.append(pltpu.make_async_copy(up_hbm.at[block], up_w.at[block], sems.at[2 * block]))
            copies.append(pltpu.make_async_copy(down_hbm.at[block], down_w.at[block], sems.at[2 * block + 1]))
        for copy in copies:
            copy.start()
        make_weff(turn, in_w, taps, weff)
        make_by_row(turn, taps, by_row)
        make_tap_rows(turn, taps, tap_rows)
        make_spread(spread, three)
        make_in_three(in_w, in_three)
        out_hi, out_lo = split(jnp.concatenate([out_t[...]] * 8, axis=0))
        out_three[...] = jnp.concatenate([out_hi, out_hi, out_lo], axis=-1)
        copies[0].wait()
        temb[...] = embed(turn, clock, other_clock, time_w)
        states = [[own[...], inner[...]]]
        copies[1].wait()
        copies[2].wait()
    ones = by_row[0]
    for dy in range(1, TAPS):
        ones = ones + by_row[dy]
    for ref in wide:
        clear_sides(ref)

    def place(k, j):
        i = j if k == 0 else 2 * OWN - 1 - j
        return i if i < count + REACH else None

    after = first_block(
        states, place, count, [ones], first_time, temb, gain, up_w, up_b, down_w, weff, in_three,
        shift, patch, centre, spread, three, normed,
    )
    for t in range(TIMES):
        kept[t] = after[t][0 : OWN - HALO]
        for half in range(2):
            wide[2 * t + half][:, PAD : PAD + COLS, :] = after[t][:, :, half * LANES : (half + 1) * LANES]
    for t in range(TIMES):

        def source(i, half, dx):
            at = PAD - HALO + dx
            return wide[2 * t + half][i - HALO, at : at + COLS, :]

        def done(h, half, x):
            partial[2 * t + half, h] = x

        depthwise(tap_rows, source, pairs_of(NEAR), lambda h, half: jnp.zeros((COLS, LANES), F32), done)
    if not last:
        copies[3].wait()
        copies[4].wait()


def edge_kernel(last, *refs):
    if last:
        flags, outer, own, outer_terms, mine, *refs = refs
    else:
        flags, outer, own, *refs = refs
    (clock, other_clock, partial, kept, temb, weff, by_row, tap_rows, spread, three, in_three, out_three, up_w, down_w, gain, up_b,
     first_out, second_out, shift, patch, centre, normed, second_normed, *wide) = refs
    conv_buf = wide[2 * TIMES :]
    turn, inside = flags[0], flags[1].astype(F32)
    first_time = 1 if last else 0
    count = len(EDGE)
    ones = []
    for r in EDGE:
        seen = jnp.zeros((COLS, WIDTH), F32)
        hidden = jnp.zeros((COLS, WIDTH), F32)
        for dy in range(TAPS):
            if r + dy - HALO >= 0:
                seen = seen + by_row[dy]
            else:
                hidden = hidden + by_row[dy]
        ones.append(seen + hidden * inside)
    for ref in wide[: 2 * TIMES]:
        clear_sides(ref)
    low, high = both_clocks(turn, clock, other_clock)
    sizes = [low[:, 2:3], low[:, 3:4], high[:, 2:3], high[:, 3:4]]
    group = lane_group((1, LANES))

    def place(k, j):
        if j >= REACH:
            return None
        return REACH - 1 - j if k == 0 else REACH + j

    states, state = [], [outer[...], own[...]]
    for t in range(TIMES if last else 0):
        state = [state[0] + outer_terms[t].astype(F32), state[1] + mine[t]]
        states.append(state)
    after = first_block(
        states if last else [state], place, count, ones, first_time, temb, gain, up_w, up_b, down_w, weff, in_three,
        shift, patch, centre, spread, three, normed,
    )
    for t in range(TIMES):
        for half in range(2):
            lanes = slice(half * LANES, (half + 1) * LANES)
            wide[2 * t + half][0:HALO, PAD : PAD + COLS, :] = after[t][0:HALO, :, lanes] * inside
            wide[2 * t + half][HALO:, PAD : PAD + COLS, :] = after[t][HALO:, :, lanes]
    touched = len(pairs_of(EDGE))
    stream = []
    for t in range(TIMES):

        def source(i, half, dx):
            at = PAD - HALO + dx
            return wide[2 * t + half][i + HALO, at : at + COLS, :]

        def done(h, half, x):
            conv_buf[t][h, :, half * LANES : (half + 1) * LANES] = x

        depthwise(tap_rows, source, pairs_of(EDGE), lambda h, half: partial[2 * t + half, h], done)
        for h in range(OWN):
            low = (t * OWN + h) * COLS
            if h < touched:
                conv = conv_buf[t][h]
            else:
                conv = jnp.concatenate([partial[2 * t + half, h] for half in range(2)], axis=-1)
            second_normed[low : low + COLS, :] = normalise(conv, gain[1:2, :])
        stream += [after[t][HALO:].reshape(HALO * COLS, WIDTH), kept[t].reshape((OWN - HALO) * COLS, WIDTH)]
    out = pointwise(second_normed[...], 1, up_w, up_b, down_w)
    hi, lo = split(jnp.concatenate(stream, axis=0) + out)
    drifts = dot_nt(jnp.concatenate([hi, lo, hi], axis=-1), out_three[...]).reshape(TIMES, OWN, COLS, LANES)
    terms = []
    for t in range(TIMES):
        dense = drifts[t, 0]
        for j in range(1, OWN):
            dense = jnp.where(group == j, drifts[t, j], dense)
        terms.append(dense * sizes[first_time + t])
    if last:
        n0 = states[0][1]
        n1 = n0 + terms[0]
        n2 = n1 + terms[1]
        n3 = n2 + terms[2]
        turned = turn == 1
        for i, (early, late) in enumerate(((n0, n2), (n1, n3))):
            first_out[i] = jnp.where(turned, late, early)
            second_out[i] = jnp.where(turned, early, late)
    else:
        for t in range(TIMES):
            first_out[t] = terms[t]
            second_out[t] = terms[t].astype(BF16)


SMEM = pl.BlockSpec(memory_space=pltpu.SMEM)
VMEM = pl.BlockSpec(memory_space=pltpu.VMEM)
HBM = pl.BlockSpec(memory_space=pltpu.HBM)
SMALL = pltpu.CompilerParams(vmem_limit_bytes=4 * 2**20)
LARGE = pltpu.CompilerParams(vmem_limit_bytes=20 * 2**20)


def working(count, many):
    return [
        pltpu.VMEM((many, count + REACH, WIDE, LANES), F32),
        pltpu.VMEM((many, count + REACH, COLS, LANES), BF16),
        pltpu.VMEM((many, count, COLS, LANES), BF16),
        pltpu.VMEM((TIMES * count * COLS, WIDTH), BF16),
    ]


def near(last, up_w, down_w, *args):
    outs = [pltpu.VMEM((2 * TIMES, OWN, COLS, LANES), F32), pltpu.VMEM((TIMES, OWN - HALO, COLS, WIDTH), F32)]
    scratch = working(len(NEAR), TIMES if last else 1) + [pltpu.VMEM((len(NEAR), WIDE, LANES), F32)] * (2 * TIMES)
    if last:
        specs = [SMEM] + [VMEM] * (len(args) - 1)
    else:
        outs += [pltpu.VMEM((8, WIDTH), F32), pltpu.VMEM((TAPS * LANES, WIDTH), BF16), pltpu.VMEM((TAPS, COLS, WIDTH), F32)]
        outs += [pltpu.VMEM((2, 56, LANES), F32), pltpu.VMEM((LANES, OWN * LANES), BF16)]
        outs += [pltpu.VMEM((2 * LANES, OWN * LANES), BF16), pltpu.VMEM((LANES, WIDTH), BF16), pltpu.VMEM((LANES, 3 * WIDTH), BF16)]
        outs += [pltpu.VMEM(up_w.shape, BF16), pltpu.VMEM(down_w.shape, BF16)]
        scratch += [pltpu.VMEM((WIDTH, WIDTH), F32), pltpu.SemaphoreType.DMA((5,))]
        specs = [SMEM] + [VMEM] * 4 + [HBM] * 3 + [VMEM] * 5
    return pl.pallas_call(
        functools.partial(near_kernel, last),
        out_shape=outs,
        in_specs=specs,
        out_specs=[VMEM] * len(outs),
        scratch_shapes=scratch,
        compiler_params=LARGE,
    )(*args)


def edge(last, *args):
    if last:
        outs = [jax.ShapeDtypeStruct((2, COLS, LANES), F32)] * 2
    else:
        outs = [jax.ShapeDtypeStruct((TIMES, COLS, LANES), kind) for kind in (F32, BF16)]
    touched = len(pairs_of(EDGE))
    return pl.pallas_call(
        functools.partial(edge_kernel, last),
        out_shape=outs,
        in_specs=[SMEM] + [VMEM] * (len(args) - 1),
        out_specs=[VMEM, VMEM],
        scratch_shapes=working(len(EDGE), TIMES if last else 1)
        + [pltpu.VMEM((TIMES * OWN * COLS, WIDTH), BF16)]
        + [pltpu.VMEM((len(EDGE), WIDE, LANES), F32)] * (2 * TIMES)
        + [pltpu.VMEM((touched, COLS, WIDTH), F32)] * TIMES,
        compiler_params=LARGE,
    )(*args)


def prepare(flags, times, sizes, turned_start):
    dense = jax.ShapeDtypeStruct((COLS, LANES), F32)
    return pl.pallas_call(
        prepare_kernel,
        out_shape=[dense, dense, jax.ShapeDtypeStruct((8, LANES), F32)],
        in_specs=[SMEM, SMEM, SMEM, VMEM],
        out_specs=[VMEM] * 3,
        compiler_params=SMALL,
    )(flags, times, sizes, turned_start)


def finish(flags, keep, got):
    return pl.pallas_call(
        finish_kernel,
        out_shape=jax.ShapeDtypeStruct((2, 2 * OWN, CHAN, COLS), F32),
        in_specs=[SMEM, VMEM, VMEM],
        out_specs=VMEM,
        compiler_params=SMALL,
    )(flags, keep, got)


def on_device(
    start_state, timesteps, step_sizes, in_weight, time_weight, conv_kernel, norm_gain, up_weight, up_bias, down_weight, out_weight,
):
    space = lax.axis_size("space")
    s, tm = lax.axis_index("space"), lax.axis_index("tm")
    beside = [(0, 1), (1, 0)]
    across = []
    for i in range(space - 1):
        across += [(2 * i + 1, 2 * i + 2), (2 * i + 2, 2 * i + 1)]

    def over_tm(x):
        return lax.ppermute(x, "tm", beside)

    def over_space(x):
        return lax.ppermute(x, ("space", "tm"), across)

    flags = jnp.stack([tm, jnp.where(tm == 0, s > 0, s < space - 1).astype(jnp.int32)]).astype(jnp.int32)
    own, inner, clock = prepare(flags, pinned(timesteps), pinned(step_sizes), pinned(start_state.transpose(0, 2, 1)))
    other_clock = over_tm(clock)
    outer = over_space(jnp.where(s < space, own, 0.0))
    taps = conv_kernel.transpose(1, 2, 0, 3)

    partial, kept, *made = near(
        False, up_weight, down_weight, flags, own, inner, clock, other_clock,
        pinned(time_weight), pinned(up_weight), pinned(down_weight), in_weight, taps, norm_gain, up_bias, out_weight.T,
    )
    rest = (norm_gain, up_bias)
    terms, sent = edge(False, flags, outer, own, clock, other_clock, partial, kept, *made, *rest)
    inner_terms, outer_terms = over_tm(sent), over_space(sent)
    partial, kept = near(True, up_weight, down_weight, flags, own, inner, terms, inner_terms, *made, *rest)
    keep, give = edge(True, flags, outer, own, outer_terms, terms, clock, other_clock, partial, kept, *made, *rest)
    return finish(flags, keep, over_tm(give)).transpose(0, 1, 3, 2)


def solution(mesh):
    both = P(("groups", "tm"))
    return jax.shard_map(
        on_device,
        mesh=mesh,
        in_specs=(P(("groups", "space"), None, None), both, both) + (P(),) * 8,
        out_specs=P("tm", ("groups", "space"), None, None),
        check_vma=False,
    )
```

```python
import functools
import math

import jax
import jax.numpy as jnp
from jax import lax
from jax.experimental import pallas as pl
from jax.experimental.pallas import tpu as pltpu
from jax.sharding import PartitionSpec as P

HIGH = lax.Precision.HIGHEST
F32, BF16 = jnp.float32, jnp.bfloat16
COLS, CHAN, WIDTH, HIDDEN, LANES = 32, 16, 256, 1024, 128
OWN, TAPS, HALO = 8, 7, 3
REACH = 2 * HALO
PAD = 8
WIDE = COLS + 2 * PAD
TIMES = 3
CHUNK = 256


def split(x):
    hi = x.astype(BF16)
    return hi, (x - hi.astype(F32)).astype(BF16)


def dot(a, b):
    return lax.dot_general(a, b, (((1,), (0,)), ((), ())), preferred_element_type=F32)


def dot_nt(a, b):
    return lax.dot_general(a, b, (((1,), (1,)), ((), ())), preferred_element_type=F32)


def lane_group(shape):
    return lax.broadcasted_iota(jnp.int32, shape, len(shape) - 1) // CHAN


def make_spread(spread, three):
    row = lax.broadcasted_iota(jnp.int32, (CHAN, LANES), 0)
    col = lax.broadcasted_iota(jnp.int32, (CHAN, LANES), 1)
    hit, group = row == col % CHAN, col // CHAN
    spread[...] = jnp.zeros_like(spread)
    three[...] = jnp.zeros_like(three)

    def cells(where):
        return jnp.where(where, 1.0, 0.0).astype(BF16)

    for j in range(OWN):
        rows, lanes = slice(j * CHAN, (j + 1) * CHAN), slice(j * LANES, (j + 1) * LANES)
        spread[rows, lanes] = cells(hit)
        three[rows, lanes] = cells(hit & ((group == 0) | (group == 2)))
        three[LANES + j * CHAN : LANES + (j + 1) * CHAN, lanes] = cells(hit & (group == 1))


def normalise(conv, gain):
    mean = jnp.mean(conv, axis=-1, keepdims=True)
    centered = conv - mean
    var = jnp.mean(centered * centered, axis=-1, keepdims=True)
    return (centered * lax.rsqrt(var + 1e-06) * gain).astype(BF16)


def gelu(x):
    x = x.astype(BF16)
    inner = x * (BF16(0.7978845608028654) + BF16(0.035677408136300125) * (x * x))
    half = BF16(0.5) * x
    return half + half * jnp.tanh(inner)


def prepare_kernel(flags, times, sizes, start, own, inner, clock):
    turned = flags[0] == 1
    top = to_dense([start[h] for h in range(OWN)])
    bottom = to_dense([start[2 * OWN - 1 - h] for h in range(OWN)])
    own[...] = jnp.where(turned, bottom, top)
    inner[...] = jnp.where(turned, top, bottom)
    lane = lax.broadcasted_iota(jnp.int32, clock.shape, 1)
    values = (times[0].astype(F32), times[1].astype(F32), sizes[0], sizes[1])
    filled = jnp.zeros(clock.shape, F32)
    for i, value in enumerate(values):
        filled = jnp.where(lane == i, value, filled)
    clock[...] = filled


def finish_kernel(flags, keep, got, out):
    turned = flags[0] == 1
    for t in range(2):
        top = jnp.where(turned, got[t], keep[t])
        bottom = jnp.where(turned, keep[t], got[t])
        out[t, 0:OWN] = top.T.reshape(OWN, CHAN, COLS)
        flipped = bottom.T.reshape(OWN, CHAN, COLS)
        for h in range(OWN):
            out[t, 2 * OWN - 1 - h] = flipped[h]


def pinned(x):
    return pltpu.with_memory_space_constraint(x, pltpu.HBM)


def to_dense(rows):
    return jnp.concatenate(rows, axis=0).T


def row_of(turn, dy):
    return dy + turn * (TAPS - 1 - 2 * dy)


def both_clocks(turn, mine, other):
    first = turn == 0
    return jnp.where(first, mine[0:1, :], other[0:1, :]), jnp.where(first, other[0:1, :], mine[0:1, :])


def embed(turn, mine, other, time_w):
    low, high = both_clocks(turn, mine, other)
    steps = jnp.concatenate([low[:, 0:1], low[:, 1:2], high[:, 0:1], high[:, 1:2]] * 2, axis=0)
    lane = lax.broadcasted_iota(jnp.int32, (1, LANES), 1).astype(F32)
    angle = steps * jnp.exp(lane * (-math.log(10000.0) / LANES))
    feats = jnp.concatenate([jnp.sin(angle), jnp.cos(angle)], axis=1)
    return lax.dot_general(feats, time_w[...], (((1,), (0,)), ((), ())), precision=HIGH, preferred_element_type=F32)


def make_weff(turn, in_w, taps, weff):
    weff[...] = jnp.zeros_like(weff)
    for dy in range(TAPS):
        for dx in range(TAPS):
            low = dy * LANES + dx * CHAN
            weff[low : low + CHAN, :] = (in_w[...] * taps[row_of(turn, dy), dx, 0:1, :]).astype(BF16)


def make_by_row(turn, taps, by_row):
    column = lax.broadcasted_iota(jnp.int32, (COLS, WIDTH), 0)
    for dy in range(TAPS):
        total = jnp.zeros((COLS, WIDTH), F32)
        for dx in range(TAPS):
            ok = (column + (dx - HALO) >= 0) & (column + (dx - HALO) < COLS)
            total = total + jnp.where(ok, taps[row_of(turn, dy), dx, 0:1, :], 0.0)
        by_row[dy] = total


def make_in_three(in_w, in_three):
    hi, lo = split(in_w[...])
    in_three[...] = jnp.concatenate([hi, hi, lo, jnp.zeros((LANES - 3 * CHAN, WIDTH), BF16)], axis=0)


def make_tap_rows(turn, taps, tap_rows):
    for dy in range(TAPS):
        for dx in range(TAPS):
            for half in range(2):
                lanes = slice(half * LANES, (half + 1) * LANES)
                tap_rows[half, dy * TAPS + dx : dy * TAPS + dx + 1, :] = taps[row_of(turn, dy), dx, 1:2, lanes]


def clear_sides(ref):
    side = jnp.zeros(ref.shape[:-2] + (PAD, LANES), F32)
    ref[..., 0:PAD, :] = side
    ref[..., PAD + COLS :, :] = side


def block_zero(states, place, count, weff, in_three, shift, patch, centre, spread, three):
    rows, many, blocks = count + REACH, len(states), len(states[0])
    hi, lo = split(jnp.concatenate([block for state in states for block in state], axis=0))

    def spots(flat):
        for n in range(many):
            for k in range(blocks):
                low = (n * blocks + k) * COLS
                for j in range(OWN):
                    i = place(k, j)
                    if i is not None:
                        yield n, i, flat[low : low + COLS, j * LANES : (j + 1) * LANES]

    clear_sides(shift)
    for n, i, x in spots(dot(hi, spread[...])):
        shift[n, i, PAD : PAD + COLS, :] = x
    for n, i, x in spots(dot(jnp.concatenate([hi, lo], axis=-1), three[...])):
        if HALO <= i < HALO + count:
            centre[n, i - HALO] = x.astype(BF16)
    group = lane_group((COLS, LANES))
    at = PAD - HALO
    for n in range(many):
        for i in range(rows):
            picked = shift[n, i, at : at + COLS, :]
            for dx in range(1, TAPS):
                picked = jnp.where(group == dx, shift[n, i, at + dx : at + dx + COLS, :], picked)
            patch[n, i] = picked.astype(BF16)
    cells = many * count * COLS
    wide = [patch[0:many, dy : dy + count].reshape(cells, LANES) for dy in range(TAPS)]
    base = dot(jnp.concatenate(wide, axis=-1), weff[...])
    stream = dot(centre[0:many].reshape(cells, LANES), in_three[...])
    shape = (many, count, COLS, WIDTH)
    return base.reshape(shape), stream.reshape(shape)


def first_block(states, place, count, ones, first_time, temb, gain, up_w, up_b, down_w, weff, in_three, *scratch):
    *scratch, normed = scratch
    base, stream = block_zero(states, place, count, weff, in_three, *scratch)
    residual = []
    for t in range(TIMES):
        n = min(t, len(states) - 1)
        shown = temb[first_time + t : first_time + t + 1, :]
        lift = [ones[i] * shown for i in range(len(ones))]
        for i in range(count):
            low = (t * count + i) * COLS
            normed[low : low + COLS, :] = normalise(base[n, i] + lift[min(i, len(ones) - 1)], gain[0:1, :])
        residual.append(stream[n] + shown)
    out = pointwise(normed[...], 0, up_w, up_b, down_w).reshape(TIMES, count, COLS, WIDTH)
    return [residual[t] + out[t] for t in range(TIMES)]


def pointwise(normed, block, up_w, up_b, down_w):
    hidden = []
    for low in range(0, HIDDEN, CHUNK):
        hidden.append(gelu(dot(normed, up_w[block, :, low : low + CHUNK]) + up_b[block : block + 1, low : low + CHUNK]))
    return dot(jnp.concatenate(hidden, axis=-1), down_w[block])


def depthwise(tap_rows, source, pairs, begin, done):
    heights = sorted(pairs)
    groups = [heights[i : i + 4] for i in range(0, len(heights), 4)]
    for half in range(2):
        for group in groups:
            acc = {h: begin(h, half) for h in group}
            needed = sorted({i for h in group for i in pairs[h]})
            for dx in range(TAPS):
                for i in needed:
                    x = source(i, half, dx)
                    for h in group:
                        if i in pairs[h]:
                            at = (i - h + HALO) * TAPS + dx
                            acc[h] = acc[h] + x * tap_rows[half, at : at + 1, :]
            for h in group:
                done(h, half, acc[h])


NEAR = range(HALO, OWN + HALO)
EDGE = range(-HALO, HALO)


def pairs_of(rows):
    found = {h: [i for i in rows if abs(i - h) <= HALO] for h in range(OWN)}
    return {h: listed for h, listed in found.items() if listed}


def near_kernel(last, *refs):
    first_time = 1 if last else 0
    count = len(NEAR)
    if last:
        (flags, own, inner, mine, inner_terms, temb, weff, by_row, tap_rows, spread, three, in_three, _, gain, up_w, down_w, up_b,
         partial, kept, shift, patch, centre, normed, *wide) = refs
        turn = flags[0]
        states, state = [], [own[...], inner[...]]
        for t in range(TIMES):
            state = [state[0] + mine[t], state[1] + inner_terms[t].astype(F32)]
            states.append(state)
    else:
        (flags, own, inner, clock, other_clock, time_hbm, up_hbm, down_hbm, gain_hbm, in_w, taps, up_b, out_t,
         partial, kept, temb, weff, by_row, tap_rows, spread, three, in_three, out_three, gain, up_w, down_w,
         shift, patch, centre, normed, *wide, time_w, sems) = refs
        turn = flags[0]
        copies = [pltpu.make_async_copy(time_hbm, time_w, sems.at[4])]
        for block in range(2):
            copies.append(pltpu.make_async_copy(up_hbm.at[block], up_w.at[block], sems.at[2 * block]))
            copies.append(pltpu.make_async_copy(down_hbm.at[block], down_w.at[block], sems.at[2 * block + 1]))
        copies.append(pltpu.make_async_copy(gain_hbm, gain, sems.at[5]))
        for copy in copies:
            copy.start()
        make_weff(turn, in_w, taps, weff)
        make_by_row(turn, taps, by_row)
        make_tap_rows(turn, taps, tap_rows)
        make_spread(spread, three)
        make_in_three(in_w, in_three)
        out_hi, out_lo = split(jnp.concatenate([out_t[...]] * 8, axis=0))
        out_three[...] = jnp.concatenate([out_hi, out_hi, out_lo], axis=-1)
        copies[0].wait()
        temb[...] = embed(turn, clock, other_clock, time_w)
        states = [[own[...], inner[...]]]
        copies[1].wait()
        copies[2].wait()
        copies[5].wait()
    ones = by_row[0]
    for dy in range(1, TAPS):
        ones = ones + by_row[dy]
    for ref in wide:
        clear_sides(ref)

    def place(k, j):
        i = j if k == 0 else 2 * OWN - 1 - j
        return i if i < count + REACH else None

    after = first_block(
        states, place, count, [ones], first_time, temb, gain, up_w, up_b, down_w, weff, in_three,
        shift, patch, centre, spread, three, normed,
    )
    for t in range(TIMES):
        kept[t] = after[t][0 : OWN - HALO]
        for half in range(2):
            wide[2 * t + half][:, PAD : PAD + COLS, :] = after[t][:, :, half * LANES : (half + 1) * LANES]
    for t in range(TIMES):

        def source(i, half, dx):
            at = PAD - HALO + dx
            return wide[2 * t + half][i - HALO, at : at + COLS, :]

        def done(h, half, x):
            partial[2 * t + half, h] = x

        depthwise(tap_rows, source, pairs_of(NEAR), lambda h, half: jnp.zeros((COLS, LANES), F32), done)
    if not last:
        copies[3].wait()
        copies[4].wait()


def edge_kernel(last, *refs):
    if last:
        flags, outer, own, outer_terms, mine, *refs = refs
    else:
        flags, outer, own, *refs = refs
    (clock, other_clock, partial, kept, temb, weff, by_row, tap_rows, spread, three, in_three, out_three, gain, up_w, down_w, up_b,
     first_out, second_out, shift, patch, centre, normed, second_normed, *wide) = refs
    conv_buf = wide[2 * TIMES :]
    turn, inside = flags[0], flags[1].astype(F32)
    first_time = 1 if last else 0
    count = len(EDGE)
    ones = []
    for r in EDGE:
        seen = jnp.zeros((COLS, WIDTH), F32)
        hidden = jnp.zeros((COLS, WIDTH), F32)
        for dy in range(TAPS):
            if r + dy - HALO >= 0:
                seen = seen + by_row[dy]
            else:
                hidden = hidden + by_row[dy]
        ones.append(seen + hidden * inside)
    for ref in wide[: 2 * TIMES]:
        clear_sides(ref)
    low, high = both_clocks(turn, clock, other_clock)
    sizes = [low[:, 2:3], low[:, 3:4], high[:, 2:3], high[:, 3:4]]
    group = lane_group((1, LANES))

    def place(k, j):
        if j >= REACH:
            return None
        return REACH - 1 - j if k == 0 else REACH + j

    states, state = [], [outer[...], own[...]]
    for t in range(TIMES if last else 0):
        state = [state[0] + outer_terms[t].astype(F32), state[1] + mine[t]]
        states.append(state)
    after = first_block(
        states if last else [state], place, count, ones, first_time, temb, gain, up_w, up_b, down_w, weff, in_three,
        shift, patch, centre, spread, three, normed,
    )
    for t in range(TIMES):
        for half in range(2):
            lanes = slice(half * LANES, (half + 1) * LANES)
            wide[2 * t + half][0:HALO, PAD : PAD + COLS, :] = after[t][0:HALO, :, lanes] * inside
            wide[2 * t + half][HALO:, PAD : PAD + COLS, :] = after[t][HALO:, :, lanes]
    touched = len(pairs_of(EDGE))
    stream = []
    for t in range(TIMES):

        def source(i, half, dx):
            at = PAD - HALO + dx
            return wide[2 * t + half][i + HALO, at : at + COLS, :]

        def done(h, half, x):
            conv_buf[t][h, :, half * LANES : (half + 1) * LANES] = x

        depthwise(tap_rows, source, pairs_of(EDGE), lambda h, half: partial[2 * t + half, h], done)
        for h in range(OWN):
            low = (t * OWN + h) * COLS
            if h < touched:
                conv = conv_buf[t][h]
            else:
                conv = jnp.concatenate([partial[2 * t + half, h] for half in range(2)], axis=-1)
            second_normed[low : low + COLS, :] = normalise(conv, gain[1:2, :])
        stream += [after[t][HALO:].reshape(HALO * COLS, WIDTH), kept[t].reshape((OWN - HALO) * COLS, WIDTH)]
    out = pointwise(second_normed[...], 1, up_w, up_b, down_w)
    hi, lo = split(jnp.concatenate(stream, axis=0) + out)
    drifts = dot_nt(jnp.concatenate([hi, lo, hi], axis=-1), out_three[...]).reshape(TIMES, OWN, COLS, LANES)
    terms = []
    for t in range(TIMES):
        dense = drifts[t, 0]
        for j in range(1, OWN):
            dense = jnp.where(group == j, drifts[t, j], dense)
        terms.append(dense * sizes[first_time + t])
    if last:
        n0 = states[0][1]
        n1 = n0 + terms[0]
        n2 = n1 + terms[1]
        n3 = n2 + terms[2]
        turned = turn == 1
        for i, (early, late) in enumerate(((n0, n2), (n1, n3))):
            first_out[i] = jnp.where(turned, late, early)
            second_out[i] = jnp.where(turned, early, late)
    else:
        for t in range(TIMES):
            first_out[t] = terms[t]
            second_out[t] = terms[t].astype(BF16)


SMEM = pl.BlockSpec(memory_space=pltpu.SMEM)
VMEM = pl.BlockSpec(memory_space=pltpu.VMEM)
HBM = pl.BlockSpec(memory_space=pltpu.HBM)
SMALL = pltpu.CompilerParams(vmem_limit_bytes=4 * 2**20)
LARGE = pltpu.CompilerParams(vmem_limit_bytes=20 * 2**20)


def working(count, many):
    return [
        pltpu.VMEM((many, count + REACH, WIDE, LANES), F32),
        pltpu.VMEM((many, count + REACH, COLS, LANES), BF16),
        pltpu.VMEM((many, count, COLS, LANES), BF16),
        pltpu.VMEM((TIMES * count * COLS, WIDTH), BF16),
    ]


def near(last, up_w, down_w, *args):
    outs = [pltpu.VMEM((2 * TIMES, OWN, COLS, LANES), F32), pltpu.VMEM((TIMES, OWN - HALO, COLS, WIDTH), F32)]
    scratch = working(len(NEAR), TIMES if last else 1) + [pltpu.VMEM((len(NEAR), WIDE, LANES), F32)] * (2 * TIMES)
    if last:
        specs = [SMEM] + [VMEM] * (len(args) - 1)
    else:
        outs += [pltpu.VMEM((8, WIDTH), F32), pltpu.VMEM((TAPS * LANES, WIDTH), BF16), pltpu.VMEM((TAPS, COLS, WIDTH), F32)]
        outs += [pltpu.VMEM((2, 56, LANES), F32), pltpu.VMEM((LANES, OWN * LANES), BF16)]
        outs += [pltpu.VMEM((2 * LANES, OWN * LANES), BF16), pltpu.VMEM((LANES, WIDTH), BF16), pltpu.VMEM((LANES, 3 * WIDTH), BF16)]
        outs += [pltpu.VMEM((2, WIDTH), F32)]
        outs += [pltpu.VMEM(up_w.shape, BF16), pltpu.VMEM(down_w.shape, BF16)]
        scratch += [pltpu.VMEM((WIDTH, WIDTH), F32), pltpu.SemaphoreType.DMA((6,))]
        specs = [SMEM] + [VMEM] * 4 + [HBM] * 4 + [VMEM] * 4
    return pl.pallas_call(
        functools.partial(near_kernel, last),
        out_shape=outs,
        in_specs=specs,
        out_specs=[VMEM] * len(outs),
        scratch_shapes=scratch,
        compiler_params=LARGE,
    )(*args)


def edge(last, *args):
    if last:
        outs = [jax.ShapeDtypeStruct((2, COLS, LANES), F32)] * 2
    else:
        outs = [jax.ShapeDtypeStruct((TIMES, COLS, LANES), kind) for kind in (F32, BF16)]
    touched = len(pairs_of(EDGE))
    return pl.pallas_call(
        functools.partial(edge_kernel, last),
        out_shape=outs,
        in_specs=[SMEM] + [VMEM] * (len(args) - 1),
        out_specs=[VMEM, VMEM],
        scratch_shapes=working(len(EDGE), TIMES if last else 1)
        + [pltpu.VMEM((TIMES * OWN * COLS, WIDTH), BF16)]
        + [pltpu.VMEM((len(EDGE), WIDE, LANES), F32)] * (2 * TIMES)
        + [pltpu.VMEM((touched, COLS, WIDTH), F32)] * TIMES,
        compiler_params=LARGE,
    )(*args)


def prepare(flags, times, sizes, turned_start):
    dense = jax.ShapeDtypeStruct((COLS, LANES), F32)
    return pl.pallas_call(
        prepare_kernel,
        out_shape=[dense, dense, jax.ShapeDtypeStruct((32, LANES), F32)],
        in_specs=[SMEM, SMEM, SMEM, VMEM],
        out_specs=[VMEM] * 3,
        compiler_params=SMALL,
    )(flags, times, sizes, turned_start)


def finish(flags, keep, got):
    return pl.pallas_call(
        finish_kernel,
        out_shape=jax.ShapeDtypeStruct((2, 2 * OWN, CHAN, COLS), F32),
        in_specs=[SMEM, VMEM, VMEM],
        out_specs=VMEM,
        compiler_params=SMALL,
    )(flags, keep, got)


def on_device(
    start_state, timesteps, step_sizes, in_weight, time_weight, conv_kernel, norm_gain, up_weight, up_bias, down_weight, out_weight,
):
    space = lax.axis_size("space")
    s, tm = lax.axis_index("space"), lax.axis_index("tm")
    beside = [(0, 1), (1, 0)]
    across = []
    for i in range(space - 1):
        across += [(2 * i + 1, 2 * i + 2), (2 * i + 2, 2 * i + 1)]

    def over_tm(x):
        return lax.ppermute(x, "tm", beside)

    def over_space(x):
        return lax.ppermute(x, ("space", "tm"), across)

    flags = jnp.stack([tm, jnp.where(tm == 0, s > 0, s < space - 1).astype(jnp.int32)]).astype(jnp.int32)
    own, inner, clock = prepare(flags, pinned(timesteps), pinned(step_sizes), pinned(start_state.transpose(0, 2, 1)))
    other_clock = over_tm(clock)
    outer = over_space(own)
    taps = conv_kernel.transpose(1, 2, 0, 3)

    partial, kept, *made = near(
        False, up_weight, down_weight, flags, own, inner, clock, other_clock,
        pinned(time_weight), pinned(up_weight), pinned(down_weight), pinned(norm_gain), in_weight, taps, up_bias, out_weight.T,
    )
    rest = (up_bias,)
    terms, sent = edge(False, flags, outer, own, clock, other_clock, partial, kept, *made, *rest)
    inner_terms, outer_terms = over_tm(sent), over_space(sent)
    partial, kept = near(True, up_weight, down_weight, flags, own, inner, terms, inner_terms, *made, *rest)
    keep, give = edge(True, flags, outer, own, outer_terms, terms, clock, other_clock, partial, kept, *made, *rest)
    return finish(flags, keep, over_tm(give)).transpose(0, 1, 3, 2)


def solution(mesh):
    both = P(("groups", "tm"))
    return jax.shard_map(
        on_device,
        mesh=mesh,
        in_specs=(P(("groups", "space"), None, None), both, both) + (P(),) * 8,
        out_specs=P("tm", ("groups", "space"), None, None),
        check_vma=False,
    )
```

```python
import functools
import math

import jax
import jax.numpy as jnp
from jax import lax
from jax.experimental import pallas as pl
from jax.experimental.pallas import tpu as pltpu
from jax.sharding import PartitionSpec as P

HIGH = lax.Precision.HIGHEST
F32, BF16 = jnp.float32, jnp.bfloat16
COLS, CHAN, WIDTH, HIDDEN, LANES = 32, 16, 256, 1024, 128
OWN, TAPS, HALO = 8, 7, 3
REACH = 2 * HALO
PAD = 8
WIDE = COLS + 2 * PAD
TIMES = 3
CHUNK = 256


def split(x):
    hi = x.astype(BF16)
    return hi, (x - hi.astype(F32)).astype(BF16)


def dot(a, b):
    return lax.dot_general(a, b, (((1,), (0,)), ((), ())), preferred_element_type=F32)


def dot_nt(a, b):
    return lax.dot_general(a, b, (((1,), (1,)), ((), ())), preferred_element_type=F32)


def lane_group(shape):
    return lax.broadcasted_iota(jnp.int32, shape, len(shape) - 1) // CHAN


def make_spread(spread, three):
    row = lax.broadcasted_iota(jnp.int32, (CHAN, LANES), 0)
    col = lax.broadcasted_iota(jnp.int32, (CHAN, LANES), 1)
    hit, group = row == col % CHAN, col // CHAN
    spread[...] = jnp.zeros_like(spread)
    three[...] = jnp.zeros_like(three)

    def cells(where):
        return jnp.where(where, 1.0, 0.0).astype(BF16)

    for j in range(OWN):
        rows, lanes = slice(j * CHAN, (j + 1) * CHAN), slice(j * LANES, (j + 1) * LANES)
        spread[rows, lanes] = cells(hit)
        three[rows, lanes] = cells(hit & ((group == 0) | (group == 2)))
        three[LANES + j * CHAN : LANES + (j + 1) * CHAN, lanes] = cells(hit & (group == 1))


def normalise(conv, gain):
    mean = jnp.mean(conv, axis=-1, keepdims=True)
    centered = conv - mean
    var = jnp.mean(centered * centered, axis=-1, keepdims=True)
    return (centered * lax.rsqrt(var + 1e-06) * gain).astype(BF16)


def gelu(x):
    x = x.astype(BF16)
    inner = x * (BF16(0.7978845608028654) + BF16(0.035677408136300125) * (x * x))
    half = BF16(0.5) * x
    return half + half * jnp.tanh(inner)


def prepare_kernel(flags, times, sizes, start, own, inner, clock):
    turned = flags[0] == 1
    top = to_dense([start[h] for h in range(OWN)])
    bottom = to_dense([start[2 * OWN - 1 - h] for h in range(OWN)])
    own[...] = jnp.where(turned, bottom, top)
    inner[...] = jnp.where(turned, top, bottom)
    lane = lax.broadcasted_iota(jnp.int32, clock.shape, 1)
    values = (times[0].astype(F32), times[1].astype(F32), sizes[0], sizes[1])
    filled = jnp.zeros(clock.shape, F32)
    for i, value in enumerate(values):
        filled = jnp.where(lane == i, value, filled)
    clock[...] = filled


def finish_kernel(flags, keep, got, out):
    turned = flags[0] == 1
    for t in range(2):
        top = jnp.where(turned, got[t], keep[t])
        bottom = jnp.where(turned, keep[t], got[t])
        out[t, 0:OWN] = top.T.reshape(OWN, CHAN, COLS)
        flipped = bottom.T.reshape(OWN, CHAN, COLS)
        for h in range(OWN):
            out[t, 2 * OWN - 1 - h] = flipped[h]


def pinned(x):
    return pltpu.with_memory_space_constraint(x, pltpu.HBM)


def to_dense(rows):
    return jnp.concatenate(rows, axis=0).T


def row_of(turn, dy):
    return dy + turn * (TAPS - 1 - 2 * dy)


def both_clocks(turn, mine, other):
    first = turn == 0
    return jnp.where(first, mine[0:1, :], other[0:1, :]), jnp.where(first, other[0:1, :], mine[0:1, :])


def embed(turn, mine, other, time_w):
    low, high = both_clocks(turn, mine, other)
    steps = jnp.concatenate([low[:, 0:1], low[:, 1:2], high[:, 0:1], high[:, 1:2]] * 2, axis=0)
    lane = lax.broadcasted_iota(jnp.int32, (1, LANES), 1).astype(F32)
    angle = steps * jnp.exp(lane * (-math.log(10000.0) / LANES))
    feats = jnp.concatenate([jnp.sin(angle), jnp.cos(angle)], axis=1)
    return lax.dot_general(feats, time_w[...], (((1,), (0,)), ((), ())), precision=HIGH, preferred_element_type=F32)


def make_weff(turn, in_w, taps, weff):
    weff[...] = jnp.zeros_like(weff)
    for dy in range(TAPS):
        for dx in range(TAPS):
            low = dy * LANES + dx * CHAN
            weff[low : low + CHAN, :] = (in_w[...] * taps[row_of(turn, dy), dx, 0:1, :]).astype(BF16)


def make_by_row(turn, taps, by_row):
    column = lax.broadcasted_iota(jnp.int32, (COLS, WIDTH), 0)
    for dy in range(TAPS):
        total = jnp.zeros((COLS, WIDTH), F32)
        for dx in range(TAPS):
            ok = (column + (dx - HALO) >= 0) & (column + (dx - HALO) < COLS)
            total = total + jnp.where(ok, taps[row_of(turn, dy), dx, 0:1, :], 0.0)
        by_row[dy] = total


def make_in_three(in_w, in_three):
    hi, lo = split(in_w[...])
    in_three[...] = jnp.concatenate([hi, hi, lo, jnp.zeros((LANES - 3 * CHAN, WIDTH), BF16)], axis=0)


def make_tap_rows(turn, taps, tap_rows):
    for dy in range(TAPS):
        for dx in range(TAPS):
            for half in range(2):
                lanes = slice(half * LANES, (half + 1) * LANES)
                tap_rows[half, dy * TAPS + dx : dy * TAPS + dx + 1, :] = taps[row_of(turn, dy), dx, 1:2, lanes]


def clear_sides(ref):
    side = jnp.zeros(ref.shape[:-2] + (PAD, LANES), F32)
    ref[..., 0:PAD, :] = side
    ref[..., PAD + COLS :, :] = side


def block_zero(states, place, count, weff, in_three, shift, patch, centre, spread, three):
    rows, many, blocks = count + REACH, len(states), len(states[0])
    hi, lo = split(jnp.concatenate([block for state in states for block in state], axis=0))

    def spots(flat):
        for n in range(many):
            for k in range(blocks):
                low = (n * blocks + k) * COLS
                for j in range(OWN):
                    i = place(k, j)
                    if i is not None:
                        yield n, i, flat[low : low + COLS, j * LANES : (j + 1) * LANES]

    clear_sides(shift)
    for n, i, x in spots(dot(hi, spread[...])):
        shift[n, i, PAD : PAD + COLS, :] = x
    for n, i, x in spots(dot(jnp.concatenate([hi, lo], axis=-1), three[...])):
        if HALO <= i < HALO + count:
            centre[n, i - HALO] = x.astype(BF16)
    group = lane_group((COLS, LANES))
    at = PAD - HALO
    for n in range(many):
        for i in range(rows):
            picked = shift[n, i, at : at + COLS, :]
            for dx in range(1, TAPS):
                picked = jnp.where(group == dx, shift[n, i, at + dx : at + dx + COLS, :], picked)
            patch[n, i] = picked.astype(BF16)
    cells = many * count * COLS
    wide = [patch[0:many, dy : dy + count].reshape(cells, LANES) for dy in range(TAPS)]
    base = dot(jnp.concatenate(wide, axis=-1), weff[...])
    stream = dot(centre[0:many].reshape(cells, LANES), in_three[...])
    shape = (many, count, COLS, WIDTH)
    return base.reshape(shape), stream.reshape(shape)


def first_block(states, place, count, ones, first_time, temb, gain, up_w, up_b, down_w, weff, in_three, *scratch):
    *scratch, normed = scratch
    base, stream = block_zero(states, place, count, weff, in_three, *scratch)
    residual = []
    for t in range(TIMES):
        n = min(t, len(states) - 1)
        shown = temb[first_time + t : first_time + t + 1, :]
        lift = [ones[i] * shown for i in range(len(ones))]
        for i in range(count):
            low = (t * count + i) * COLS
            normed[low : low + COLS, :] = normalise(base[n, i] + lift[min(i, len(ones) - 1)], gain[0:1, :])
        residual.append(stream[n] + shown)
    out = pointwise(normed[...], 0, up_w, up_b, down_w).reshape(TIMES, count, COLS, WIDTH)
    return [residual[t] + out[t] for t in range(TIMES)]


def pointwise(normed, block, up_w, up_b, down_w):
    hidden = []
    for low in range(0, HIDDEN, CHUNK):
        hidden.append(gelu(dot(normed, up_w[block, :, low : low + CHUNK]) + up_b[block : block + 1, low : low + CHUNK]))
    return dot(jnp.concatenate(hidden, axis=-1), down_w[block])


def depthwise(tap_rows, half, source, pairs, begin, done, group_size=4):
    heights = sorted(pairs)
    groups = [heights[i : i + group_size] for i in range(0, len(heights), group_size)]
    for group in groups:
        acc = {h: begin(h) for h in group}
        needed = sorted({i for h in group for i in pairs[h]})
        for dx in range(TAPS):
            for i in needed:
                x = source(i, dx)
                for h in group:
                    if i in pairs[h]:
                        at = (i - h + HALO) * TAPS + dx
                        acc[h] = acc[h] + x * tap_rows[half, at : at + 1, :]
        for h in group:
            done(h, acc[h])


NEAR = range(HALO, OWN + HALO)
EDGE = range(-HALO, HALO)


def pairs_of(rows):
    found = {h: [i for i in rows if abs(i - h) <= HALO] for h in range(OWN)}
    return {h: listed for h, listed in found.items() if listed}


def near_kernel(last, *refs):
    first_time = 1 if last else 0
    count = len(NEAR)
    if last:
        (flags, own, inner, mine, inner_terms, temb, weff, by_row, tap_rows, spread, three, in_three, _, gain, up_w, down_w, up_b,
         partial, kept, shift, patch, centre, normed, wide) = refs
        turn = flags[0]
        states, state = [], [own[...], inner[...]]
        for t in range(TIMES):
            state = [state[0] + mine[t], state[1] + inner_terms[t].astype(F32)]
            states.append(state)
    else:
        (flags, own, inner, clock, other_clock, time_hbm, up_hbm, down_hbm, gain_hbm, in_w, taps, up_b, out_t,
         partial, kept, temb, weff, by_row, tap_rows, spread, three, in_three, out_three, gain, up_w, down_w,
         shift, patch, centre, normed, wide, time_w, sems) = refs
        turn = flags[0]
        copies = [pltpu.make_async_copy(time_hbm, time_w, sems.at[4])]
        for block in range(2):
            copies.append(pltpu.make_async_copy(up_hbm.at[block], up_w.at[block], sems.at[2 * block]))
            copies.append(pltpu.make_async_copy(down_hbm.at[block], down_w.at[block], sems.at[2 * block + 1]))
        copies.append(pltpu.make_async_copy(gain_hbm, gain, sems.at[5]))
        for copy in copies:
            copy.start()
        make_weff(turn, in_w, taps, weff)
        make_by_row(turn, taps, by_row)
        make_tap_rows(turn, taps, tap_rows)
        make_spread(spread, three)
        make_in_three(in_w, in_three)
        out_hi, out_lo = split(jnp.concatenate([out_t[...]] * 8, axis=0))
        out_three[...] = jnp.concatenate([out_hi, out_hi, out_lo], axis=-1)
        copies[0].wait()
        temb[...] = embed(turn, clock, other_clock, time_w)
        states = [[own[...], inner[...]]]
        copies[1].wait()
        copies[2].wait()
        copies[5].wait()
    ones = by_row[0]
    for dy in range(1, TAPS):
        ones = ones + by_row[dy]
    clear_sides(wide)

    def place(k, j):
        i = j if k == 0 else 2 * OWN - 1 - j
        return i if i < count + REACH else None

    after = first_block(
        states, place, count, [ones], first_time, temb, gain, up_w, up_b, down_w, weff, in_three,
        shift, patch, centre, spread, three, normed,
    )
    for t in range(TIMES):
        kept[t] = after[t][0 : OWN - HALO]
        for half in range(2):
            wide[2 * t + half, :, PAD : PAD + COLS, :] = after[t][:, :, half * LANES : (half + 1) * LANES]

    def tapped(half, t, carry):
        def source(i, dx):
            low = PAD - HALO + dx
            return wide[2 * t + half, i - HALO, low : low + COLS, :]

        def done(h, x):
            partial[2 * t + half, h] = x

        depthwise(tap_rows, half, source, pairs_of(NEAR), lambda h: jnp.zeros((COLS, LANES), F32), done, OWN)
        return carry

    for half in range(2):
        lax.fori_loop(0, TIMES, functools.partial(tapped, half), 0)
    if not last:
        copies[3].wait()
        copies[4].wait()


def edge_kernel(last, *refs):
    if last:
        flags, outer, own, outer_terms, mine, *refs = refs
    else:
        flags, outer, own, *refs = refs
    (clock, other_clock, partial, kept, temb, weff, by_row, tap_rows, spread, three, in_three, out_three, gain, up_w, down_w, up_b,
     first_out, second_out, shift, patch, centre, normed, second_normed, *wide) = refs
    conv_buf = wide[2 * TIMES :]
    turn, inside = flags[0], flags[1].astype(F32)
    first_time = 1 if last else 0
    count = len(EDGE)
    ones = []
    for r in EDGE:
        seen = jnp.zeros((COLS, WIDTH), F32)
        hidden = jnp.zeros((COLS, WIDTH), F32)
        for dy in range(TAPS):
            if r + dy - HALO >= 0:
                seen = seen + by_row[dy]
            else:
                hidden = hidden + by_row[dy]
        ones.append(seen + hidden * inside)
    for ref in wide[: 2 * TIMES]:
        clear_sides(ref)
    low, high = both_clocks(turn, clock, other_clock)
    sizes = [low[:, 2:3], low[:, 3:4], high[:, 2:3], high[:, 3:4]]
    group = lane_group((1, LANES))

    def place(k, j):
        if j >= REACH:
            return None
        return REACH - 1 - j if k == 0 else REACH + j

    states, state = [], [outer[...], own[...]]
    for t in range(TIMES if last else 0):
        state = [state[0] + outer_terms[t].astype(F32), state[1] + mine[t]]
        states.append(state)
    after = first_block(
        states if last else [state], place, count, ones, first_time, temb, gain, up_w, up_b, down_w, weff, in_three,
        shift, patch, centre, spread, three, normed,
    )
    for t in range(TIMES):
        for half in range(2):
            lanes = slice(half * LANES, (half + 1) * LANES)
            wide[2 * t + half][0:HALO, PAD : PAD + COLS, :] = after[t][0:HALO, :, lanes] * inside
            wide[2 * t + half][HALO:, PAD : PAD + COLS, :] = after[t][HALO:, :, lanes]
    touched = len(pairs_of(EDGE))
    stream = []
    for t in range(TIMES):

        def source(half, i, dx):
            low = PAD - HALO + dx
            return wide[2 * t + half][i + HALO, low : low + COLS, :]

        def done(half, h, x):
            conv_buf[t][h, :, half * LANES : (half + 1) * LANES] = x

        for half in range(2):
            depthwise(
                tap_rows, half, functools.partial(source, half), pairs_of(EDGE), lambda h: partial[2 * t + half, h],
                functools.partial(done, half),
            )
        for h in range(OWN):
            low = (t * OWN + h) * COLS
            if h < touched:
                conv = conv_buf[t][h]
            else:
                conv = jnp.concatenate([partial[2 * t + half, h] for half in range(2)], axis=-1)
            second_normed[low : low + COLS, :] = normalise(conv, gain[1:2, :])
        stream += [after[t][HALO:].reshape(HALO * COLS, WIDTH), kept[t].reshape((OWN - HALO) * COLS, WIDTH)]
    out = pointwise(second_normed[...], 1, up_w, up_b, down_w)
    hi, lo = split(jnp.concatenate(stream, axis=0) + out)
    drifts = dot_nt(jnp.concatenate([hi, lo, hi], axis=-1), out_three[...]).reshape(TIMES, OWN, COLS, LANES)
    terms = []
    for t in range(TIMES):
        dense = drifts[t, 0]
        for j in range(1, OWN):
            dense = jnp.where(group == j, drifts[t, j], dense)
        terms.append(dense * sizes[first_time + t])
    if last:
        n0 = states[0][1]
        n1 = n0 + terms[0]
        n2 = n1 + terms[1]
        n3 = n2 + terms[2]
        turned = turn == 1
        for i, (early, late) in enumerate(((n0, n2), (n1, n3))):
            first_out[i] = jnp.where(turned, late, early)
            second_out[i] = jnp.where(turned, early, late)
    else:
        for t in range(TIMES):
            first_out[t] = terms[t]
            second_out[t] = terms[t].astype(BF16)


SMEM = pl.BlockSpec(memory_space=pltpu.SMEM)
VMEM = pl.BlockSpec(memory_space=pltpu.VMEM)
HBM = pl.BlockSpec(memory_space=pltpu.HBM)
SMALL = pltpu.CompilerParams(vmem_limit_bytes=4 * 2**20)
LARGE = pltpu.CompilerParams(vmem_limit_bytes=20 * 2**20)


def working(count, many):
    return [
        pltpu.VMEM((many, count + REACH, WIDE, LANES), F32),
        pltpu.VMEM((many, count + REACH, COLS, LANES), BF16),
        pltpu.VMEM((many, count, COLS, LANES), BF16),
        pltpu.VMEM((TIMES * count * COLS, WIDTH), BF16),
    ]


def near(last, up_w, down_w, *args):
    outs = [pltpu.VMEM((2 * TIMES, OWN, COLS, LANES), F32), pltpu.VMEM((TIMES, OWN - HALO, COLS, WIDTH), F32)]
    scratch = working(len(NEAR), TIMES if last else 1) + [pltpu.VMEM((2 * TIMES, len(NEAR), WIDE, LANES), F32)]
    if last:
        specs = [SMEM] + [VMEM] * (len(args) - 1)
    else:
        outs += [pltpu.VMEM((8, WIDTH), F32), pltpu.VMEM((TAPS * LANES, WIDTH), BF16), pltpu.VMEM((TAPS, COLS, WIDTH), F32)]
        outs += [pltpu.VMEM((2, 56, LANES), F32), pltpu.VMEM((LANES, OWN * LANES), BF16)]
        outs += [pltpu.VMEM((2 * LANES, OWN * LANES), BF16), pltpu.VMEM((LANES, WIDTH), BF16), pltpu.VMEM((LANES, 3 * WIDTH), BF16)]
        outs += [pltpu.VMEM((2, WIDTH), F32)]
        outs += [pltpu.VMEM(up_w.shape, BF16), pltpu.VMEM(down_w.shape, BF16)]
        scratch += [pltpu.VMEM((WIDTH, WIDTH), F32), pltpu.SemaphoreType.DMA((6,))]
        specs = [SMEM] + [VMEM] * 4 + [HBM] * 4 + [VMEM] * 4
    return pl.pallas_call(
        functools.partial(near_kernel, last),
        out_shape=outs,
        in_specs=specs,
        out_specs=[VMEM] * len(outs),
        scratch_shapes=scratch,
        compiler_params=LARGE,
    )(*args)


def edge(last, *args):
    if last:
        outs = [jax.ShapeDtypeStruct((2, COLS, LANES), F32)] * 2
    else:
        outs = [jax.ShapeDtypeStruct((TIMES, COLS, LANES), kind) for kind in (F32, BF16)]
    touched = len(pairs_of(EDGE))
    return pl.pallas_call(
        functools.partial(edge_kernel, last),
        out_shape=outs,
        in_specs=[SMEM] + [VMEM] * (len(args) - 1),
        out_specs=[VMEM, VMEM],
        scratch_shapes=working(len(EDGE), TIMES if last else 1)
        + [pltpu.VMEM((TIMES * OWN * COLS, WIDTH), BF16)]
        + [pltpu.VMEM((len(EDGE), WIDE, LANES), F32)] * (2 * TIMES)
        + [pltpu.VMEM((touched, COLS, WIDTH), F32)] * TIMES,
        compiler_params=LARGE,
    )(*args)


def prepare(flags, times, sizes, turned_start):
    dense = jax.ShapeDtypeStruct((COLS, LANES), F32)
    return pl.pallas_call(
        prepare_kernel,
        out_shape=[dense, dense, jax.ShapeDtypeStruct((32, LANES), F32)],
        in_specs=[SMEM, SMEM, SMEM, VMEM],
        out_specs=[VMEM] * 3,
        compiler_params=SMALL,
    )(flags, times, sizes, turned_start)


def finish(flags, keep, got):
    return pl.pallas_call(
        finish_kernel,
        out_shape=jax.ShapeDtypeStruct((2, 2 * OWN, CHAN, COLS), F32),
        in_specs=[SMEM, VMEM, VMEM],
        out_specs=VMEM,
        compiler_params=SMALL,
    )(flags, keep, got)


def on_device(
    start_state, timesteps, step_sizes, in_weight, time_weight, conv_kernel, norm_gain, up_weight, up_bias, down_weight, out_weight,
):
    space = lax.axis_size("space")
    s, tm = lax.axis_index("space"), lax.axis_index("tm")
    beside = [(0, 1), (1, 0)]
    across = []
    for i in range(space - 1):
        across += [(2 * i + 1, 2 * i + 2), (2 * i + 2, 2 * i + 1)]

    def over_tm(x):
        return lax.ppermute(x, "tm", beside)

    def over_space(x):
        return lax.ppermute(x, ("space", "tm"), across)

    flags = jnp.stack([tm, jnp.where(tm == 0, s > 0, s < space - 1).astype(jnp.int32)]).astype(jnp.int32)
    own, inner, clock = prepare(flags, pinned(timesteps), pinned(step_sizes), pinned(start_state.transpose(0, 2, 1)))
    other_clock = over_tm(clock)
    outer = over_space(own)
    taps = conv_kernel.transpose(1, 2, 0, 3)

    partial, kept, *made = near(
        False, up_weight, down_weight, flags, own, inner, clock, other_clock,
        pinned(time_weight), pinned(up_weight), pinned(down_weight), pinned(norm_gain), in_weight, taps, up_bias, out_weight.T,
    )
    rest = (up_bias,)
    terms, sent = edge(False, flags, outer, own, clock, other_clock, partial, kept, *made, *rest)
    inner_terms, outer_terms = over_tm(sent), over_space(sent)
    partial, kept = near(True, up_weight, down_weight, flags, own, inner, terms, inner_terms, *made, *rest)
    keep, give = edge(True, flags, outer, own, outer_terms, terms, clock, other_clock, partial, kept, *made, *rest)
    return finish(flags, keep, over_tm(give)).transpose(0, 1, 3, 2)


def solution(mesh):
    both = P(("groups", "tm"))
    return jax.shard_map(
        on_device,
        mesh=mesh,
        in_specs=(P(("groups", "space"), None, None), both, both) + (P(),) * 8,
        out_specs=P("tm", ("groups", "space"), None, None),
        check_vma=False,
    )
```

```python
import functools
import math

import jax
import jax.numpy as jnp
from jax import lax
from jax.experimental import pallas as pl
from jax.experimental.pallas import tpu as pltpu
from jax.sharding import PartitionSpec as P

HIGH = lax.Precision.HIGHEST
F32, BF16 = jnp.float32, jnp.bfloat16
COLS, CHAN, WIDTH, HIDDEN, LANES = 32, 16, 256, 1024, 128
OWN, TAPS, HALO = 8, 7, 3
REACH = 2 * HALO
PAD = 8
WIDE = COLS + 2 * PAD
TIMES = 3
CHUNK = 256


def split(x):
    hi = x.astype(BF16)
    return hi, (x - hi.astype(F32)).astype(BF16)


def dot(a, b):
    return lax.dot_general(a, b, (((1,), (0,)), ((), ())), preferred_element_type=F32)


def dot_nt(a, b):
    return lax.dot_general(a, b, (((1,), (1,)), ((), ())), preferred_element_type=F32)


def lane_group(shape):
    return lax.broadcasted_iota(jnp.int32, shape, len(shape) - 1) // CHAN


def make_spread(spread, three):
    row = lax.broadcasted_iota(jnp.int32, (CHAN, LANES), 0)
    col = lax.broadcasted_iota(jnp.int32, (CHAN, LANES), 1)
    hit, group = row == col % CHAN, col // CHAN
    spread[...] = jnp.zeros_like(spread)
    three[...] = jnp.zeros_like(three)

    def cells(where):
        return jnp.where(where, 1.0, 0.0).astype(BF16)

    for j in range(OWN):
        rows, lanes = slice(j * CHAN, (j + 1) * CHAN), slice(j * LANES, (j + 1) * LANES)
        spread[rows, lanes] = cells(hit)
        three[rows, lanes] = cells(hit & ((group == 0) | (group == 2)))
        three[LANES + j * CHAN : LANES + (j + 1) * CHAN, lanes] = cells(hit & (group == 1))


def normalise(conv, gain):
    mean = jnp.mean(conv, axis=-1, keepdims=True)
    centered = conv - mean
    var = jnp.mean(centered * centered, axis=-1, keepdims=True)
    return (centered * lax.rsqrt(var + 1e-06) * gain).astype(BF16)


def gelu(x):
    x = x.astype(BF16)
    inner = x * (BF16(0.7978845608028654) + BF16(0.035677408136300125) * (x * x))
    half = BF16(0.5) * x
    return half + half * jnp.tanh(inner)


def prepare_kernel(flags, times, sizes, start, own, inner, clock):
    turned = flags[0] == 1
    top = to_dense([start[h] for h in range(OWN)])
    bottom = to_dense([start[2 * OWN - 1 - h] for h in range(OWN)])
    own[...] = jnp.where(turned, bottom, top)
    inner[...] = jnp.where(turned, top, bottom)
    lane = lax.broadcasted_iota(jnp.int32, clock.shape, 1)
    values = (times[0].astype(F32), times[1].astype(F32), sizes[0], sizes[1])
    filled = jnp.zeros(clock.shape, F32)
    for i, value in enumerate(values):
        filled = jnp.where(lane == i, value, filled)
    clock[...] = filled


def finish_kernel(flags, keep, got, out):
    turned = flags[0] == 1
    for t in range(2):
        top = jnp.where(turned, got[t], keep[t])
        bottom = jnp.where(turned, keep[t], got[t])
        out[t, 0:OWN] = top.T.reshape(OWN, CHAN, COLS)
        flipped = bottom.T.reshape(OWN, CHAN, COLS)
        for h in range(OWN):
            out[t, 2 * OWN - 1 - h] = flipped[h]


def pinned(x):
    return pltpu.with_memory_space_constraint(x, pltpu.HBM)


def to_dense(rows):
    return jnp.concatenate(rows, axis=0).T


def row_of(turn, dy):
    return dy + turn * (TAPS - 1 - 2 * dy)


def both_clocks(turn, mine, other):
    first = turn == 0
    return jnp.where(first, mine[0:1, :], other[0:1, :]), jnp.where(first, other[0:1, :], mine[0:1, :])


def embed(turn, mine, other, time_w):
    low, high = both_clocks(turn, mine, other)
    steps = jnp.concatenate([low[:, 0:1], low[:, 1:2], high[:, 0:1], high[:, 1:2]] * 2, axis=0)
    lane = lax.broadcasted_iota(jnp.int32, (1, LANES), 1).astype(F32)
    angle = steps * jnp.exp(lane * (-math.log(10000.0) / LANES))
    feats = jnp.concatenate([jnp.sin(angle), jnp.cos(angle)], axis=1)
    return lax.dot_general(feats, time_w[...], (((1,), (0,)), ((), ())), precision=HIGH, preferred_element_type=F32)


def make_weff(turn, in_w, taps, weff):
    weff[...] = jnp.zeros_like(weff)
    for dy in range(TAPS):
        for dx in range(TAPS):
            low = dy * LANES + dx * CHAN
            weff[low : low + CHAN, :] = (in_w[...] * taps[row_of(turn, dy), dx, 0:1, :]).astype(BF16)


def make_by_row(turn, taps, by_row):
    column = lax.broadcasted_iota(jnp.int32, (COLS, WIDTH), 0)
    for dy in range(TAPS):
        total = jnp.zeros((COLS, WIDTH), F32)
        for dx in range(TAPS):
            ok = (column + (dx - HALO) >= 0) & (column + (dx - HALO) < COLS)
            total = total + jnp.where(ok, taps[row_of(turn, dy), dx, 0:1, :], 0.0)
        by_row[dy] = total


def make_in_three(in_w, in_three):
    hi, lo = split(in_w[...])
    in_three[...] = jnp.concatenate([hi, hi, lo, jnp.zeros((LANES - 3 * CHAN, WIDTH), BF16)], axis=0)


def make_tap_rows(turn, taps, tap_rows):
    for dy in range(TAPS):
        for dx in range(TAPS):
            for half in range(2):
                lanes = slice(half * LANES, (half + 1) * LANES)
                tap_rows[half, dy * TAPS + dx : dy * TAPS + dx + 1, :] = taps[row_of(turn, dy), dx, 1:2, lanes]


def clear_sides(ref):
    side = jnp.zeros(ref.shape[:-2] + (PAD, LANES), F32)
    ref[..., 0:PAD, :] = side
    ref[..., PAD + COLS :, :] = side


def block_zero(states, place, count, weff, in_three, shift, patch, centre, spread, three):
    rows, many, blocks = count + REACH, len(states), len(states[0])
    hi, lo = split(jnp.concatenate([block for state in states for block in state], axis=0))

    def spots(flat):
        for n in range(many):
            for k in range(blocks):
                low = (n * blocks + k) * COLS
                for j in range(OWN):
                    i = place(k, j)
                    if i is not None:
                        yield n, i, flat[low : low + COLS, j * LANES : (j + 1) * LANES]

    clear_sides(shift)
    for n, i, x in spots(dot(hi, spread[...])):
        shift[n, i, PAD : PAD + COLS, :] = x
    for n, i, x in spots(dot(jnp.concatenate([hi, lo], axis=-1), three[...])):
        if HALO <= i < HALO + count:
            centre[n, i - HALO] = x.astype(BF16)
    group = lane_group((COLS, LANES))
    at = PAD - HALO
    for n in range(many):
        for i in range(rows):
            picked = shift[n, i, at : at + COLS, :]
            for dx in range(1, TAPS):
                picked = jnp.where(group == dx, shift[n, i, at + dx : at + dx + COLS, :], picked)
            patch[n, i] = picked.astype(BF16)
    cells = many * count * COLS
    wide = [patch[0:many, dy : dy + count].reshape(cells, LANES) for dy in range(TAPS)]
    base = dot(jnp.concatenate(wide, axis=-1), weff[...])
    stream = dot(centre[0:many].reshape(cells, LANES), in_three[...])
    shape = (many, count, COLS, WIDTH)
    return base.reshape(shape), stream.reshape(shape)


def first_block(
    states, place, count, ones, first_time, temb, gain, up_w, up_b, down_w, weff, in_three, shift, patch, centre, spread, three,
    normed, copies=(), batched=True,
):
    base, stream = block_zero(states, place, count, weff, in_three, shift, patch, centre, spread, three)
    cells, residual = count * COLS, []

    def prepare_time(t):
        n = min(t, len(states) - 1)
        shown = temb[first_time + t : first_time + t + 1, :]
        lift = [ones[i] * shown for i in range(len(ones))]
        for i in range(count):
            low = t * cells + i * COLS
            normed[low : low + COLS, :] = normalise(base[n, i] + lift[min(i, len(ones) - 1)], gain[0:1, :])
        residual.append(stream[n] + shown)

    if batched:
        for t in range(TIMES):
            prepare_time(t)
        for copy in copies:
            copy.wait()
        out = pointwise(normed[...], 0, up_w, up_b, down_w).reshape(TIMES, count, COLS, WIDTH)
    for t in range(TIMES):
        if batched:
            yield residual[t] + out[t]
        else:
            prepare_time(t)
            single = pointwise(normed[t * cells : (t + 1) * cells, :], 0, up_w, up_b, down_w)
            yield residual[t] + single.reshape(count, COLS, WIDTH)


def pointwise(normed, block, up_w, up_b, down_w):
    hidden = []
    for low in range(0, HIDDEN, CHUNK):
        hidden.append(gelu(dot(normed, up_w[block, :, low : low + CHUNK]) + up_b[block : block + 1, low : low + CHUNK]))
    return dot(jnp.concatenate(hidden, axis=-1), down_w[block])


def depthwise(tap_rows, half, source, pairs, begin, done, group_size=4):
    heights = sorted(pairs)
    groups = [heights[i : i + group_size] for i in range(0, len(heights), group_size)]
    for group in groups:
        acc = {h: begin(h) for h in group}
        needed = sorted({i for h in group for i in pairs[h]})
        for dx in range(TAPS):
            for i in needed:
                x = source(i, dx)
                for h in group:
                    if i in pairs[h]:
                        at = (i - h + HALO) * TAPS + dx
                        acc[h] = acc[h] + x * tap_rows[half, at : at + 1, :]
        for h in group:
            done(h, acc[h])


NEAR = range(HALO, OWN + HALO)
EDGE = range(-HALO, HALO)


def pairs_of(rows):
    found = {h: [i for i in rows if abs(i - h) <= HALO] for h in range(OWN)}
    return {h: listed for h, listed in found.items() if listed}


def near_kernel(last, *refs):
    first_time = 1 if last else 0
    count = len(NEAR)
    if last:
        (flags, own, inner, mine, inner_terms, temb, weff, by_row, tap_rows, spread, three, in_three, _, gain, up_w, down_w, up_b,
         partial, kept, shift, patch, centre, normed, wide) = refs
        turn = flags[0]
        copies, states, state = [], [], [own[...], inner[...]]
        for t in range(TIMES):
            state = [state[0] + mine[t], state[1] + inner_terms[t].astype(F32)]
            states.append(state)
    else:
        (flags, own, inner, clock, other_clock, time_hbm, up_hbm, down_hbm, gain_hbm, in_w, taps, up_b, out_t,
         partial, kept, temb, weff, by_row, tap_rows, spread, three, in_three, out_three, gain, up_w, down_w,
         shift, patch, centre, normed, wide, time_w, sems) = refs
        turn = flags[0]
        copies = [pltpu.make_async_copy(time_hbm, time_w, sems.at[4]), pltpu.make_async_copy(gain_hbm, gain, sems.at[5])]
        for block in range(2):
            copies.append(pltpu.make_async_copy(up_hbm.at[block], up_w.at[block], sems.at[2 * block]))
            copies.append(pltpu.make_async_copy(down_hbm.at[block], down_w.at[block], sems.at[2 * block + 1]))
        for copy in copies:
            copy.start()
        make_weff(turn, in_w, taps, weff)
        make_by_row(turn, taps, by_row)
        make_tap_rows(turn, taps, tap_rows)
        make_spread(spread, three)
        make_in_three(in_w, in_three)
        out_hi, out_lo = split(jnp.concatenate([out_t[...]] * 8, axis=0))
        out_three[...] = jnp.concatenate([out_hi, out_hi, out_lo], axis=-1)
        copies[0].wait()
        temb[...] = embed(turn, clock, other_clock, time_w)
        states = [[own[...], inner[...]]]
        copies[1].wait()
    ones = by_row[0]
    for dy in range(1, TAPS):
        ones = ones + by_row[dy]
    clear_sides(wide)

    def place(k, j):
        i = j if k == 0 else 2 * OWN - 1 - j
        return i if i < count + REACH else None

    found = first_block(
        states, place, count, [ones], first_time, temb, gain, up_w, up_b, down_w, weff, in_three,
        shift, patch, centre, spread, three, normed, copies[2:4],
    )
    for t, after in enumerate(found):
        kept[t] = after[0 : OWN - HALO]
        for half in range(2):
            wide[2 * t + half, :, PAD : PAD + COLS, :] = after[:, :, half * LANES : (half + 1) * LANES]

    def tapped(half, t, carry):
        def source(i, dx):
            low = PAD - HALO + dx
            return wide[2 * t + half, i - HALO, low : low + COLS, :]

        def done(h, x):
            partial[2 * t + half, h] = x

        depthwise(tap_rows, half, source, pairs_of(NEAR), lambda h: jnp.zeros((COLS, LANES), F32), done, OWN)
        return carry

    lax.fori_loop(0, TIMES, lambda t, carry: tapped(1, t, tapped(0, t, carry)), 0)
    if not last:
        copies[4].wait()
        copies[5].wait()


def edge_kernel(last, *refs):
    if last:
        flags, outer, own, outer_terms, mine, *refs = refs
    else:
        flags, outer, own, *refs = refs
    (clock, other_clock, partial, kept, temb, weff, by_row, tap_rows, spread, three, in_three, out_three, gain, up_w, down_w, up_b,
     first_out, second_out, shift, patch, centre, normed, second_normed, *wide) = refs
    conv_buf = wide[2 * TIMES :]
    turn, inside = flags[0], flags[1].astype(F32)
    first_time = 1 if last else 0
    count = len(EDGE)
    ones = []
    for r in EDGE:
        seen = jnp.zeros((COLS, WIDTH), F32)
        hidden = jnp.zeros((COLS, WIDTH), F32)
        for dy in range(TAPS):
            if r + dy - HALO >= 0:
                seen = seen + by_row[dy]
            else:
                hidden = hidden + by_row[dy]
        ones.append(seen + hidden * inside)
    for ref in wide[: 2 * TIMES]:
        clear_sides(ref)
    low, high = both_clocks(turn, clock, other_clock)
    sizes = [low[:, 2:3], low[:, 3:4], high[:, 2:3], high[:, 3:4]]
    group = lane_group((1, LANES))

    def place(k, j):
        if j >= REACH:
            return None
        return REACH - 1 - j if k == 0 else REACH + j

    states, state = [], [outer[...], own[...]]
    for t in range(TIMES if last else 0):
        state = [state[0] + outer_terms[t].astype(F32), state[1] + mine[t]]
        states.append(state)
    found = first_block(
        states if last else [state], place, count, ones, first_time, temb, gain, up_w, up_b, down_w, weff, in_three,
        shift, patch, centre, spread, three, normed,
    )
    touched = len(pairs_of(EDGE))
    terms = []
    for t, after in enumerate(found):
        for half in range(2):
            lanes = slice(half * LANES, (half + 1) * LANES)
            wide[2 * t + half][0:HALO, PAD : PAD + COLS, :] = after[0:HALO, :, lanes] * inside
            wide[2 * t + half][HALO:, PAD : PAD + COLS, :] = after[HALO:, :, lanes]

        def source(half, i, dx):
            low = PAD - HALO + dx
            return wide[2 * t + half][i + HALO, low : low + COLS, :]

        def done(half, h, x):
            conv_buf[t][h, :, half * LANES : (half + 1) * LANES] = x

        for half in range(2):
            depthwise(
                tap_rows, half, functools.partial(source, half), pairs_of(EDGE), lambda h: partial[2 * t + half, h],
                functools.partial(done, half),
            )
        first = t * OWN * COLS
        for h in range(OWN):
            low = first + h * COLS
            if h < touched:
                conv = conv_buf[t][h]
            else:
                conv = jnp.concatenate([partial[2 * t + half, h] for half in range(2)], axis=-1)
            second_normed[low : low + COLS, :] = normalise(conv, gain[1:2, :])
        stream = [after[HALO:].reshape(HALO * COLS, WIDTH), kept[t].reshape((OWN - HALO) * COLS, WIDTH)]
        out = pointwise(second_normed[first : first + OWN * COLS, :], 1, up_w, up_b, down_w)
        hi, lo = split(jnp.concatenate(stream, axis=0) + out)
        drift = dot_nt(jnp.concatenate([hi, lo, hi], axis=-1), out_three[...]).reshape(OWN, COLS, LANES)
        dense = drift[0]
        for j in range(1, OWN):
            dense = jnp.where(group == j, drift[j], dense)
        terms.append(dense * sizes[first_time + t])
    if last:
        n0 = states[0][1]
        n1 = n0 + terms[0]
        n2 = n1 + terms[1]
        n3 = n2 + terms[2]
        turned = turn == 1
        for i, (early, late) in enumerate(((n0, n2), (n1, n3))):
            first_out[i] = jnp.where(turned, late, early)
            second_out[i] = jnp.where(turned, early, late)
    else:
        for t in range(TIMES):
            first_out[t] = terms[t]
            second_out[t] = terms[t].astype(BF16)


SMEM = pl.BlockSpec(memory_space=pltpu.SMEM)
VMEM = pl.BlockSpec(memory_space=pltpu.VMEM)
HBM = pl.BlockSpec(memory_space=pltpu.HBM)
SMALL = pltpu.CompilerParams(vmem_limit_bytes=4 * 2**20)
LARGE = pltpu.CompilerParams(vmem_limit_bytes=20 * 2**20)


def working(count, many):
    return [
        pltpu.VMEM((many, count + REACH, WIDE, LANES), F32),
        pltpu.VMEM((many, count + REACH, COLS, LANES), BF16),
        pltpu.VMEM((many, count, COLS, LANES), BF16),
        pltpu.VMEM((TIMES * count * COLS, WIDTH), BF16),
    ]


def near(last, up_w, down_w, *args):
    outs = [pltpu.VMEM((2 * TIMES, OWN, COLS, LANES), F32), pltpu.VMEM((TIMES, OWN - HALO, COLS, WIDTH), F32)]
    scratch = working(len(NEAR), TIMES if last else 1) + [pltpu.VMEM((2 * TIMES, len(NEAR), WIDE, LANES), F32)]
    if last:
        specs = [SMEM] + [VMEM] * (len(args) - 1)
    else:
        outs += [pltpu.VMEM((8, WIDTH), F32), pltpu.VMEM((TAPS * LANES, WIDTH), BF16), pltpu.VMEM((TAPS, COLS, WIDTH), F32)]
        outs += [pltpu.VMEM((2, 56, LANES), F32), pltpu.VMEM((LANES, OWN * LANES), BF16)]
        outs += [pltpu.VMEM((2 * LANES, OWN * LANES), BF16), pltpu.VMEM((LANES, WIDTH), BF16), pltpu.VMEM((LANES, 3 * WIDTH), BF16)]
        outs += [pltpu.VMEM((2, WIDTH), F32)]
        outs += [pltpu.VMEM(up_w.shape, BF16), pltpu.VMEM(down_w.shape, BF16)]
        scratch += [pltpu.VMEM((WIDTH, WIDTH), F32), pltpu.SemaphoreType.DMA((6,))]
        specs = [SMEM] + [VMEM] * 4 + [HBM] * 4 + [VMEM] * 4
    return pl.pallas_call(
        functools.partial(near_kernel, last),
        out_shape=outs,
        in_specs=specs,
        out_specs=[VMEM] * len(outs),
        scratch_shapes=scratch,
        compiler_params=LARGE,
    )(*args)


def edge(last, *args):
    if last:
        outs = [jax.ShapeDtypeStruct((2, COLS, LANES), F32)] * 2
    else:
        outs = [jax.ShapeDtypeStruct((TIMES, COLS, LANES), kind) for kind in (F32, BF16)]
    touched = len(pairs_of(EDGE))
    return pl.pallas_call(
        functools.partial(edge_kernel, last),
        out_shape=outs,
        in_specs=[SMEM] + [VMEM] * (len(args) - 1),
        out_specs=[VMEM, VMEM],
        scratch_shapes=working(len(EDGE), TIMES if last else 1)
        + [pltpu.VMEM((TIMES * OWN * COLS, WIDTH), BF16)]
        + [pltpu.VMEM((len(EDGE), WIDE, LANES), F32)] * (2 * TIMES)
        + [pltpu.VMEM((touched, COLS, WIDTH), F32)] * TIMES,
        compiler_params=LARGE,
    )(*args)


def prepare(flags, times, sizes, turned_start):
    dense = jax.ShapeDtypeStruct((COLS, LANES), F32)
    return pl.pallas_call(
        prepare_kernel,
        out_shape=[dense, dense, jax.ShapeDtypeStruct((32, LANES), F32)],
        in_specs=[SMEM, SMEM, SMEM, VMEM],
        out_specs=[VMEM] * 3,
        compiler_params=SMALL,
    )(flags, times, sizes, turned_start)


def finish(flags, keep, got):
    return pl.pallas_call(
        finish_kernel,
        out_shape=jax.ShapeDtypeStruct((2, 2 * OWN, CHAN, COLS), F32),
        in_specs=[SMEM, VMEM, VMEM],
        out_specs=VMEM,
        compiler_params=SMALL,
    )(flags, keep, got)


def on_device(
    start_state, timesteps, step_sizes, in_weight, time_weight, conv_kernel, norm_gain, up_weight, up_bias, down_weight, out_weight,
):
    space = lax.axis_size("space")
    s, tm = lax.axis_index("space"), lax.axis_index("tm")
    beside = [(0, 1), (1, 0)]
    across = []
    for i in range(space - 1):
        across += [(2 * i + 1, 2 * i + 2), (2 * i + 2, 2 * i + 1)]

    def over_tm(x):
        return lax.ppermute(x, "tm", beside)

    def over_space(x):
        return lax.ppermute(x, ("space", "tm"), across)

    flags = jnp.stack([tm, jnp.where(tm == 0, s > 0, s < space - 1).astype(jnp.int32)]).astype(jnp.int32)
    own, inner, clock = prepare(flags, pinned(timesteps), pinned(step_sizes), pinned(start_state.transpose(0, 2, 1)))
    other_clock = over_tm(clock)
    outer = over_space(own)
    taps = conv_kernel.transpose(1, 2, 0, 3)

    partial, kept, *made = near(
        False, up_weight, down_weight, flags, own, inner, clock, other_clock,
        pinned(time_weight), pinned(up_weight), pinned(down_weight), pinned(norm_gain), in_weight, taps, up_bias, out_weight.T,
    )
    rest = (up_bias,)
    terms, sent = edge(False, flags, outer, own, clock, other_clock, partial, kept, *made, *rest)
    inner_terms, outer_terms = over_tm(sent), over_space(sent)
    partial, kept = near(True, up_weight, down_weight, flags, own, inner, terms, inner_terms, *made, *rest)
    keep, give = edge(True, flags, outer, own, outer_terms, terms, clock, other_clock, partial, kept, *made, *rest)
    return finish(flags, keep, over_tm(give)).transpose(0, 1, 3, 2)


def solution(mesh):
    both = P(("groups", "tm"))
    return jax.shard_map(
        on_device,
        mesh=mesh,
        in_specs=(P(("groups", "space"), None, None), both, both) + (P(),) * 8,
        out_specs=P("tm", ("groups", "space"), None, None),
        check_vma=False,
    )
```

```python
import functools
import math

import jax
import jax.numpy as jnp
from jax import lax
from jax.experimental import pallas as pl
from jax.experimental.pallas import tpu as pltpu
from jax.sharding import PartitionSpec as P

HIGH = lax.Precision.HIGHEST
F32, BF16 = jnp.float32, jnp.bfloat16
COLS, CHAN, WIDTH, HIDDEN, LANES = 32, 16, 256, 1024, 128
OWN, TAPS, HALO = 8, 7, 3
REACH = 2 * HALO
PAD = 8
WIDE = COLS + 2 * PAD
TIMES = 3
CHUNK = 256


def split(x):
    hi = x.astype(BF16)
    return hi, (x - hi.astype(F32)).astype(BF16)


def dot(a, b):
    return lax.dot_general(a, b, (((1,), (0,)), ((), ())), preferred_element_type=F32)


def dot_nt(a, b):
    return lax.dot_general(a, b, (((1,), (1,)), ((), ())), preferred_element_type=F32)


def lane_group(shape):
    return lax.broadcasted_iota(jnp.int32, shape, len(shape) - 1) // CHAN


def make_spread(spread, three):
    row = lax.broadcasted_iota(jnp.int32, (CHAN, LANES), 0)
    col = lax.broadcasted_iota(jnp.int32, (CHAN, LANES), 1)
    hit, group = row == col % CHAN, col // CHAN
    spread[...] = jnp.zeros_like(spread)
    three[...] = jnp.zeros_like(three)

    def cells(where):
        return jnp.where(where, 1.0, 0.0).astype(BF16)

    for j in range(OWN):
        rows, lanes = slice(j * CHAN, (j + 1) * CHAN), slice(j * LANES, (j + 1) * LANES)
        spread[rows, lanes] = cells(hit)
        three[rows, lanes] = cells(hit & ((group == 0) | (group == 2)))
        three[LANES + j * CHAN : LANES + (j + 1) * CHAN, lanes] = cells(hit & (group == 1))


def normalise(conv, gain):
    mean = jnp.mean(conv, axis=-1, keepdims=True)
    centered = conv - mean
    var = jnp.mean(centered * centered, axis=-1, keepdims=True)
    return (centered * lax.rsqrt(var + 1e-06) * gain).astype(BF16)


def gelu(x):
    x = x.astype(BF16)
    inner = x * (BF16(0.7978845608028654) + BF16(0.035677408136300125) * (x * x))
    half = BF16(0.5) * x
    return half + half * jnp.tanh(inner)


def prepare_kernel(flags, times, sizes, start, own, inner, clock):
    turned = flags[0] == 1
    top = to_dense([start[h] for h in range(OWN)])
    bottom = to_dense([start[2 * OWN - 1 - h] for h in range(OWN)])
    own[...] = jnp.where(turned, bottom, top)
    inner[...] = jnp.where(turned, top, bottom)
    lane = lax.broadcasted_iota(jnp.int32, clock.shape, 1)
    values = (times[0].astype(F32), times[1].astype(F32), sizes[0], sizes[1])
    filled = jnp.zeros(clock.shape, F32)
    for i, value in enumerate(values):
        filled = jnp.where(lane == i, value, filled)
    clock[...] = filled


def finish_kernel(flags, keep, got, out_hbm, out, sems):
    turned = flags[0] == 1
    copies = [pltpu.make_async_copy(out.at[t], out_hbm.at[t], sems.at[t]) for t in range(2)]
    for t in range(2):
        top = jnp.where(turned, got[t], keep[t])
        bottom = jnp.where(turned, keep[t], got[t])
        out[t, 0:OWN] = top.T.reshape(OWN, CHAN, COLS)
        flipped = bottom.T.reshape(OWN, CHAN, COLS)
        for h in range(OWN):
            out[t, 2 * OWN - 1 - h] = flipped[h]
        copies[t].start()
    for copy in copies:
        copy.wait()


def pinned(x):
    return pltpu.with_memory_space_constraint(x, pltpu.HBM)


def to_dense(rows):
    return jnp.concatenate(rows, axis=0).T


def row_of(turn, dy):
    return dy + turn * (TAPS - 1 - 2 * dy)


def both_clocks(turn, mine, other):
    first = turn == 0
    return jnp.where(first, mine[0:1, :], other[0:1, :]), jnp.where(first, other[0:1, :], mine[0:1, :])


def embed(turn, mine, other, time_w):
    low, high = both_clocks(turn, mine, other)
    steps = jnp.concatenate([low[:, 0:1], low[:, 1:2], high[:, 0:1], high[:, 1:2]] * 2, axis=0)
    lane = lax.broadcasted_iota(jnp.int32, (1, LANES), 1).astype(F32)
    angle = steps * jnp.exp(lane * (-math.log(10000.0) / LANES))
    feats = jnp.concatenate([jnp.sin(angle), jnp.cos(angle)], axis=1)
    return lax.dot_general(feats, time_w[...], (((1,), (0,)), ((), ())), precision=HIGH, preferred_element_type=F32)


def make_weff(turn, in_w, taps, weff):
    weff[...] = jnp.zeros_like(weff)
    for dy in range(TAPS):
        for dx in range(TAPS):
            low = dy * LANES + dx * CHAN
            weff[low : low + CHAN, :] = (in_w[...] * taps[row_of(turn, dy), dx, 0:1, :]).astype(BF16)


def make_by_row(turn, taps, by_row):
    column = lax.broadcasted_iota(jnp.int32, (COLS, WIDTH), 0)
    for dy in range(TAPS):
        total = jnp.zeros((COLS, WIDTH), F32)
        for dx in range(TAPS):
            ok = (column + (dx - HALO) >= 0) & (column + (dx - HALO) < COLS)
            total = total + jnp.where(ok, taps[row_of(turn, dy), dx, 0:1, :], 0.0)
        by_row[dy] = total


def make_in_three(in_w, in_three):
    hi, lo = split(in_w[...])
    in_three[...] = jnp.concatenate([hi, hi, lo, jnp.zeros((LANES - 3 * CHAN, WIDTH), BF16)], axis=0)


def make_tap_rows(turn, taps, tap_rows):
    for dy in range(TAPS):
        for dx in range(TAPS):
            for half in range(2):
                lanes = slice(half * LANES, (half + 1) * LANES)
                tap_rows[half, dy * TAPS + dx : dy * TAPS + dx + 1, :] = taps[row_of(turn, dy), dx, 1:2, lanes]


def clear_sides(ref):
    side = jnp.zeros(ref.shape[:-2] + (PAD, LANES), F32)
    ref[..., 0:PAD, :] = side
    ref[..., PAD + COLS :, :] = side


def block_zero(states, place, count, weff, in_three, shift, patch, centre, spread, three):
    rows, many, blocks = count + REACH, len(states), len(states[0])
    hi, lo = split(jnp.concatenate([block for state in states for block in state], axis=0))

    def spots(flat):
        for n in range(many):
            for k in range(blocks):
                low = (n * blocks + k) * COLS
                for j in range(OWN):
                    i = place(k, j)
                    if i is not None:
                        yield n, i, flat[low : low + COLS, j * LANES : (j + 1) * LANES]

    clear_sides(shift)
    for n, i, x in spots(dot(hi, spread[...])):
        shift[n, i, PAD : PAD + COLS, :] = x
    for n, i, x in spots(dot(jnp.concatenate([hi, lo], axis=-1), three[...])):
        if HALO <= i < HALO + count:
            centre[n, i - HALO] = x.astype(BF16)
    group = lane_group((COLS, LANES))
    at = PAD - HALO
    for n in range(many):
        for i in range(rows):
            picked = shift[n, i, at : at + COLS, :]
            for dx in range(1, TAPS):
                picked = jnp.where(group == dx, shift[n, i, at + dx : at + dx + COLS, :], picked)
            patch[n, i] = picked.astype(BF16)
    cells = many * count * COLS
    wide = [patch[0:many, dy : dy + count].reshape(cells, LANES) for dy in range(TAPS)]
    base = dot(jnp.concatenate(wide, axis=-1), weff[...])
    stream = dot(centre[0:many].reshape(cells, LANES), in_three[...])
    shape = (many, count, COLS, WIDTH)
    return base.reshape(shape), stream.reshape(shape)


def first_block(
    states, place, count, ones, first_time, temb, gain, up_w, up_b, down_w, weff, in_three, shift, patch, centre, spread, three,
    normed, copies=(), batched=True,
):
    base, stream = block_zero(states, place, count, weff, in_three, shift, patch, centre, spread, three)
    cells, residual = count * COLS, []

    def prepare_time(t):
        n = min(t, len(states) - 1)
        shown = temb[first_time + t : first_time + t + 1, :]
        lift = [ones[i] * shown for i in range(len(ones))]
        for i in range(count):
            low = t * cells + i * COLS
            normed[low : low + COLS, :] = normalise(base[n, i] + lift[min(i, len(ones) - 1)], gain[0:1, :])
        residual.append(stream[n] + shown)

    if batched:
        for t in range(TIMES):
            prepare_time(t)
        for copy in copies:
            copy.wait()
        out = pointwise(normed[...], 0, up_w, up_b, down_w).reshape(TIMES, count, COLS, WIDTH)
    for t in range(TIMES):
        if batched:
            yield residual[t] + out[t]
        else:
            prepare_time(t)
            single = pointwise(normed[t * cells : (t + 1) * cells, :], 0, up_w, up_b, down_w)
            yield residual[t] + single.reshape(count, COLS, WIDTH)


def pointwise(normed, block, up_w, up_b, down_w):
    hidden = []
    for low in range(0, HIDDEN, CHUNK):
        hidden.append(gelu(dot(normed, up_w[block, :, low : low + CHUNK]) + up_b[block : block + 1, low : low + CHUNK]))
    return dot(jnp.concatenate(hidden, axis=-1), down_w[block])


def depthwise(tap_rows, half, source, pairs, begin, done, group_size=4):
    heights = sorted(pairs)
    groups = [heights[i : i + group_size] for i in range(0, len(heights), group_size)]
    for group in groups:
        acc = {h: begin(h) for h in group}
        needed = sorted({i for h in group for i in pairs[h]})
        for dx in range(TAPS):
            for i in needed:
                x = source(i, dx)
                for h in group:
                    if i in pairs[h]:
                        at = (i - h + HALO) * TAPS + dx
                        acc[h] = acc[h] + x * tap_rows[half, at : at + 1, :]
        for h in group:
            done(h, acc[h])


NEAR = range(HALO, OWN + HALO)
EDGE = range(-HALO, HALO)


def pairs_of(rows):
    found = {h: [i for i in rows if abs(i - h) <= HALO] for h in range(OWN)}
    return {h: listed for h, listed in found.items() if listed}


def near_kernel(last, *refs):
    first_time = 1 if last else 0
    count = len(NEAR)
    if last:
        (flags, own, inner, mine, inner_terms, temb, weff, by_row, tap_rows, spread, three, in_three, _, gain, up_w, down_w, up_b,
         partial, kept, shift, patch, centre, normed, wide) = refs
        turn = flags[0]
        copies, states, state = [], [], [own[...], inner[...]]
        for t in range(TIMES):
            state = [state[0] + mine[t], state[1] + inner_terms[t].astype(F32)]
            states.append(state)
    else:
        (flags, own, inner, clock, other_clock, time_hbm, up_hbm, down_hbm, gain_hbm, in_w, taps, up_b, out_t,
         partial, kept, temb, weff, by_row, tap_rows, spread, three, in_three, out_three, gain, up_w, down_w,
         shift, patch, centre, normed, wide, time_w, sems) = refs
        turn = flags[0]
        copies = [pltpu.make_async_copy(time_hbm, time_w, sems.at[4]), pltpu.make_async_copy(gain_hbm, gain, sems.at[5])]
        for block in range(2):
            copies.append(pltpu.make_async_copy(up_hbm.at[block], up_w.at[block], sems.at[2 * block]))
            copies.append(pltpu.make_async_copy(down_hbm.at[block], down_w.at[block], sems.at[2 * block + 1]))
        for copy in copies:
            copy.start()
        make_weff(turn, in_w, taps, weff)
        make_by_row(turn, taps, by_row)
        make_tap_rows(turn, taps, tap_rows)
        make_spread(spread, three)
        make_in_three(in_w, in_three)
        out_hi, out_lo = split(jnp.concatenate([out_t[...]] * 8, axis=0))
        out_three[...] = jnp.concatenate([out_hi, out_hi, out_lo], axis=-1)
        copies[0].wait()
        temb[...] = embed(turn, clock, other_clock, time_w)
        states = [[own[...], inner[...]]]
        copies[1].wait()
    ones = by_row[0]
    for dy in range(1, TAPS):
        ones = ones + by_row[dy]
    clear_sides(wide)

    def place(k, j):
        i = j if k == 0 else 2 * OWN - 1 - j
        return i if i < count + REACH else None

    found = first_block(
        states, place, count, [ones], first_time, temb, gain, up_w, up_b, down_w, weff, in_three,
        shift, patch, centre, spread, three, normed, copies[2:4],
    )
    for t, after in enumerate(found):
        kept[t] = after[0 : OWN - HALO]
        for half in range(2):
            wide[2 * t + half, :, PAD : PAD + COLS, :] = after[:, :, half * LANES : (half + 1) * LANES]

    def tapped(half, t, carry):
        def source(i, dx):
            low = PAD - HALO + dx
            return wide[2 * t + half, i - HALO, low : low + COLS, :]

        def done(h, x):
            partial[2 * t + half, h] = x

        depthwise(tap_rows, half, source, pairs_of(NEAR), lambda h: jnp.zeros((COLS, LANES), F32), done, OWN)
        return carry

    lax.fori_loop(0, TIMES, lambda t, carry: tapped(1, t, tapped(0, t, carry)), 0)
    if not last:
        copies[4].wait()
        copies[5].wait()


def edge_kernel(last, *refs):
    if last:
        flags, outer, own, outer_terms, mine, *refs = refs
    else:
        flags, outer, own, *refs = refs
    (clock, other_clock, partial, kept, temb, weff, by_row, tap_rows, spread, three, in_three, out_three, gain, up_w, down_w, up_b,
     first_out, second_out, shift, patch, centre, normed, second_normed, *wide) = refs
    conv_buf = wide[2 * TIMES :]
    turn, inside = flags[0], flags[1].astype(F32)
    first_time = 1 if last else 0
    count = len(EDGE)
    ones = []
    for r in EDGE:
        seen = jnp.zeros((COLS, WIDTH), F32)
        hidden = jnp.zeros((COLS, WIDTH), F32)
        for dy in range(TAPS):
            if r + dy - HALO >= 0:
                seen = seen + by_row[dy]
            else:
                hidden = hidden + by_row[dy]
        ones.append(seen + hidden * inside)
    for ref in wide[: 2 * TIMES]:
        clear_sides(ref)
    low, high = both_clocks(turn, clock, other_clock)
    sizes = [low[:, 2:3], low[:, 3:4], high[:, 2:3], high[:, 3:4]]
    group = lane_group((1, LANES))

    def place(k, j):
        if j >= REACH:
            return None
        return REACH - 1 - j if k == 0 else REACH + j

    states, state = [], [outer[...], own[...]]
    for t in range(TIMES if last else 0):
        state = [state[0] + outer_terms[t].astype(F32), state[1] + mine[t]]
        states.append(state)
    found = first_block(
        states if last else [state], place, count, ones, first_time, temb, gain, up_w, up_b, down_w, weff, in_three,
        shift, patch, centre, spread, three, normed,
    )
    touched = len(pairs_of(EDGE))
    terms = []
    for t, after in enumerate(found):
        for half in range(2):
            lanes = slice(half * LANES, (half + 1) * LANES)
            wide[2 * t + half][0:HALO, PAD : PAD + COLS, :] = after[0:HALO, :, lanes] * inside
            wide[2 * t + half][HALO:, PAD : PAD + COLS, :] = after[HALO:, :, lanes]

        def source(half, i, dx):
            low = PAD - HALO + dx
            return wide[2 * t + half][i + HALO, low : low + COLS, :]

        def done(half, h, x):
            conv_buf[t][h, :, half * LANES : (half + 1) * LANES] = x

        for half in range(2):
            depthwise(
                tap_rows, half, functools.partial(source, half), pairs_of(EDGE), lambda h: partial[2 * t + half, h],
                functools.partial(done, half),
            )
        first = t * OWN * COLS
        for h in range(OWN):
            low = first + h * COLS
            if h < touched:
                conv = conv_buf[t][h]
            else:
                conv = jnp.concatenate([partial[2 * t + half, h] for half in range(2)], axis=-1)
            second_normed[low : low + COLS, :] = normalise(conv, gain[1:2, :])
        stream = [after[HALO:].reshape(HALO * COLS, WIDTH), kept[t].reshape((OWN - HALO) * COLS, WIDTH)]
        out = pointwise(second_normed[first : first + OWN * COLS, :], 1, up_w, up_b, down_w)
        hi, lo = split(jnp.concatenate(stream, axis=0) + out)
        drift = dot_nt(jnp.concatenate([hi, lo, hi], axis=-1), out_three[...]).reshape(OWN, COLS, LANES)
        dense = drift[0]
        for j in range(1, OWN):
            dense = jnp.where(group == j, drift[j], dense)
        terms.append(dense * sizes[first_time + t])
    if last:
        n0 = states[0][1]
        n1 = n0 + terms[0]
        n2 = n1 + terms[1]
        n3 = n2 + terms[2]
        turned = turn == 1
        for i, (early, late) in enumerate(((n0, n2), (n1, n3))):
            first_out[i] = jnp.where(turned, late, early)
            second_out[i] = jnp.where(turned, early, late)
    else:
        for t in range(TIMES):
            first_out[t] = terms[t]
            second_out[t] = terms[t].astype(BF16)


SMEM = pl.BlockSpec(memory_space=pltpu.SMEM)
VMEM = pl.BlockSpec(memory_space=pltpu.VMEM)
HBM = pl.BlockSpec(memory_space=pltpu.HBM)
SMALL = pltpu.CompilerParams(vmem_limit_bytes=4 * 2**20)
LARGE = pltpu.CompilerParams(vmem_limit_bytes=20 * 2**20)


def working(count, many):
    return [
        pltpu.VMEM((many, count + REACH, WIDE, LANES), F32),
        pltpu.VMEM((many, count + REACH, COLS, LANES), BF16),
        pltpu.VMEM((many, count, COLS, LANES), BF16),
        pltpu.VMEM((TIMES * count * COLS, WIDTH), BF16),
    ]


def near(last, up_w, down_w, *args):
    outs = [pltpu.VMEM((2 * TIMES, OWN, COLS, LANES), F32), pltpu.VMEM((TIMES, OWN - HALO, COLS, WIDTH), F32)]
    scratch = working(len(NEAR), TIMES if last else 1) + [pltpu.VMEM((2 * TIMES, len(NEAR), WIDE, LANES), F32)]
    if last:
        specs = [SMEM] + [VMEM] * (len(args) - 1)
    else:
        outs += [pltpu.VMEM((8, WIDTH), F32), pltpu.VMEM((TAPS * LANES, WIDTH), BF16), pltpu.VMEM((TAPS, COLS, WIDTH), F32)]
        outs += [pltpu.VMEM((2, 56, LANES), F32), pltpu.VMEM((LANES, OWN * LANES), BF16)]
        outs += [pltpu.VMEM((2 * LANES, OWN * LANES), BF16), pltpu.VMEM((LANES, WIDTH), BF16), pltpu.VMEM((LANES, 3 * WIDTH), BF16)]
        outs += [pltpu.VMEM((2, WIDTH), F32)]
        outs += [pltpu.VMEM(up_w.shape, BF16), pltpu.VMEM(down_w.shape, BF16)]
        scratch += [pltpu.VMEM((WIDTH, WIDTH), F32), pltpu.SemaphoreType.DMA((6,))]
        specs = [SMEM] + [VMEM] * 4 + [HBM] * 4 + [VMEM] * 4
    return pl.pallas_call(
        functools.partial(near_kernel, last),
        out_shape=outs,
        in_specs=specs,
        out_specs=[VMEM] * len(outs),
        scratch_shapes=scratch,
        compiler_params=LARGE,
    )(*args)


def edge(last, *args):
    if last:
        outs = [jax.ShapeDtypeStruct((2, COLS, LANES), F32)] * 2
    else:
        outs = [jax.ShapeDtypeStruct((TIMES, COLS, LANES), kind) for kind in (F32, BF16)]
    touched = len(pairs_of(EDGE))
    return pl.pallas_call(
        functools.partial(edge_kernel, last),
        out_shape=outs,
        in_specs=[SMEM] + [VMEM] * (len(args) - 1),
        out_specs=[VMEM, VMEM],
        scratch_shapes=working(len(EDGE), TIMES if last else 1)
        + [pltpu.VMEM((TIMES * OWN * COLS, WIDTH), BF16)]
        + [pltpu.VMEM((len(EDGE), WIDE, LANES), F32)] * (2 * TIMES)
        + [pltpu.VMEM((touched, COLS, WIDTH), F32)] * TIMES,
        compiler_params=LARGE,
    )(*args)


def prepare(flags, times, sizes, turned_start):
    dense = jax.ShapeDtypeStruct((COLS, LANES), F32)
    return pl.pallas_call(
        prepare_kernel,
        out_shape=[dense, dense, jax.ShapeDtypeStruct((32, LANES), F32)],
        in_specs=[SMEM, SMEM, SMEM, VMEM],
        out_specs=[VMEM] * 3,
        compiler_params=SMALL,
    )(flags, times, sizes, turned_start)


def finish(flags, keep, got):
    return pl.pallas_call(
        finish_kernel,
        out_shape=jax.ShapeDtypeStruct((2, 2 * OWN, CHAN, COLS), F32),
        in_specs=[SMEM, VMEM, VMEM],
        out_specs=HBM,
        scratch_shapes=[pltpu.VMEM((2, 2 * OWN, CHAN, COLS), F32), pltpu.SemaphoreType.DMA((2,))],
        compiler_params=SMALL,
    )(flags, keep, got)


def on_device(
    start_state, timesteps, step_sizes, in_weight, time_weight, conv_kernel, norm_gain, up_weight, up_bias, down_weight, out_weight,
):
    space = lax.axis_size("space")
    s, tm = lax.axis_index("space"), lax.axis_index("tm")
    beside = [(0, 1), (1, 0)]
    across = []
    for i in range(space - 1):
        across += [(2 * i + 1, 2 * i + 2), (2 * i + 2, 2 * i + 1)]

    def over_tm(x):
        return lax.ppermute(x, "tm", beside)

    def over_space(x):
        return lax.ppermute(x, ("space", "tm"), across)

    flags = jnp.stack([tm, jnp.where(tm == 0, s > 0, s < space - 1).astype(jnp.int32)]).astype(jnp.int32)
    own, inner, clock = prepare(flags, pinned(timesteps), pinned(step_sizes), pinned(start_state.transpose(0, 2, 1)))
    other_clock = over_tm(clock)
    outer = over_space(own)
    taps = conv_kernel.transpose(1, 2, 0, 3)

    partial, kept, *made = near(
        False, up_weight, down_weight, flags, own, inner, clock, other_clock,
        pinned(time_weight), pinned(up_weight), pinned(down_weight), pinned(norm_gain), in_weight, taps, up_bias, out_weight.T,
    )
    rest = (up_bias,)
    terms, sent = edge(False, flags, outer, own, clock, other_clock, partial, kept, *made, *rest)
    inner_terms, outer_terms = over_tm(sent), over_space(sent)
    partial, kept = near(True, up_weight, down_weight, flags, own, inner, terms, inner_terms, *made, *rest)
    keep, give = edge(True, flags, outer, own, outer_terms, terms, clock, other_clock, partial, kept, *made, *rest)
    return finish(flags, keep, over_tm(give)).transpose(0, 1, 3, 2)


def solution(mesh):
    both = P(("groups", "tm"))
    return jax.shard_map(
        on_device,
        mesh=mesh,
        in_specs=(P(("groups", "space"), None, None), both, both) + (P(),) * 8,
        out_specs=P("tm", ("groups", "space"), None, None),
        check_vma=False,
    )
```

```python
import functools
import math

import jax
import jax.numpy as jnp
from jax import lax
from jax.experimental import pallas as pl
from jax.experimental.pallas import tpu as pltpu
from jax.sharding import PartitionSpec as P

HIGH = lax.Precision.HIGHEST
F32, BF16 = jnp.float32, jnp.bfloat16
COLS, CHAN, WIDTH, HIDDEN, LANES = 32, 16, 256, 1024, 128
OWN, TAPS, HALO = 8, 7, 3
REACH = 2 * HALO
PAD = 8
WIDE = COLS + 2 * PAD
TIMES = 3
CHUNK = 256


def split(x):
    hi = x.astype(BF16)
    return hi, (x - hi.astype(F32)).astype(BF16)


def dot(a, b):
    return lax.dot_general(a, b, (((1,), (0,)), ((), ())), preferred_element_type=F32)


def dot_nt(a, b):
    return lax.dot_general(a, b, (((1,), (1,)), ((), ())), preferred_element_type=F32)


def lane_group(shape):
    return lax.broadcasted_iota(jnp.int32, shape, len(shape) - 1) // CHAN


def make_spread(spread, three):
    row = lax.broadcasted_iota(jnp.int32, (CHAN, LANES), 0)
    col = lax.broadcasted_iota(jnp.int32, (CHAN, LANES), 1)
    hit, group = row == col % CHAN, col // CHAN
    spread[...] = jnp.zeros_like(spread)
    three[...] = jnp.zeros_like(three)

    def cells(where):
        return jnp.where(where, 1.0, 0.0).astype(BF16)

    for j in range(OWN):
        rows, lanes = slice(j * CHAN, (j + 1) * CHAN), slice(j * LANES, (j + 1) * LANES)
        spread[rows, lanes] = cells(hit)
        three[rows, lanes] = cells(hit & ((group == 0) | (group == 2)))
        three[LANES + j * CHAN : LANES + (j + 1) * CHAN, lanes] = cells(hit & (group == 1))


def normalise(conv, gain):
    mean = jnp.mean(conv, axis=-1, keepdims=True)
    centered = conv - mean
    var = jnp.mean(centered * centered, axis=-1, keepdims=True)
    return (centered * lax.rsqrt(var + 1e-06) * gain).astype(BF16)


def gelu(x):
    x = x.astype(BF16)
    inner = x * (BF16(0.7978845608028654) + BF16(0.035677408136300125) * (x * x))
    half = BF16(0.5) * x
    return half + half * jnp.tanh(inner)


def prepare_kernel(flags, times, sizes, start, own, inner, clock):
    turned = flags[0] == 1
    top = to_dense([start[h] for h in range(OWN)])
    bottom = to_dense([start[2 * OWN - 1 - h] for h in range(OWN)])
    own[...] = jnp.where(turned, bottom, top)
    inner[...] = jnp.where(turned, top, bottom)
    lane = lax.broadcasted_iota(jnp.int32, clock.shape, 1)
    values = (times[0].astype(F32), times[1].astype(F32), sizes[0], sizes[1])
    filled = jnp.zeros(clock.shape, F32)
    for i, value in enumerate(values):
        filled = jnp.where(lane == i, value, filled)
    clock[...] = filled


def finish_kernel(flags, keep, got, out):
    turned = flags[0] == 1
    for t in range(2):
        top = jnp.where(turned, got[t], keep[t])
        bottom = jnp.where(turned, keep[t], got[t])
        out[t, 0:OWN] = top.T.reshape(OWN, CHAN, COLS)
        flipped = bottom.T.reshape(OWN, CHAN, COLS)
        for h in range(OWN):
            out[t, 2 * OWN - 1 - h] = flipped[h]


def pinned(x):
    return pltpu.with_memory_space_constraint(x, pltpu.HBM)


def to_dense(rows):
    return jnp.concatenate(rows, axis=0).T


def row_of(turn, dy):
    return dy + turn * (TAPS - 1 - 2 * dy)


def both_clocks(turn, mine, other):
    first = turn == 0
    return jnp.where(first, mine[0:1, :], other[0:1, :]), jnp.where(first, other[0:1, :], mine[0:1, :])


def embed(turn, mine, other, time_w):
    low, high = both_clocks(turn, mine, other)
    steps = jnp.concatenate([low[:, 0:1], low[:, 1:2], high[:, 0:1], high[:, 1:2]] * 2, axis=0)
    lane = lax.broadcasted_iota(jnp.int32, (1, LANES), 1).astype(F32)
    angle = steps * jnp.exp(lane * (-math.log(10000.0) / LANES))
    feats = jnp.concatenate([jnp.sin(angle), jnp.cos(angle)], axis=1)
    return lax.dot_general(feats, time_w[...], (((1,), (0,)), ((), ())), precision=HIGH, preferred_element_type=F32)


def make_weff(turn, in_w, taps, weff):
    weff[...] = jnp.zeros_like(weff)
    for dy in range(TAPS):
        for dx in range(TAPS):
            low = dy * LANES + dx * CHAN
            weff[low : low + CHAN, :] = (in_w[...] * taps[row_of(turn, dy), dx, 0:1, :]).astype(BF16)


def make_by_row(turn, taps, by_row):
    column = lax.broadcasted_iota(jnp.int32, (COLS, WIDTH), 0)
    for dy in range(TAPS):
        total = jnp.zeros((COLS, WIDTH), F32)
        for dx in range(TAPS):
            ok = (column + (dx - HALO) >= 0) & (column + (dx - HALO) < COLS)
            total = total + jnp.where(ok, taps[row_of(turn, dy), dx, 0:1, :], 0.0)
        by_row[dy] = total


def make_in_three(in_w, in_three):
    hi, lo = split(in_w[...])
    in_three[...] = jnp.concatenate([hi, hi, lo, jnp.zeros((LANES - 3 * CHAN, WIDTH), BF16)], axis=0)


def make_tap_rows(turn, taps, tap_rows):
    for dy in range(TAPS):
        for dx in range(TAPS):
            for half in range(2):
                lanes = slice(half * LANES, (half + 1) * LANES)
                tap_rows[half, dy * TAPS + dx : dy * TAPS + dx + 1, :] = taps[row_of(turn, dy), dx, 1:2, lanes]


def clear_sides(ref):
    side = jnp.zeros(ref.shape[:-2] + (PAD, LANES), F32)
    ref[..., 0:PAD, :] = side
    ref[..., PAD + COLS :, :] = side


def block_zero(states, place, count, weff, in_three, shift, patch, centre, spread, three):
    rows, many, blocks = count + REACH, len(states), len(states[0])
    hi, lo = split(jnp.concatenate([block for state in states for block in state], axis=0))

    def spots(flat):
        for n in range(many):
            for k in range(blocks):
                low = (n * blocks + k) * COLS
                for j in range(OWN):
                    i = place(k, j)
                    if i is not None:
                        yield n, i, flat[low : low + COLS, j * LANES : (j + 1) * LANES]

    clear_sides(shift)
    for n, i, x in spots(dot(hi, spread[...])):
        shift[n, i, PAD : PAD + COLS, :] = x
    for n, i, x in spots(dot(jnp.concatenate([hi, lo], axis=-1), three[...])):
        if HALO <= i < HALO + count:
            centre[n, i - HALO] = x.astype(BF16)
    group = lane_group((COLS, LANES))
    at = PAD - HALO
    for n in range(many):
        for i in range(rows):
            picked = shift[n, i, at : at + COLS, :]
            for dx in range(1, TAPS):
                picked = jnp.where(group == dx, shift[n, i, at + dx : at + dx + COLS, :], picked)
            patch[n, i] = picked.astype(BF16)
    cells = many * count * COLS
    wide = [patch[0:many, dy : dy + count].reshape(cells, LANES) for dy in range(TAPS)]
    base = dot(jnp.concatenate(wide, axis=-1), weff[...])
    stream = dot(centre[0:many].reshape(cells, LANES), in_three[...])
    shape = (many, count, COLS, WIDTH)
    return base.reshape(shape), stream.reshape(shape)


def first_block(
    states, place, count, ones, first_time, temb, gain, up_w, up_b, down_w, weff, in_three, shift, patch, centre, spread, three,
    normed, copies=(), batched=True,
):
    base, stream = block_zero(states, place, count, weff, in_three, shift, patch, centre, spread, three)
    cells, residual = count * COLS, []

    def prepare_time(t):
        n = min(t, len(states) - 1)
        shown = temb[first_time + t : first_time + t + 1, :]
        lift = [ones[i] * shown for i in range(len(ones))]
        for i in range(count):
            low = t * cells + i * COLS
            normed[low : low + COLS, :] = normalise(base[n, i] + lift[min(i, len(ones) - 1)], gain[0:1, :])
        residual.append(stream[n] + shown)

    if batched:
        for t in range(TIMES):
            prepare_time(t)
        for copy in copies:
            copy.wait()
        out = pointwise(normed[...], 0, up_w, up_b, down_w).reshape(TIMES, count, COLS, WIDTH)
    for t in range(TIMES):
        if batched:
            yield residual[t] + out[t]
        else:
            prepare_time(t)
            single = pointwise(normed[t * cells : (t + 1) * cells, :], 0, up_w, up_b, down_w)
            yield residual[t] + single.reshape(count, COLS, WIDTH)


def pointwise(normed, block, up_w, up_b, down_w):
    hidden = []
    for low in range(0, HIDDEN, CHUNK):
        hidden.append(gelu(dot(normed, up_w[block, :, low : low + CHUNK]) + up_b[block : block + 1, low : low + CHUNK]))
    return dot(jnp.concatenate(hidden, axis=-1), down_w[block])


def depthwise(tap_rows, half, source, pairs, begin, done, group_size=4):
    heights = sorted(pairs)
    groups = [heights[i : i + group_size] for i in range(0, len(heights), group_size)]
    for group in groups:
        acc = {h: begin(h) for h in group}
        needed = sorted({i for h in group for i in pairs[h]})
        for dx in range(TAPS):
            for i in needed:
                x = source(i, dx)
                for h in group:
                    if i in pairs[h]:
                        at = (i - h + HALO) * TAPS + dx
                        acc[h] = acc[h] + x * tap_rows[half, at : at + 1, :]
        for h in group:
            done(h, acc[h])


NEAR = range(HALO, OWN + HALO)
EDGE = range(-HALO, HALO)


def pairs_of(rows):
    found = {h: [i for i in rows if abs(i - h) <= HALO] for h in range(OWN)}
    return {h: listed for h, listed in found.items() if listed}


def near_kernel(last, *refs):
    first_time = 1 if last else 0
    count = len(NEAR)
    if last:
        (flags, own, inner, mine, inner_terms, temb, weff, by_row, tap_rows, spread, three, in_three, _, gain, up_w, down_w, up_b,
         partial, kept, shift, patch, centre, normed, wide) = refs
        turn = flags[0]
        copies, states, state = [], [], [own[...], inner[...]]
        for t in range(TIMES):
            state = [state[0] + mine[t], state[1] + inner_terms[t].astype(F32)]
            states.append(state)
    else:
        (flags, own, inner, clock, other_clock, time_hbm, up_hbm, down_hbm, gain_hbm, in_w, taps, up_b, out_t,
         partial, kept, temb, weff, by_row, tap_rows, spread, three, in_three, out_three, gain, up_w, down_w,
         shift, patch, centre, normed, wide, time_w, sems) = refs
        turn = flags[0]
        copies = [pltpu.make_async_copy(time_hbm, time_w, sems.at[4]), pltpu.make_async_copy(gain_hbm, gain, sems.at[5])]
        for block in range(2):
            copies.append(pltpu.make_async_copy(up_hbm.at[block], up_w.at[block], sems.at[2 * block]))
            copies.append(pltpu.make_async_copy(down_hbm.at[block], down_w.at[block], sems.at[2 * block + 1]))
        for copy in copies:
            copy.start()
        make_weff(turn, in_w, taps, weff)
        make_by_row(turn, taps, by_row)
        make_tap_rows(turn, taps, tap_rows)
        make_spread(spread, three)
        make_in_three(in_w, in_three)
        out_hi, out_lo = split(jnp.concatenate([out_t[...]] * 8, axis=0))
        out_three[...] = jnp.concatenate([out_hi, out_hi, out_lo], axis=-1)
        copies[0].wait()
        temb[...] = embed(turn, clock, other_clock, time_w)
        states = [[own[...], inner[...]]]
        copies[1].wait()
    ones = by_row[0]
    for dy in range(1, TAPS):
        ones = ones + by_row[dy]
    clear_sides(wide)

    def place(k, j):
        i = j if k == 0 else 2 * OWN - 1 - j
        return i if i < count + REACH else None

    found = first_block(
        states, place, count, [ones], first_time, temb, gain, up_w, up_b, down_w, weff, in_three,
        shift, patch, centre, spread, three, normed, copies[2:4],
    )
    for t, after in enumerate(found):
        kept[t] = after[0 : OWN - HALO]
        for half in range(2):
            wide[2 * t + half, :, PAD : PAD + COLS, :] = after[:, :, half * LANES : (half + 1) * LANES]

    def tapped(half, t, carry):
        def source(i, dx):
            low = PAD - HALO + dx
            return wide[2 * t + half, i - HALO, low : low + COLS, :]

        def done(h, x):
            partial[2 * t + half, h] = x

        depthwise(tap_rows, half, source, pairs_of(NEAR), lambda h: jnp.zeros((COLS, LANES), F32), done, OWN)
        return carry

    lax.fori_loop(0, TIMES, lambda t, carry: tapped(1, t, tapped(0, t, carry)), 0)
    if not last:
        copies[4].wait()
        copies[5].wait()


def edge_kernel(last, *refs):
    if last:
        flags, outer, own, outer_terms, mine, *refs = refs
    else:
        flags, outer, own, *refs = refs
    (clock, other_clock, partial, kept, temb, weff, by_row, tap_rows, spread, three, in_three, out_three, gain, up_w, down_w, up_b,
     first_out, second_out, shift, patch, centre, normed, second_normed, *wide) = refs
    conv_buf = wide[2 * TIMES :]
    turn, inside = flags[0], flags[1].astype(F32)
    first_time = 1 if last else 0
    count = len(EDGE)
    ones = []
    for r in EDGE:
        seen = jnp.zeros((COLS, WIDTH), F32)
        hidden = jnp.zeros((COLS, WIDTH), F32)
        for dy in range(TAPS):
            if r + dy - HALO >= 0:
                seen = seen + by_row[dy]
            else:
                hidden = hidden + by_row[dy]
        ones.append(seen + hidden * inside)
    for ref in wide[: 2 * TIMES]:
        clear_sides(ref)
    low, high = both_clocks(turn, clock, other_clock)
    sizes = [low[:, 2:3], low[:, 3:4], high[:, 2:3], high[:, 3:4]]
    group = lane_group((1, LANES))

    def place(k, j):
        if j >= REACH:
            return None
        return REACH - 1 - j if k == 0 else REACH + j

    states, state = [], [outer[...], own[...]]
    for t in range(TIMES if last else 0):
        state = [state[0] + outer_terms[t].astype(F32), state[1] + mine[t]]
        states.append(state)
    found = first_block(
        states if last else [state], place, count, ones, first_time, temb, gain, up_w, up_b, down_w, weff, in_three,
        shift, patch, centre, spread, three, normed,
    )
    touched = len(pairs_of(EDGE))
    terms = []
    for t, after in enumerate(found):
        for half in range(2):
            lanes = slice(half * LANES, (half + 1) * LANES)
            wide[2 * t + half][0:HALO, PAD : PAD + COLS, :] = after[0:HALO, :, lanes] * inside
            wide[2 * t + half][HALO:, PAD : PAD + COLS, :] = after[HALO:, :, lanes]

        def source(half, i, dx):
            low = PAD - HALO + dx
            return wide[2 * t + half][i + HALO, low : low + COLS, :]

        def done(half, h, x):
            conv_buf[t][h, :, half * LANES : (half + 1) * LANES] = x

        for half in range(2):
            depthwise(
                tap_rows, half, functools.partial(source, half), pairs_of(EDGE), lambda h: partial[2 * t + half, h],
                functools.partial(done, half), OWN,
            )
        first = t * OWN * COLS
        for h in range(OWN):
            low = first + h * COLS
            if h < touched:
                conv = conv_buf[t][h]
            else:
                conv = jnp.concatenate([partial[2 * t + half, h] for half in range(2)], axis=-1)
            second_normed[low : low + COLS, :] = normalise(conv, gain[1:2, :])
        stream = [after[HALO:].reshape(HALO * COLS, WIDTH), kept[t].reshape((OWN - HALO) * COLS, WIDTH)]
        out = pointwise(second_normed[first : first + OWN * COLS, :], 1, up_w, up_b, down_w)
        hi, lo = split(jnp.concatenate(stream, axis=0) + out)
        drift = dot_nt(jnp.concatenate([hi, lo, hi], axis=-1), out_three[...]).reshape(OWN, COLS, LANES)
        dense = drift[0]
        for j in range(1, OWN):
            dense = jnp.where(group == j, drift[j], dense)
        terms.append(dense * sizes[first_time + t])
    if last:
        n0 = states[0][1]
        n1 = n0 + terms[0]
        n2 = n1 + terms[1]
        n3 = n2 + terms[2]
        turned = turn == 1
        for i, (early, late) in enumerate(((n0, n2), (n1, n3))):
            first_out[i] = jnp.where(turned, late, early)
            second_out[i] = jnp.where(turned, early, late)
    else:
        for t in range(TIMES):
            first_out[t] = terms[t]
            second_out[t] = terms[t].astype(BF16)


SMEM = pl.BlockSpec(memory_space=pltpu.SMEM)
VMEM = pl.BlockSpec(memory_space=pltpu.VMEM)
HBM = pl.BlockSpec(memory_space=pltpu.HBM)
SMALL = pltpu.CompilerParams(vmem_limit_bytes=4 * 2**20)
LARGE = pltpu.CompilerParams(vmem_limit_bytes=20 * 2**20)


def working(count, many):
    return [
        pltpu.VMEM((many, count + REACH, WIDE, LANES), F32),
        pltpu.VMEM((many, count + REACH, COLS, LANES), BF16),
        pltpu.VMEM((many, count, COLS, LANES), BF16),
        pltpu.VMEM((TIMES * count * COLS, WIDTH), BF16),
    ]


def near(last, up_w, down_w, *args):
    outs = [pltpu.VMEM((2 * TIMES, OWN, COLS, LANES), F32), pltpu.VMEM((TIMES, OWN - HALO, COLS, WIDTH), F32)]
    scratch = working(len(NEAR), TIMES if last else 1) + [pltpu.VMEM((2 * TIMES, len(NEAR), WIDE, LANES), F32)]
    if last:
        specs = [SMEM] + [VMEM] * (len(args) - 1)
    else:
        outs += [pltpu.VMEM((8, WIDTH), F32), pltpu.VMEM((TAPS * LANES, WIDTH), BF16), pltpu.VMEM((TAPS, COLS, WIDTH), F32)]
        outs += [pltpu.VMEM((2, 56, LANES), F32), pltpu.VMEM((LANES, OWN * LANES), BF16)]
        outs += [pltpu.VMEM((2 * LANES, OWN * LANES), BF16), pltpu.VMEM((LANES, WIDTH), BF16), pltpu.VMEM((LANES, 3 * WIDTH), BF16)]
        outs += [pltpu.VMEM((2, WIDTH), F32)]
        outs += [pltpu.VMEM(up_w.shape, BF16), pltpu.VMEM(down_w.shape, BF16)]
        scratch += [pltpu.VMEM((WIDTH, WIDTH), F32), pltpu.SemaphoreType.DMA((6,))]
        specs = [SMEM] + [VMEM] * 4 + [HBM] * 4 + [VMEM] * 4
    return pl.pallas_call(
        functools.partial(near_kernel, last),
        out_shape=outs,
        in_specs=specs,
        out_specs=[VMEM] * len(outs),
        scratch_shapes=scratch,
        compiler_params=LARGE,
    )(*args)


def edge(last, *args):
    if last:
        outs = [jax.ShapeDtypeStruct((2, COLS, LANES), F32)] * 2
    else:
        outs = [jax.ShapeDtypeStruct((TIMES, COLS, LANES), kind) for kind in (F32, BF16)]
    touched = len(pairs_of(EDGE))
    return pl.pallas_call(
        functools.partial(edge_kernel, last),
        out_shape=outs,
        in_specs=[SMEM] + [VMEM] * (len(args) - 1),
        out_specs=[VMEM, VMEM],
        scratch_shapes=working(len(EDGE), TIMES if last else 1)
        + [pltpu.VMEM((TIMES * OWN * COLS, WIDTH), BF16)]
        + [pltpu.VMEM((len(EDGE), WIDE, LANES), F32)] * (2 * TIMES)
        + [pltpu.VMEM((touched, COLS, WIDTH), F32)] * TIMES,
        compiler_params=LARGE,
    )(*args)


def prepare(flags, times, sizes, turned_start):
    dense = jax.ShapeDtypeStruct((COLS, LANES), F32)
    return pl.pallas_call(
        prepare_kernel,
        out_shape=[dense, dense, jax.ShapeDtypeStruct((32, LANES), F32)],
        in_specs=[SMEM, SMEM, SMEM, VMEM],
        out_specs=[VMEM] * 3,
        compiler_params=SMALL,
    )(flags, times, sizes, turned_start)


def finish(flags, keep, got):
    return pl.pallas_call(
        finish_kernel,
        out_shape=jax.ShapeDtypeStruct((2, 2 * OWN, CHAN, COLS), F32),
        in_specs=[SMEM, VMEM, VMEM],
        out_specs=VMEM,
        compiler_params=SMALL,
    )(flags, keep, got)


def on_device(
    start_state, timesteps, step_sizes, in_weight, time_weight, conv_kernel, norm_gain, up_weight, up_bias, down_weight, out_weight,
):
    space = lax.axis_size("space")
    s, tm = lax.axis_index("space"), lax.axis_index("tm")
    beside = [(0, 1), (1, 0)]
    across = []
    for i in range(space - 1):
        across += [(2 * i + 1, 2 * i + 2), (2 * i + 2, 2 * i + 1)]

    def over_tm(x):
        return lax.ppermute(x, "tm", beside)

    def over_space(x):
        return lax.ppermute(x, ("space", "tm"), across)

    flags = jnp.stack([tm, jnp.where(tm == 0, s > 0, s < space - 1).astype(jnp.int32)]).astype(jnp.int32)
    own, inner, clock = prepare(flags, pinned(timesteps), pinned(step_sizes), pinned(start_state.transpose(0, 2, 1)))
    other_clock = over_tm(clock)
    outer = over_space(own)
    taps = conv_kernel.transpose(1, 2, 0, 3)

    partial, kept, *made = near(
        False, up_weight, down_weight, flags, own, inner, clock, other_clock,
        pinned(time_weight), pinned(up_weight), pinned(down_weight), pinned(norm_gain), in_weight, taps, up_bias, out_weight.T,
    )
    rest = (up_bias,)
    terms, sent = edge(False, flags, outer, own, clock, other_clock, partial, kept, *made, *rest)
    inner_terms, outer_terms = over_tm(sent), over_space(sent)
    partial, kept = near(True, up_weight, down_weight, flags, own, inner, terms, inner_terms, *made, *rest)
    keep, give = edge(True, flags, outer, own, outer_terms, terms, clock, other_clock, partial, kept, *made, *rest)
    return finish(flags, keep, over_tm(give)).transpose(0, 1, 3, 2)


def solution(mesh):
    both = P(("groups", "tm"))
    return jax.shard_map(
        on_device,
        mesh=mesh,
        in_specs=(P(("groups", "space"), None, None), both, both) + (P(),) * 8,
        out_specs=P("tm", ("groups", "space"), None, None),
        check_vma=False,
    )
```
